32 devices in a mesh: grp: 2 (over y), seq: 8 (over z, core), sp: 2 (over x), rep: 1.
Axes of the slice: x: 2, y: 2, z: 4, core: 2. Of those that a mesh axis runs over, the one named last changes fastest.
Arguments:
- queries: bfloat16 [32, 192, 2048], P(('grp', 'sp', 'seq'), 'rep'), parts along dimension 0, may hold values from -8 to 8
- keys: bfloat16 [32, 192, 2048], P(('grp', 'sp', 'seq'), 'rep'), parts along dimension 0, may hold values from -6 to 6
- values: bfloat16 [32, 192, 2048], P(('grp', 'sp', 'seq'), 'rep'), parts along dimension 0, may hold values from -16 to 16
- text_keys: bfloat16 [512, 2048], P('grp'), parts along dimension 0, may hold values from -6 to 6
- text_values: bfloat16 [512, 2048], P('grp'), parts along dimension 0, may hold values from -16 to 16
- text_count: int32 [2], P('grp'), parts along dimension 0, may hold values from 128 to 256
Outputs:
- attended: bfloat16 [32, 192, 2048], P(('grp', 'sp', 'seq'), 'rep'), parts along dimension 0
The draws below stay inside these ranges and needn't reach their ends.
There are 2 independent parts, one for each index of `grp`. The reference program is written for one: setup_inputs(seed, part) draws one part's arguments, and reference() takes and returns one part's arrays. A program takes and returns all parts, laid end to end along the dimension named above; each array names one. Nothing has to cross between parts.
All inputs are finite; a program needn't handle non-finite values.
Results may differ from the reference program's by a relative error of at most 0.0035.
Values may be sent and summed in bfloat16 or wider, within the bound.
No kernel may reach another device: no remote copies, remote signals or barrier semaphores. Data moves between devices by JAX's collectives and lax.ppermute only.
A program may use at most 64 MiB of HBM per device.

```python
import math
import jax
import jax.numpy as jnp
from jax import lax

HEADS = 16
HDIM = 128
WIDTH = 2048
TILE = 192
COLS = 4
TILES = 16
TEXT = 256
WIN = 9


def paired_fields(key):
    base = jax.random.fold_in(key, 1234)
    key_query, key_key = jax.random.split(base, 2)
    shape = (TILES, TILE, WIDTH)
    query_field = jnp.clip(jax.random.normal(key_query, shape, jnp.float32) * 2.0, -8.0, 8.0)
    key_field = jnp.clip(jax.random.normal(key_key, shape, jnp.float32), -6.0, 6.0)
    return (query_field, key_field)


def draw_queries(key, part):
    return paired_fields(key)[0].astype(jnp.bfloat16)


def draw_keys(key, part):
    return paired_fields(key)[1].astype(jnp.bfloat16)


def block_levels(key, extent, cuts, least, top_value):
    loudness = 1.0
    for dim, shards_of in cuts:
        steps = jax.random.uniform(jax.random.fold_in(jax.random.fold_in(key, 6), dim), (shards_of,), jnp.float32, least / len(cuts), top_value / len(cuts))
        loudness = loudness * jnp.repeat(jnp.exp(steps), extent[dim] // shards_of).reshape((-1,) + (1,) * (len(extent) - 1 - dim))
    return loudness


def gaussian(rng, shape, scale, reach, pieces=(), kind=jnp.bfloat16):
    level = block_levels(rng, shape, pieces, -0.22, 0.18) if pieces else 1.0
    values = jax.random.normal(rng, shape, jnp.float32) * scale * level
    return jnp.minimum(jnp.maximum(values, -reach), reach).astype(kind)


def setup_inputs(seed: int = 0, part: int = 0) -> dict:
    key_of = jax.random.split(jax.random.key(seed), 7)
    part_keys = jax.random.split(jax.random.fold_in(key_of[6], part), 7)
    queries = draw_queries(jax.random.fold_in(jax.random.fold_in(key_of[6], part), 71), part)
    keys = draw_keys(jax.random.fold_in(jax.random.fold_in(key_of[6], part), 71), part)
    values = gaussian(part_keys[2], (TILES, TILE, WIDTH), 4.0, 16.0, ((0, 16),))
    text_keys = gaussian(part_keys[3], (TEXT, WIDTH), 1.0, 6.0)
    text_values = gaussian(part_keys[4], (TEXT, WIDTH), 4.0, 16.0)
    text_count = jax.random.randint(part_keys[5], (1,), TEXT // 2, TEXT + 1).astype(jnp.int32)
    return dict(queries=queries, keys=keys, values=values, text_keys=text_keys, text_values=text_values, text_count=text_count)


masked_score = -1e+30

def reference(queries, keys, values, text_keys, text_values, text_count):
    score_scale = 1.0 / math.sqrt(HDIM)
    text_live = jnp.arange(TEXT, dtype=jnp.int32) < text_count[0]
    text_key_rows = text_keys.astype(jnp.float32).reshape(TEXT, HEADS, HDIM)
    text_val_rows = text_values.astype(jnp.float32).reshape(TEXT, HEADS, HDIM)
    position = jnp.arange(WIN, dtype=jnp.int32)
    col_step = position % 3 - 1
    shifts = (position // 3 - 1) * COLS + col_step

    def one_tile(tile_num):
        targets = tile_num + shifts
        column = tile_num % COLS + col_step
        inside = (targets >= 0) & (targets < TILES) & (column >= 0) & (column < COLS)
        safe = jnp.clip(targets, 0, TILES - 1).astype(jnp.int32)
        near_keys = keys[safe].astype(jnp.float32).reshape(WIN * TILE, HEADS, HDIM)
        near_values = values[safe].astype(jnp.float32).reshape(WIN * TILE, HEADS, HDIM)
        query_rows = queries[tile_num].astype(jnp.float32).reshape(TILE, HEADS, HDIM)
        img_scores = jnp.einsum('qhd,khd->hqk', query_rows, near_keys) * score_scale
        img_scores = jnp.where(jnp.repeat(inside, TILE)[None, None, :], img_scores, masked_score)
        txt_scores = jnp.einsum('qhd,khd->hqk', query_rows, text_key_rows) * score_scale
        txt_scores = jnp.where(text_live[None, None, :], txt_scores, masked_score)
        row_top = jnp.maximum(lax.optimization_barrier(jnp.max(img_scores, axis=-1)), lax.optimization_barrier(jnp.max(txt_scores, axis=-1)))
        img_exp = jnp.exp(img_scores - row_top[..., None])
        txt_exp = jnp.exp(txt_scores - row_top[..., None])
        row_total = lax.optimization_barrier(jnp.sum(img_exp, axis=-1)) + lax.optimization_barrier(jnp.sum(txt_exp, axis=-1))
        img_weights = lax.optimization_barrier(img_exp.astype(jnp.bfloat16)).astype(jnp.float32)
        txt_weights = lax.optimization_barrier(txt_exp.astype(jnp.bfloat16)).astype(jnp.float32)
        summed = jnp.einsum('hqk,khd->qhd', img_weights, near_values)
        summed = summed + jnp.einsum('hqk,khd->qhd', txt_weights, text_val_rows)
        summed = summed / jnp.transpose(row_total)[:, :, None]
        return summed.reshape(TILE, WIDTH).astype(jnp.bfloat16)
    return lax.map(one_tile, jnp.arange(TILES, dtype=jnp.int32))
```

```python
import functools
import math

import jax
import jax.numpy as jnp
from jax import lax
from jax.experimental import pallas as pl
from jax.experimental.pallas import tpu as pltpu
from jax.sharding import PartitionSpec as P

HDIM = 128
COLS = 4
CHUNKS = 2

masked_score = -1e30
exp2_scale = math.log2(math.e) / math.sqrt(HDIM)


def attend_kernel(n_halo, info, q_own, q_got, k_own, v_own, text_k, text_v, *refs):
    tiles = refs[: 5 + 3 * n_halo]
    o_own, o_got, keys, vals = refs[5 + 3 * n_halo :]
    got, sib_own, sib_got, cross_own, cross_got = tiles[:5]
    rows = q_got.shape[0]
    length = k_own.shape[1]
    a_is_own = info[1] == 1
    cross_pen = jnp.where(info[2] == 1, 0.0, -masked_score)
    text_live = lax.broadcasted_iota(jnp.int32, (1, text_k.shape[0]), 1) < info[3]

    at = 0
    ends = []
    read = lambda ref: (ref[0], ref[1])
    sources = [(k_own[0], v_own[0])]
    sources += [read(ref) for ref in (sib_own, got, sib_got, cross_own, cross_got)]
    sources += [(text_k[...], text_v[...])]
    sources += [read(ref) for ref in tiles[5:]]
    for key, val in sources:
        keys[at : at + key.shape[0]] = key
        vals[at : at + key.shape[0]] = val
        at += key.shape[0]
        ends.append(at)
    main_end, cross_end, text_end = ends[3], ends[5], ends[6]

    mine, theirs = q_own[0], q_got[...]
    q_a = jnp.where(a_is_own, mine, theirs)
    q_b = jnp.where(a_is_own, theirs, mine)
    both = jnp.concatenate([q_a, q_b], axis=0)

    def scores_of(q, lo, hi):
        return lax.dot_general(
            q, keys[lo:hi], (((1,), (1,)), ((), ())), preferred_element_type=jnp.float32
        )

    def top_of(scores):
        return jnp.max(scores, axis=-1, keepdims=True)

    s_main = scores_of(both, 0, main_end)
    s_cross = scores_of(both, main_end, cross_end)
    s_text = jnp.where(text_live, scores_of(both, cross_end, text_end), masked_score)
    top = jnp.maximum(jnp.maximum(top_of(s_main), top_of(s_cross) - cross_pen), top_of(s_text))

    tops = [top[:rows], top[rows:]]
    halos = []
    for j in range(n_halo):
        halo_pen = jnp.where(info[4 + j] == 1, 0.0, -masked_score)
        lo = text_end + 3 * j * length
        q = (q_a, q_b)[j]
        parts = [
            (lo, lo + 2 * length, halo_pen),
            (lo + 2 * length, lo + 3 * length, jnp.maximum(halo_pen, cross_pen)),
        ]
        for start, stop, pen in parts:
            s = scores_of(q, start, stop)
            tops[j] = jnp.maximum(tops[j], top_of(s) - pen)
            halos.append((j, s, start, stop, pen))
    top = jnp.concatenate(tops, axis=0) * exp2_scale
    tops = [top[:rows], top[rows:]]

    def weigh(s, row_top, start, stop):
        w = jnp.exp2(s * exp2_scale - row_top)
        total = jnp.sum(w, axis=-1, keepdims=True)
        out = jnp.dot(
            w.astype(jnp.bfloat16), vals[start:stop], preferred_element_type=jnp.float32
        )
        return total, out

    total, summed = weigh(s_main, top, 0, main_end)
    for s, row_top, start, stop in (
        (s_cross, top + cross_pen, main_end, cross_end),
        (s_text, top, cross_end, text_end),
    ):
        more_total, more = weigh(s, row_top, start, stop)
        total, summed = total + more_total, summed + more
    totals = [total[:rows], total[rows:]]
    sums = [summed[:rows], summed[rows:]]
    for j, s, start, stop, pen in halos:
        more_total, more = weigh(s, tops[j] + pen, start, stop)
        totals[j], sums[j] = totals[j] + more_total, sums[j] + more
    out_a = (sums[0] / totals[0]).astype(jnp.bfloat16)
    out_b = (sums[1] / totals[1]).astype(jnp.bfloat16)
    o_own[...] = jnp.where(a_is_own, out_a, out_b)
    o_got[...] = jnp.where(a_is_own, out_b, out_a)


def attend(info, queries, q_got, keys, values, text_k, text_v, tiles, n_halo):
    rows, width = q_got.shape
    length = keys.shape[1]
    heads = width // HDIM
    text_len = text_k.shape[0]
    full = lambda n: pl.BlockSpec((1, n, HDIM), lambda h, info: (0, 0, info[0] + h))
    text = pl.BlockSpec((text_len, HDIM), lambda h, info: (0, info[0] + h))
    pair = pl.BlockSpec((2, length, HDIM), lambda h, info: (0, 0, h))
    flat = pl.BlockSpec((rows, HDIM), lambda h, info: (0, h))
    total_keys = (6 + 3 * n_halo) * length + text_len
    pairs = heads * 2 * rows * total_keys
    return pl.pallas_call(
        functools.partial(attend_kernel, n_halo),
        grid_spec=pltpu.PrefetchScalarGridSpec(
            num_scalar_prefetch=1,
            grid=(heads,),
            in_specs=[full(rows), flat, full(length), full(length), text, text]
            + [pair] * len(tiles),
            out_specs=[flat, flat],
            scratch_shapes=[pltpu.VMEM((total_keys, HDIM), jnp.bfloat16)] * 2,
        ),
        out_shape=[jax.ShapeDtypeStruct((rows, width), jnp.bfloat16)] * 2,
        cost_estimate=pl.CostEstimate(
            flops=4 * pairs * HDIM,
            bytes_accessed=heads * HDIM * 2 * (2 * total_keys + 4 * rows),
            transcendentals=pairs,
        ),
        compiler_params=pltpu.CompilerParams(vmem_limit_bytes=40 * 2**20),
    )(info, queries, q_got, keys, values, text_k, text_v, *tiles)


def body(queries, keys, values, text_keys, text_values, text_count):
    n_seq, n_sp = lax.axis_size("seq"), lax.axis_size("sp")
    tile = lax.axis_index("sp") * n_seq + lax.axis_index("seq")
    col, odd, pair = tile % COLS, tile // COLS % 2, tile // (2 * COLS)
    n_pairs = n_sp * n_seq // (2 * COLS)
    one_halo = n_pairs == 2
    if lax.axis_size("rep") > 1:
        keys = lax.all_gather(keys, "rep", axis=1, tiled=True)
        values = lax.all_gather(values, "rep", axis=1, tiled=True)
    half = queries.shape[2] // 2
    part = half // CHUNKS
    mine, other = odd * half, (1 - odd) * half

    def xor(x, mask, keep=lambda i: True):
        return lax.ppermute(x, "seq", [(i, i ^ mask) for i in range(n_seq) if keep(i)])

    def sibling(x):
        return xor(x, 1)

    def cross(x):
        return xor(x, 3, lambda i: i % COLS in (1, 2))

    def swap(x):
        return xor(x, COLS)

    def cut(x, at):
        return lax.dynamic_slice_in_dim(x[0], at, part, 1)

    def cut_pair(at):
        return jnp.stack([cut(keys, at), cut(values, at)])

    step = 2 * COLS
    n_tiles = n_sp * n_seq
    if one_halo:
        a_own = (odd == 1) == (pair == 0)
    else:
        a_own = odd == 0

    def across(x, tile_perm):
        place = lambda i: i % n_seq * n_sp + i // n_seq
        return lax.ppermute(x, ("seq", "sp"), [(place(i), place(j)) for i, j in tile_perm])

    def halo_of(own, got):
        if one_halo:
            perm = [(i, (i + step) % n_tiles) for i in range(n_tiles)]
            return [across(jnp.where(a_own, own, got), perm)]
        high = jnp.where(odd == 1, own, got)
        low = jnp.where(odd == 0, own, got)
        down = [(i, i + step) for i in range(n_tiles - step)]
        up = [(i + step, i) for i in range(n_tiles - step)]
        return [across(high, down), across(low, up)]

    if one_halo:
        live = [jnp.int32(1)]
    else:
        live = [pair > 0, pair < n_pairs - 1]

    own_parts, got_parts = [], []
    for c in range(CHUNKS):
        own = cut_pair(mine + c * part)
        got = swap(cut_pair(other + c * part))
        q_got = swap(cut(queries, other + c * part))
        halos = halo_of(own, got)
        tiles = [got, sibling(own), sibling(got), cross(own), cross(got)]
        for halo in halos:
            tiles += [halo, sibling(halo), cross(halo)]
        first_head = (mine + c * part) // HDIM
        info = jnp.stack(
            [
                jnp.asarray(x, jnp.int32)
                for x in (first_head, a_own, (col == 1) | (col == 2), text_count[0], *live)
            ]
        )
        o_own, o_got = attend(
            info, queries, q_got, keys, values, text_keys, text_values, tiles, len(halos)
        )
        own_parts.append(o_own)
        got_parts.append(swap(o_got))
    own = jnp.concatenate(own_parts, axis=1)
    got = jnp.concatenate(got_parts, axis=1)
    out = jnp.where(
        odd == 0, jnp.concatenate([own, got], axis=1), jnp.concatenate([got, own], axis=1)
    )
    return out[None]


def solution(mesh):
    in_specs = (
        P(("grp", "sp", "seq"), "rep", None),
        P(("grp", "sp", "seq"), "rep", None),
        P(("grp", "sp", "seq"), "rep", None),
        P("grp", None),
        P("grp", None),
        P("grp"),
    )
    out_specs = P(("grp", "sp", "seq"), "rep", None)
    return jax.shard_map(body, mesh=mesh, in_specs=in_specs, out_specs=out_specs, check_vma=False)
```

```python
import functools
import math

import jax
import jax.numpy as jnp
from jax import lax
from jax.experimental import pallas as pl
from jax.experimental.pallas import tpu as pltpu
from jax.sharding import PartitionSpec as P

HDIM = 128
COLS = 4
CHUNKS = 2
STEP_HEADS = 2

masked_score = -1e30
exp2_scale = math.log2(math.e) / math.sqrt(HDIM)
vmem_limit = 56 * 2**20


def pack_kernel(n, at, *refs):
    sources, out, sems = refs[:n], refs[-2], refs[-1]
    width = out.shape[2]
    start = pl.multiple_of(at[0], HDIM)
    copies = [
        pltpu.make_async_copy(src.at[0, :, pl.ds(start, width)], out.at[j], sems.at[j])
        for j, src in enumerate(sources)
    ]
    for copy in copies:
        copy.start()
    for copy in copies:
        copy.wait()


def pack(sources, at, width):
    n, length = len(sources), sources[0].shape[1]
    return pl.pallas_call(
        functools.partial(pack_kernel, n),
        in_specs=[pl.BlockSpec(memory_space=pltpu.SMEM)]
        + [pl.BlockSpec(memory_space=pl.ANY)] * n,
        out_specs=pl.BlockSpec(memory_space=pl.ANY),
        out_shape=jax.ShapeDtypeStruct((n, length, width), jnp.bfloat16),
        scratch_shapes=[pltpu.SemaphoreType.DMA((n,))],
        cost_estimate=pl.CostEstimate(
            flops=0, bytes_accessed=4 * n * length * width, transcendentals=0
        ),
    )(at.reshape(1), *sources)


def attend_kernel(info, q_ref, text_k, text_v, *refs):
    tiles, (out_ref, keys, vals) = refs[:9], refs[-3:]
    rows = q_ref.shape[1]
    cross_pen = jnp.where(info[1] == 1, 0.0, -masked_score)
    text_live = lax.broadcasted_iota(jnp.int32, (1, text_k.shape[0]), 1) < info[3]

    def run(with_halo):
        for j in range(q_ref.shape[2] // HDIM):
            head = slice(j * HDIM, (j + 1) * HDIM)
            read = lambda ref: (ref[0, :, head], ref[1, :, head])
            sources = [read(ref) for ref in tiles[:6]]
            sources += [(text_k[:, head], text_v[:, head])]
            if with_halo:
                sources += [read(ref) for ref in tiles[6:]]
            ends = [0]
            for key, val in sources:
                keys[j, ends[-1] : ends[-1] + key.shape[0]] = key
                vals[j, ends[-1] : ends[-1] + key.shape[0]] = val
                ends.append(ends[-1] + key.shape[0])
            n = ends[-1]
            scores = lax.dot_general(
                q_ref[0, :, head],
                keys[j, :n],
                (((1,), (1,)), ((), ())),
                preferred_element_type=jnp.float32,
            )
            parts = [
                (scores[:, : ends[4]], 0.0),
                (scores[:, ends[4] : ends[6]], cross_pen),
                (jnp.where(text_live, scores[:, ends[6] : ends[7]], masked_score), 0.0),
            ]
            if with_halo:
                parts += [(scores[:, ends[7] : ends[9]], 0.0), (scores[:, ends[9] :], cross_pen)]
            top = None
            for s, pen in parts:
                here = jnp.max(s, axis=-1, keepdims=True) - pen
                top = here if top is None else jnp.maximum(top, here)
            top = top * exp2_scale
            total, weights = 0.0, []
            for s, pen in parts:
                w = jnp.exp2(s * exp2_scale - (top + pen))
                total = total + jnp.sum(w, axis=-1, keepdims=True)
                weights.append(w.astype(jnp.bfloat16))
            summed = jnp.dot(
                jnp.concatenate(weights, axis=1), vals[j, :n], preferred_element_type=jnp.float32
            )
            out_ref[0, :, head] = (summed / total).astype(jnp.bfloat16)

    pl.when(info[2] == 1)(lambda: run(True))
    pl.when(info[2] == 0)(lambda: run(False))


def attend(info, q, text_k, text_v, tiles, heads, out_width, q_full=False, into=None):
    rows, length = q.shape[1], tiles[0][0].shape[1]
    text_len = text_k.shape[0]
    step = math.gcd(STEP_HEADS, heads)
    width = step * HDIM
    full = pl.BlockSpec((1, rows, width), lambda h, info: (0, 0, info[0] // step + h))
    flat = pl.BlockSpec((1, rows, width), lambda h, info: (0, 0, h))
    text = pl.BlockSpec((text_len, width), lambda h, info: (0, info[0] // step + h))

    def tile(first):
        return pl.BlockSpec((2, length, width), lambda h, info: (0, 0, first // step + h))

    total_keys = len(tiles) * length + text_len
    pairs = heads * rows * total_keys
    extra = [] if into is None else [into]
    return pl.pallas_call(
        attend_kernel,
        grid_spec=pltpu.PrefetchScalarGridSpec(
            num_scalar_prefetch=1,
            grid=(heads // step,),
            in_specs=[full if q_full else flat, text, text]
            + [tile(first) for _, first in tiles]
            + [pl.BlockSpec(memory_space=pl.ANY)] * len(extra),
            out_specs=full if q_full else flat,
            scratch_shapes=[pltpu.VMEM((step, total_keys, HDIM), jnp.bfloat16)] * 2,
        ),
        out_shape=jax.ShapeDtypeStruct((1, rows, out_width), jnp.bfloat16),
        input_output_aliases={4 + len(tiles): 0} if extra else {},
        cost_estimate=pl.CostEstimate(
            flops=4 * pairs * HDIM,
            bytes_accessed=heads * HDIM * 2 * (2 * total_keys + 2 * rows),
            transcendentals=pairs,
        ),
        compiler_params=pltpu.CompilerParams(vmem_limit_bytes=vmem_limit),
    )(info, q, text_k, text_v, *[array for array, _ in tiles], *extra)


def after(x, *others):
    return lax.optimization_barrier((x, *others))[0]


def body(queries, keys, values, text_keys, text_values, text_count):
    n_seq, n_sp = lax.axis_size("seq"), lax.axis_size("sp")
    tile = lax.axis_index("sp") * n_seq + lax.axis_index("seq")
    col, odd, pair = tile % COLS, tile // COLS % 2, tile // (2 * COLS)
    n_tiles, span = n_sp * n_seq, 2 * COLS
    n_pairs = n_tiles // span
    if lax.axis_size("rep") > 1:
        keys = lax.all_gather(keys, "rep", axis=1, tiled=True)
        values = lax.all_gather(values, "rep", axis=1, tiled=True)
    width = queries.shape[2]
    half = width // 2
    part = half // CHUNKS
    part_heads = part // HDIM
    mine, other = odd * half, (1 - odd) * half

    def xor(x, mask, keep=lambda i: True):
        return lax.ppermute(x, "seq", [(i, i ^ mask) for i in range(n_seq) if keep(i)])

    def swap(x):
        return xor(x, COLS)

    def halo(x, down):
        pairs = [(i, i + span if i // COLS % 2 == down else i - span) for i in range(n_tiles)]
        place = lambda i: i % n_seq * n_sp + i // n_seq
        pairs = [(place(i), place(j)) for i, j in pairs if 0 <= j < n_tiles]
        return lax.ppermute(x, ("seq", "sp"), pairs)

    def across(x, first):
        return [
            (x, first),
            (xor(x, 1), first),
            (xor(x, 3, lambda i: i % COLS in (1, 2)), first),
        ]

    def window(own, got, halos):
        return [own[0], own[1], got[0], got[1], own[2], got[2], *halos]

    def info(first, halo_live):
        entries = (first, (col == 1) | (col == 2), halo_live, text_count[0])
        return jnp.stack([jnp.asarray(x, jnp.int32) for x in entries])

    low_halo, high_halo = pair > 0, pair < n_pairs - 1
    got_halo = jnp.where(odd == 1, low_halo, high_halo)
    own_halo = jnp.where(odd == 1, high_halo, low_halo)

    got, q_got = [], []
    got.append(swap(pack([keys, values], other, part)))
    own = pack([keys, values], mine, half)
    own_row = across(own, 0)
    near = across(halo(own, 1), 0)
    for c in range(1, CHUNKS):
        sent = pack([keys, values], other + c * part, part)
        got.append(swap(after(sent, got[-1])))
    for c in range(CHUNKS):
        sent = pack([queries], other + c * part, part)
        q_got.append(swap(after(sent, got[0] if c == 0 else q_got[-1])))
    got_rows = [across(x, 0) for x in got]
    far = [across(halo(x, 0), 0) for x in got]

    def shifted(row, c):
        return [(x, first + c * part_heads) for x, first in row]

    back = []
    for c in range(CHUNKS):
        first = mine // HDIM + c * part_heads
        tiles = window(shifted(own_row, c), got_rows[c], shifted(near, c))
        o = attend(
            info(first, got_halo), q_got[c], text_keys, text_values, tiles, part_heads, part
        )
        back.append(swap(o))
    out = None
    for c in range(CHUNKS):
        first = mine // HDIM + c * part_heads
        tiles = window(shifted(own_row, c), got_rows[c], far[c])
        out = attend(
            info(first, own_halo), queries, text_keys, text_values, tiles, part_heads, width,
            q_full=True, into=out,
        )
    for c in range(CHUNKS):
        out = lax.dynamic_update_slice_in_dim(out, back[c], other + c * part, 2)
    return out


def solution(mesh):
    in_specs = (
        P(("grp", "sp", "seq"), "rep", None),
        P(("grp", "sp", "seq"), "rep", None),
        P(("grp", "sp", "seq"), "rep", None),
        P("grp", None),
        P("grp", None),
        P("grp"),
    )
    out_specs = P(("grp", "sp", "seq"), "rep", None)
    return jax.shard_map(body, mesh=mesh, in_specs=in_specs, out_specs=out_specs, check_vma=False)
```

```python
import functools
import math

import jax
import jax.numpy as jnp
from jax import lax
from jax.experimental import pallas as pl
from jax.experimental.pallas import tpu as pltpu
from jax.sharding import PartitionSpec as P

HDIM = 128
COLS = 4
CHUNKS = 2
STEP_HEADS = 1

masked_score = -1e30
exp2_scale = math.log2(math.e) / math.sqrt(HDIM)
vmem_limit = 56 * 2**20


def pack_kernel(sizes, at, *refs):
    sources, outs = refs[: sum(sizes)], refs[sum(sizes) :]
    i = 0
    for size, out in zip(sizes, outs):
        for j in range(size):
            out[j] = sources[i + j][0]
        i += size


def pack(groups):
    sizes = [len(sources) for sources, _, _ in groups]
    at = jnp.stack([jnp.asarray(column // width, jnp.int32) for _, column, width in groups])

    def source_spec(g, length, width):
        return pl.BlockSpec((1, length, width), lambda _, at: (0, 0, at[g]))

    in_specs, out_specs, out_shape, args = [], [], [], []
    for g, (sources, _, width) in enumerate(groups):
        length = sources[0].shape[1]
        in_specs += [source_spec(g, length, width)] * len(sources)
        args += sources
        out_specs.append(pl.BlockSpec((len(sources), length, width), lambda _, at: (0, 0, 0)))
        out_shape.append(jax.ShapeDtypeStruct((len(sources), length, width), jnp.bfloat16))
    return pl.pallas_call(
        functools.partial(pack_kernel, sizes),
        grid_spec=pltpu.PrefetchScalarGridSpec(
            num_scalar_prefetch=1, grid=(1,), in_specs=in_specs, out_specs=out_specs
        ),
        out_shape=out_shape,
        cost_estimate=pl.CostEstimate(
            flops=0, bytes_accessed=sum(4 * math.prod(o.shape) for o in out_shape), transcendentals=0
        ),
        compiler_params=pltpu.CompilerParams(vmem_limit_bytes=vmem_limit),
    )(at, *args)


def attend_kernel(halo_flag, info, q_ref, text_k, text_v, *refs):
    tiles, (out_ref, keys, vals) = refs[:9], refs[-3:]
    rows = q_ref.shape[1]
    cross_pen = jnp.where(info[1] == 1, 0.0, -masked_score)
    text_live = lax.broadcasted_iota(jnp.int32, (1, text_k.shape[0]), 1) < info[2]

    def run(with_halo):
        for j in range(q_ref.shape[2] // HDIM):
            head = slice(j * HDIM, (j + 1) * HDIM)
            read = lambda ref: (ref[0, :, head], ref[1, :, head])
            sources = [read(ref) for ref in tiles[:6]]
            sources += [(text_k[:, head], text_v[:, head])]
            if with_halo:
                sources += [read(ref) for ref in tiles[6:]]
            ends = [0]
            for key, val in sources:
                keys[j, ends[-1] : ends[-1] + key.shape[0]] = key
                vals[j, ends[-1] : ends[-1] + key.shape[0]] = val
                ends.append(ends[-1] + key.shape[0])
            n = ends[-1]
            scores = lax.dot_general(
                q_ref[0, :, head],
                keys[j, :n],
                (((1,), (1,)), ((), ())),
                preferred_element_type=jnp.float32,
            )
            parts = [
                (scores[:, : ends[4]], 0.0),
                (scores[:, ends[4] : ends[6]], cross_pen),
                (jnp.where(text_live, scores[:, ends[6] : ends[7]], masked_score), 0.0),
            ]
            if with_halo:
                parts += [(scores[:, ends[7] : ends[9]], 0.0), (scores[:, ends[9] :], cross_pen)]
            top = None
            for s, pen in parts:
                here = jnp.max(s, axis=-1, keepdims=True) - pen
                top = here if top is None else jnp.maximum(top, here)
            top = top * exp2_scale
            total, weights = 0.0, []
            for s, pen in parts:
                w = jnp.exp2(s * exp2_scale - (top + pen))
                total = total + jnp.sum(w, axis=-1, keepdims=True)
                weights.append(w.astype(jnp.bfloat16))
            summed = jnp.dot(
                jnp.concatenate(weights, axis=1), vals[j, :n], preferred_element_type=jnp.float32
            )
            out_ref[0, :, head] = (summed / total).astype(jnp.bfloat16)

    pl.when(info[halo_flag] == 1)(lambda: run(True))
    pl.when(info[halo_flag] == 0)(lambda: run(False))


def attend(info, halo_flag, q, text_k, text_v, tiles, first, heads, out_width, q_full=False, into=None):
    rows, length = q.shape[1], tiles[0][0].shape[1]
    text_len = text_k.shape[0]
    step = math.gcd(STEP_HEADS, heads)
    width = step * HDIM
    full = pl.BlockSpec((1, rows, width), lambda h, info: (0, 0, (info[0] + first) // step + h))
    flat = pl.BlockSpec((1, rows, width), lambda h, info: (0, 0, h))
    text = pl.BlockSpec((text_len, width), lambda h, info: (0, (info[0] + first) // step + h))

    def tile(at):
        return pl.BlockSpec((2, length, width), lambda h, info: (0, 0, at // step + h))

    total_keys = len(tiles) * length + text_len
    pairs = heads * rows * total_keys
    extra = [] if into is None else [into]
    return pl.pallas_call(
        functools.partial(attend_kernel, halo_flag),
        grid_spec=pltpu.PrefetchScalarGridSpec(
            num_scalar_prefetch=1,
            grid=(heads // step,),
            in_specs=[full if q_full else flat, text, text]
            + [tile(at) for _, at in tiles]
            + [pl.BlockSpec(memory_space=pl.ANY)] * len(extra),
            out_specs=full if q_full else flat,
            scratch_shapes=[pltpu.VMEM((step, total_keys, HDIM), jnp.bfloat16)] * 2,
        ),
        out_shape=jax.ShapeDtypeStruct((1, rows, out_width), jnp.bfloat16),
        input_output_aliases={4 + len(tiles): 0} if extra else {},
        cost_estimate=pl.CostEstimate(
            flops=4 * pairs * HDIM,
            bytes_accessed=heads * HDIM * 2 * (2 * total_keys + 2 * rows),
            transcendentals=pairs,
        ),
        compiler_params=pltpu.CompilerParams(vmem_limit_bytes=vmem_limit),
    )(info, q, text_k, text_v, *[array for array, _ in tiles], *extra)


def after(x, *others):
    return lax.optimization_barrier((x, *others))[0]


def body(queries, keys, values, text_keys, text_values, text_count):
    n_seq, n_sp = lax.axis_size("seq"), lax.axis_size("sp")
    tile = lax.axis_index("sp") * n_seq + lax.axis_index("seq")
    col, odd, pair = tile % COLS, tile // COLS % 2, tile // (2 * COLS)
    n_tiles, span = n_sp * n_seq, 2 * COLS
    n_pairs = n_tiles // span
    if lax.axis_size("rep") > 1:
        keys = lax.all_gather(keys, "rep", axis=1, tiled=True)
        values = lax.all_gather(values, "rep", axis=1, tiled=True)
    width = queries.shape[2]
    half = width // 2
    part = half // CHUNKS
    part_heads = part // HDIM
    mine, other = odd * half, (1 - odd) * half

    def xor(x, mask, keep=lambda i: True):
        return lax.ppermute(x, "seq", [(i, i ^ mask) for i in range(n_seq) if keep(i)])

    def swap(x):
        return xor(x, COLS)

    def halo(x, down):
        pairs = [(i, i + span if i // COLS % 2 == down else i - span) for i in range(n_tiles)]
        place = lambda i: i % n_seq * n_sp + i // n_seq
        pairs = [(place(i), place(j)) for i, j in pairs if 0 <= j < n_tiles]
        return lax.ppermute(x, ("seq", "sp"), pairs)

    def across(x, first):
        return [
            (x, first),
            (xor(x, 1), first),
            (xor(x, 3, lambda i: i % COLS in (1, 2)), first),
        ]

    def window(own, got, halos):
        return [own[0], own[1], got[0], got[1], own[2], got[2], *halos]

    low_halo, high_halo = pair > 0, pair < n_pairs - 1
    got_halo = jnp.where(odd == 1, low_halo, high_halo)
    own_halo = jnp.where(odd == 1, high_halo, low_halo)
    entries = (mine // HDIM, (col == 1) | (col == 2), text_count[0], got_halo, own_halo)
    info = jnp.stack([jnp.asarray(x, jnp.int32) for x in entries])
    got_flag, own_flag = 3, 4

    (first_sent,) = pack([([keys, values], other, part)])
    got, q_got = [swap(first_sent)], []
    own, *rest = pack(
        [([keys, values], mine, half)]
        + [([keys, values], other + c * part, part) for c in range(1, CHUNKS)]
        + [([queries], other + c * part, part) for c in range(CHUNKS)]
    )
    sent, q_sent = rest[: CHUNKS - 1], rest[CHUNKS - 1 :]
    own_row = across(own, 0)
    near = across(halo(own, 1), 0)
    for x in sent:
        got.append(swap(after(x, got[-1])))
    for c, x in enumerate(q_sent):
        q_got.append(swap(after(x, got[0] if c == 0 else q_got[-1])))
    got_rows = [across(x, 0) for x in got]
    far = [across(halo(x, 0), 0) for x in got]

    def shifted(row, c):
        return [(x, first + c * part_heads) for x, first in row]

    out, back = None, []
    for c in range(CHUNKS):
        first = c * part_heads
        tiles = window(shifted(own_row, c), got_rows[c], shifted(near, c))
        o = attend(
            info, got_flag, q_got[c], text_keys, text_values, tiles, first, part_heads, part
        )
        back.append(swap(o))
        tiles = window(shifted(own_row, c), got_rows[c], far[c])
        out = attend(
            info, own_flag, queries, text_keys, text_values, tiles, first, part_heads, width,
            q_full=True, into=out,
        )
    for c in range(CHUNKS):
        out = lax.dynamic_update_slice_in_dim(out, back[c], other + c * part, 2)
    return out


def solution(mesh):
    in_specs = (
        P(("grp", "sp", "seq"), "rep", None),
        P(("grp", "sp", "seq"), "rep", None),
        P(("grp", "sp", "seq"), "rep", None),
        P("grp", None),
        P("grp", None),
        P("grp"),
    )
    out_specs = P(("grp", "sp", "seq"), "rep", None)
    return jax.shard_map(body, mesh=mesh, in_specs=in_specs, out_specs=out_specs, check_vma=False)
```

```python
import functools
import math

import jax
import jax.numpy as jnp
from jax import lax
from jax.experimental import pallas as pl
from jax.experimental.pallas import tpu as pltpu
from jax.sharding import PartitionSpec as P

HDIM = 128
COLS = 4
CHUNKS = 2

masked_score = -1e30
exp2_scale = math.log2(math.e) / math.sqrt(HDIM)
vmem_limit = 56 * 2**20


def pack_kernel(sizes, at, *refs):
    sources, outs = refs[: sum(sizes)], refs[sum(sizes) :]
    i = 0
    for size, out in zip(sizes, outs):
        for j in range(size):
            out[j] = sources[i + j][0]
        i += size


def pack(groups):
    sizes = [len(sources) for sources, _, _ in groups]
    at = jnp.stack([jnp.asarray(column // width, jnp.int32) for _, column, width in groups])

    def source_spec(g, length, width):
        return pl.BlockSpec((1, length, width), lambda _, at: (0, 0, at[g]))

    in_specs, out_specs, out_shape, args = [], [], [], []
    for g, (sources, _, width) in enumerate(groups):
        length = sources[0].shape[1]
        in_specs += [source_spec(g, length, width)] * len(sources)
        args += sources
        out_specs.append(pl.BlockSpec((len(sources), length, width), lambda _, at: (0, 0, 0)))
        out_shape.append(jax.ShapeDtypeStruct((len(sources), length, width), jnp.bfloat16))
    return pl.pallas_call(
        functools.partial(pack_kernel, sizes),
        grid_spec=pltpu.PrefetchScalarGridSpec(
            num_scalar_prefetch=1, grid=(1,), in_specs=in_specs, out_specs=out_specs
        ),
        out_shape=out_shape,
        cost_estimate=pl.CostEstimate(
            flops=0, bytes_accessed=sum(4 * math.prod(o.shape) for o in out_shape), transcendentals=0
        ),
        compiler_params=pltpu.CompilerParams(vmem_limit_bytes=vmem_limit),
    )(at, *args)


def attend_kernel(flag, first, places, info, q_ref, text_k, text_v, *refs):
    tiles, (out_ref, keys, vals, sems) = refs[: len(places)], refs[-4:]
    length, width = tiles[0].shape[1], keys.shape[1]
    text_len = text_k.shape[0]
    cross_pen = jnp.where(info[1] == 1, 0.0, -masked_score)
    text_live = lax.broadcasted_iota(jnp.int32, (1, text_len), 1) < info[2]
    head_at = pl.multiple_of((info[0] + first) * HDIM, HDIM)

    ends = [0]
    sources = [[], []]
    for ref, place in zip(tiles, places):
        if len(ends) == 7:
            ends.append(ends[-1] + text_len)
        ends.append(ends[-1] + length)
        for side in (0, 1):
            sources[side].append(ref.at[side, :, place * HDIM : place * HDIM + width])
    for side, text in ((0, text_k), (1, text_v)):
        sources[side].insert(6, text.at[:, pl.ds(head_at, width)])
    copies = [
        [
            pltpu.make_async_copy(src, dst.at[lo:hi], sems.at[side, i])
            for i, (src, lo, hi) in enumerate(zip(sources[side], ends, ends[1:]))
        ]
        for side, dst in ((0, keys), (1, vals))
    ]
    for copy in copies[0] + copies[1]:
        copy.start()
    for copy in copies[0]:
        copy.wait()

    def run(n):
        heads = [slice(j * HDIM, (j + 1) * HDIM) for j in range(width // HDIM)]
        ones = jnp.ones((n, HDIM), jnp.bfloat16)

        def scores_of(head):
            return lax.dot_general(
                q_ref[0, :, head],
                keys[:n, head],
                (((1,), (1,)), ((), ())),
                preferred_element_type=jnp.float32,
            )

        scores = scores_of(heads[0])
        for j, head in enumerate(heads):
            parts = [
                (scores[:, : ends[4]], 0.0),
                (scores[:, ends[4] : ends[6]], cross_pen),
                (jnp.where(text_live, scores[:, ends[6] : ends[7]], masked_score), 0.0),
            ]
            if n > ends[7]:
                parts += [(scores[:, ends[7] : ends[9]], 0.0), (scores[:, ends[9] :], cross_pen)]
            if j + 1 < len(heads):
                scores = scores_of(heads[j + 1])
            top = None
            for s, pen in parts:
                here = jnp.max(s, axis=-1, keepdims=True) - pen
                top = here if top is None else jnp.maximum(top, here)
            top = top * exp2_scale
            weights = [
                jnp.exp2(s * exp2_scale - (top + pen)).astype(jnp.bfloat16) for s, pen in parts
            ]
            if j == 0:
                for copy in copies[1]:
                    copy.wait()
            summed = jnp.dot(
                jnp.concatenate(weights, axis=1),
                jnp.concatenate([vals[:n, head], ones], axis=1),
                preferred_element_type=jnp.float32,
            )
            out_ref[0, :, head] = (summed[:, :HDIM] / summed[:, HDIM:]).astype(jnp.bfloat16)

    pl.when(info[flag] == 1)(lambda: run(ends[-1]))
    pl.when(info[flag] == 0)(lambda: run(ends[7]))


def attend(info, flag, q, text_k, text_v, tiles, first, heads, out_width, q_full=False, into=None):
    rows, length = q.shape[1], tiles[0][0].shape[1]
    width = heads * HDIM
    if q_full:
        block = pl.BlockSpec((1, rows, width), lambda _, info: (0, 0, (info[0] + first) // heads))
    else:
        block = pl.BlockSpec((1, rows, width), lambda _, info: (0, 0, 0))
    total_keys = len(tiles) * length + text_k.shape[0]
    pairs = heads * rows * total_keys
    extra = [] if into is None else [into]
    return pl.pallas_call(
        functools.partial(attend_kernel, flag, first, [place for _, place in tiles]),
        grid_spec=pltpu.PrefetchScalarGridSpec(
            num_scalar_prefetch=1,
            grid=(1,),
            in_specs=[block] + [pl.BlockSpec(memory_space=pl.ANY)] * (2 + len(tiles) + len(extra)),
            out_specs=block,
            scratch_shapes=[pltpu.VMEM((total_keys, width), jnp.bfloat16)] * 2
            + [pltpu.SemaphoreType.DMA((2, len(tiles) + 1))],
        ),
        out_shape=jax.ShapeDtypeStruct((1, rows, out_width), jnp.bfloat16),
        input_output_aliases={4 + len(tiles): 0} if extra else {},
        cost_estimate=pl.CostEstimate(
            flops=4 * pairs * HDIM,
            bytes_accessed=heads * HDIM * 2 * (2 * total_keys + 2 * rows),
            transcendentals=pairs,
        ),
        compiler_params=pltpu.CompilerParams(vmem_limit_bytes=vmem_limit),
    )(info, q, text_k, text_v, *[array for array, _ in tiles], *extra)


def after(x, *others):
    return lax.optimization_barrier((x, *others))[0]


def body(queries, keys, values, text_keys, text_values, text_count):
    n_seq, n_sp = lax.axis_size("seq"), lax.axis_size("sp")
    tile = lax.axis_index("sp") * n_seq + lax.axis_index("seq")
    col, odd, pair = tile % COLS, tile // COLS % 2, tile // (2 * COLS)
    n_tiles, span = n_sp * n_seq, 2 * COLS
    n_pairs = n_tiles // span
    if lax.axis_size("rep") > 1:
        keys = lax.all_gather(keys, "rep", axis=1, tiled=True)
        values = lax.all_gather(values, "rep", axis=1, tiled=True)
    width = queries.shape[2]
    half = width // 2
    part = half // CHUNKS
    part_heads = part // HDIM
    mine, other = odd * half, (1 - odd) * half

    def xor(x, mask, keep=lambda i: True):
        return lax.ppermute(x, "seq", [(i, i ^ mask) for i in range(n_seq) if keep(i)])

    def swap(x):
        return xor(x, COLS)

    def halo(x, down):
        pairs = [(i, i + span if i // COLS % 2 == down else i - span) for i in range(n_tiles)]
        place = lambda i: i % n_seq * n_sp + i // n_seq
        pairs = [(place(i), place(j)) for i, j in pairs if 0 <= j < n_tiles]
        return lax.ppermute(x, ("seq", "sp"), pairs)

    def across(x, first):
        return [
            (x, first),
            (xor(x, 1), first),
            (xor(x, 3, lambda i: i % COLS in (1, 2)), first),
        ]

    def window(own, got, halos):
        return [own[0], own[1], got[0], got[1], own[2], got[2], *halos]

    low_halo, high_halo = pair > 0, pair < n_pairs - 1
    got_halo = jnp.where(odd == 1, low_halo, high_halo)
    own_halo = jnp.where(odd == 1, high_halo, low_halo)
    entries = (mine // HDIM, (col == 1) | (col == 2), text_count[0], got_halo, own_halo)
    info = jnp.stack([jnp.asarray(x, jnp.int32) for x in entries])
    got_flag, own_flag = 3, 4

    (first_sent,) = pack([([keys, values], other, part)])
    got, q_got = [swap(first_sent)], []
    own, *rest = pack(
        [([keys, values], mine, half)]
        + [([keys, values], other + c * part, part) for c in range(1, CHUNKS)]
        + [([queries], other + c * part, part) for c in range(CHUNKS)]
    )
    sent, q_sent = rest[: CHUNKS - 1], rest[CHUNKS - 1 :]
    own_row = across(own, 0)
    near_halo = halo(own, 1)
    q_got.append(swap(after(q_sent[0], got[0], near_halo)))
    near = across(near_halo, 0)

    def shifted(row, c):
        return [(x, first + c * part_heads) for x, first in row]

    out, back = None, []
    for c in range(CHUNKS):
        last = c + 1 == CHUNKS
        if not last:
            got.append(swap(after(sent[c], got[c])))
        got_row = across(got[c], 0)
        far_halo = halo(got[c], 0)
        if not last:
            done = [x for x, _ in got_row[1:]] + [far_halo]
            q_got.append(swap(after(q_sent[c + 1], q_got[c], *done)))
        far = across(far_halo, 0)
        first = c * part_heads
        tiles = window(shifted(own_row, c), got_row, shifted(near, c))
        q = q_got[c] if out is None else after(q_got[c], out)
        o = attend(info, got_flag, q, text_keys, text_values, tiles, first, part_heads, part)
        back.append(swap(o))
        if not last:
            got[c + 1] = after(got[c + 1], o)
        tiles = window(shifted(own_row, c), got_row, far)
        out = attend(
            info, own_flag, queries, text_keys, text_values, tiles, first, part_heads, width,
            q_full=True, into=out,
        )
    for c in range(CHUNKS):
        out = lax.dynamic_update_slice_in_dim(out, back[c], other + c * part, 2)
    return out


def solution(mesh):
    in_specs = (
        P(("grp", "sp", "seq"), "rep", None),
        P(("grp", "sp", "seq"), "rep", None),
        P(("grp", "sp", "seq"), "rep", None),
        P("grp", None),
        P("grp", None),
        P("grp"),
    )
    out_specs = P(("grp", "sp", "seq"), "rep", None)
    return jax.shard_map(body, mesh=mesh, in_specs=in_specs, out_specs=out_specs, check_vma=False)
```

```python
import functools
import math

import jax
import jax.numpy as jnp
from jax import lax
from jax.experimental import pallas as pl
from jax.experimental.pallas import tpu as pltpu
from jax.sharding import PartitionSpec as P

HDIM = 128
COLS = 4
CHUNKS = 2

masked_score = -1e30
exp2_scale = math.log2(math.e) / math.sqrt(HDIM)
vmem_limit = 56 * 2**20


def pack_kernel(sizes, at, *refs):
    sources, outs = refs[: sum(sizes)], refs[sum(sizes) :]
    i = 0
    for size, out in zip(sizes, outs):
        for j in range(size):
            out[j] = sources[i + j][0]
        i += size


def pack(groups):
    sizes = [len(sources) for sources, _, _ in groups]
    at = jnp.stack([jnp.asarray(column // width, jnp.int32) for _, column, width in groups])

    def source_spec(g, length, width):
        return pl.BlockSpec((1, length, width), lambda _, at: (0, 0, at[g]))

    in_specs, out_specs, out_shape, args = [], [], [], []
    for g, (sources, _, width) in enumerate(groups):
        length = sources[0].shape[1]
        in_specs += [source_spec(g, length, width)] * len(sources)
        args += sources
        out_specs.append(pl.BlockSpec((len(sources), length, width), lambda _, at: (0, 0, 0)))
        out_shape.append(jax.ShapeDtypeStruct((len(sources), length, width), jnp.bfloat16))
    return pl.pallas_call(
        functools.partial(pack_kernel, sizes),
        grid_spec=pltpu.PrefetchScalarGridSpec(
            num_scalar_prefetch=1, grid=(1,), in_specs=in_specs, out_specs=out_specs
        ),
        out_shape=out_shape,
        cost_estimate=pl.CostEstimate(
            flops=0, bytes_accessed=sum(4 * math.prod(o.shape) for o in out_shape), transcendentals=0
        ),
        compiler_params=pltpu.CompilerParams(vmem_limit_bytes=vmem_limit),
    )(at, *args)


def attend_kernel(flag, first, places, info, q_ref, text_k, text_v, *refs):
    tiles, (out_ref, keys, vals, sems) = refs[: len(places)], refs[-4:]
    length, width = tiles[0].shape[1], keys.shape[1]
    text_len = text_k.shape[0]
    cross_pen = jnp.where(info[1] == 1, 0.0, -masked_score)
    text_live = lax.broadcasted_iota(jnp.int32, (1, text_len), 1) < info[2]
    head_at = pl.multiple_of((info[0] + first) * HDIM, HDIM)

    ends = [0]
    sources = [[], []]
    for ref, place in zip(tiles, places):
        if len(ends) == 7:
            ends.append(ends[-1] + text_len)
        ends.append(ends[-1] + length)
        for side in (0, 1):
            sources[side].append(ref.at[side, :, place * HDIM : place * HDIM + width])
    for side, text in ((0, text_k), (1, text_v)):
        sources[side].insert(6, text.at[:, pl.ds(head_at, width)])
    copies = [
        [
            pltpu.make_async_copy(src, dst.at[lo:hi], sems.at[side, i])
            for i, (src, lo, hi) in enumerate(zip(sources[side], ends, ends[1:]))
        ]
        for side, dst in ((0, keys), (1, vals))
    ]
    for copy in copies[0] + copies[1]:
        copy.start()
    for copy in copies[0] + copies[1]:
        copy.wait()

    def run(n):
        def one_head(j, carry):
            head = pl.ds(pl.multiple_of(j * HDIM, HDIM), HDIM)
            scores = lax.dot_general(
                q_ref[0, :, head],
                keys[:n, head],
                (((1,), (1,)), ((), ())),
                preferred_element_type=jnp.float32,
            )
            parts = [
                (scores[:, : ends[4]], 0.0),
                (scores[:, ends[4] : ends[6]], cross_pen),
                (jnp.where(text_live, scores[:, ends[6] : ends[7]], masked_score), 0.0),
            ]
            if n > ends[7]:
                parts += [(scores[:, ends[7] : ends[9]], 0.0), (scores[:, ends[9] :], cross_pen)]
            top = None
            for s, pen in parts:
                here = jnp.max(s, axis=-1, keepdims=True) - pen
                top = here if top is None else jnp.maximum(top, here)
            top = top * exp2_scale
            weights = [
                jnp.exp2(s * exp2_scale - (top + pen)).astype(jnp.bfloat16) for s, pen in parts
            ]
            summed = jnp.dot(
                jnp.concatenate(weights, axis=1),
                jnp.concatenate([vals[:n, head], jnp.ones((n, HDIM), jnp.bfloat16)], axis=1),
                preferred_element_type=jnp.float32,
            )
            out_ref[0, :, head] = (summed[:, :HDIM] / summed[:, HDIM:]).astype(jnp.bfloat16)
            return carry

        lax.fori_loop(0, width // HDIM, one_head, 0)

    pl.when(info[flag] == 1)(lambda: run(ends[-1]))
    pl.when(info[flag] == 0)(lambda: run(ends[7]))


def attend(info, flag, q, text_k, text_v, tiles, first, heads, out_width, q_full=False):
    rows, length = q.shape[1], tiles[0][0].shape[1]
    width = heads * HDIM
    if q_full:
        block = pl.BlockSpec((1, rows, width), lambda _, info: (0, 0, (info[0] + first) // heads))
    else:
        block = pl.BlockSpec((1, rows, width), lambda _, info: (0, 0, 0))
    total_keys = len(tiles) * length + text_k.shape[0]
    pairs = heads * rows * total_keys
    return pl.pallas_call(
        functools.partial(attend_kernel, flag, first, [place for _, place in tiles]),
        grid_spec=pltpu.PrefetchScalarGridSpec(
            num_scalar_prefetch=1,
            grid=(1,),
            in_specs=[block] + [pl.BlockSpec(memory_space=pl.ANY)] * (2 + len(tiles)),
            out_specs=block,
            scratch_shapes=[pltpu.VMEM((total_keys, width), jnp.bfloat16)] * 2
            + [pltpu.SemaphoreType.DMA((2, len(tiles) + 1))],
        ),
        out_shape=jax.ShapeDtypeStruct((1, rows, out_width), jnp.bfloat16),
        cost_estimate=pl.CostEstimate(
            flops=4 * pairs * HDIM,
            bytes_accessed=heads * HDIM * 2 * (2 * total_keys + 2 * rows),
            transcendentals=pairs,
        ),
        compiler_params=pltpu.CompilerParams(vmem_limit_bytes=vmem_limit),
    )(info, q, text_k, text_v, *[array for array, _ in tiles])


def after(x, *others):
    return lax.optimization_barrier((x, *others))[0]


def body(queries, keys, values, text_keys, text_values, text_count):
    n_seq, n_sp = lax.axis_size("seq"), lax.axis_size("sp")
    tile = lax.axis_index("sp") * n_seq + lax.axis_index("seq")
    col, odd, pair = tile % COLS, tile // COLS % 2, tile // (2 * COLS)
    n_tiles, span = n_sp * n_seq, 2 * COLS
    n_pairs = n_tiles // span
    if lax.axis_size("rep") > 1:
        keys = lax.all_gather(keys, "rep", axis=1, tiled=True)
        values = lax.all_gather(values, "rep", axis=1, tiled=True)
    width = queries.shape[2]
    half = width // 2
    part = half // CHUNKS
    part_heads = part // HDIM
    mine, other = odd * half, (1 - odd) * half

    def xor(x, mask, keep=lambda i: True):
        return lax.ppermute(x, "seq", [(i, i ^ mask) for i in range(n_seq) if keep(i)])

    def swap(x):
        return xor(x, COLS)

    def halo(x, down):
        pairs = [(i, i + span if i // COLS % 2 == down else i - span) for i in range(n_tiles)]
        place = lambda i: i % n_seq * n_sp + i // n_seq
        pairs = [(place(i), place(j)) for i, j in pairs if 0 <= j < n_tiles]
        return lax.ppermute(x, ("seq", "sp"), pairs)

    def across(x, first):
        return [
            (x, first),
            (xor(x, 1), first),
            (xor(x, 3, lambda i: i % COLS in (1, 2)), first),
        ]

    def window(own, got, halos):
        return [own[0], own[1], got[0], got[1], own[2], got[2], *halos]

    low_halo, high_halo = pair > 0, pair < n_pairs - 1
    got_halo = jnp.where(odd == 1, low_halo, high_halo)
    own_halo = jnp.where(odd == 1, high_halo, low_halo)
    entries = (mine // HDIM, (col == 1) | (col == 2), text_count[0], got_halo, own_halo)
    info = jnp.stack([jnp.asarray(x, jnp.int32) for x in entries])
    got_flag, own_flag = 3, 4

    (sent,) = pack([([keys, values], other, half)])
    got = swap(sent)
    own, *q_sent = pack(
        [([after(keys, sent), after(values, sent)], mine, half)]
        + [([queries], other + c * part, part) for c in range(CHUNKS)]
    )
    own_row = across(own, 0)
    near_row = across(halo(own, 1), 0)
    got = after(got, *[x for x, _ in near_row[1:]])
    q_got = [swap(after(q_sent[0], got))]
    got_row = across(got, 0)
    far = halo(got, 0)
    for c in range(1, CHUNKS):
        q_got.append(swap(after(q_sent[c], q_got[-1] if c > 1 else got_row[1][0])))

    def shifted(row, c):
        return [(x, c * part_heads) for x, _ in row]

    back = []
    for c in range(CHUNKS):
        tiles = window(shifted(own_row, c), shifted(got_row, c), shifted(near_row, c))
        o = attend(
            info, got_flag, q_got[c], text_keys, text_values, tiles, c * part_heads, part_heads,
            part,
        )
        back.append(swap(o))
        if c == 0:
            far_row = across(after(far, o), 0)
    out = attend(
        info, own_flag, after(queries, o), text_keys, text_values,
        window(own_row, got_row, far_row), 0, half // HDIM, width, q_full=True,
    )
    for c in range(CHUNKS):
        out = lax.dynamic_update_slice_in_dim(out, back[c], other + c * part, 2)
    return out


def solution(mesh):
    in_specs = (
        P(("grp", "sp", "seq"), "rep", None),
        P(("grp", "sp", "seq"), "rep", None),
        P(("grp", "sp", "seq"), "rep", None),
        P("grp", None),
        P("grp", None),
        P("grp"),
    )
    out_specs = P(("grp", "sp", "seq"), "rep", None)
    return jax.shard_map(body, mesh=mesh, in_specs=in_specs, out_specs=out_specs, check_vma=False)
```

```python
import functools
import math

import jax
import jax.numpy as jnp
from jax import lax
from jax.experimental import pallas as pl
from jax.experimental.pallas import tpu as pltpu
from jax.sharding import PartitionSpec as P

HDIM = 128
COLS = 4

masked_score = -1e30
exp2_scale = math.log2(math.e) / math.sqrt(HDIM)
vmem_limit = 56 * 2**20


def pack_kernel(sizes, at, *refs):
    sources, outs = refs[: sum(sizes)], refs[sum(sizes) :]
    i = 0
    for size, out in zip(sizes, outs):
        for j in range(size):
            out[j] = sources[i + j][0]
        i += size


def pack(groups):
    sizes = [len(sources) for sources, _, _ in groups]
    at = jnp.stack([jnp.asarray(column // width, jnp.int32) for _, column, width in groups])

    def source_spec(g, length, width):
        return pl.BlockSpec((1, length, width), lambda _, at: (0, 0, at[g]))

    in_specs, out_specs, out_shape, args = [], [], [], []
    for g, (sources, _, width) in enumerate(groups):
        length = sources[0].shape[1]
        in_specs += [source_spec(g, length, width)] * len(sources)
        args += sources
        out_specs.append(pl.BlockSpec((len(sources), length, width), lambda _, at: (0, 0, 0)))
        out_shape.append(jax.ShapeDtypeStruct((len(sources), length, width), jnp.bfloat16))
    return pl.pallas_call(
        functools.partial(pack_kernel, sizes),
        grid_spec=pltpu.PrefetchScalarGridSpec(
            num_scalar_prefetch=1, grid=(1,), in_specs=in_specs, out_specs=out_specs
        ),
        out_shape=out_shape,
        cost_estimate=pl.CostEstimate(
            flops=0, bytes_accessed=sum(4 * math.prod(o.shape) for o in out_shape), transcendentals=0
        ),
        compiler_params=pltpu.CompilerParams(vmem_limit_bytes=vmem_limit),
    )(at, *args)


def join_kernel(*refs):
    for j, ref in enumerate(refs[:-1]):
        refs[-1][j] = ref[...]


def join(tiles):
    shape = (len(tiles), *tiles[0].shape)
    return pl.pallas_call(
        join_kernel,
        out_shape=jax.ShapeDtypeStruct(shape, jnp.bfloat16),
        cost_estimate=pl.CostEstimate(
            flops=0, bytes_accessed=4 * math.prod(shape), transcendentals=0
        ),
        compiler_params=pltpu.CompilerParams(vmem_limit_bytes=vmem_limit),
    )(*tiles)


def attend_kernel(flag, turn, info, q_a, q_b, text_k, text_v, own, other, halo, *refs):
    out_a, out_b, keys, vals, sems = refs
    length, width = own.shape[2:]
    text_len = text_k.shape[0]
    base = info[0]
    head_at = pl.multiple_of(info[1] * HDIM, HDIM)
    text_live = lax.broadcasted_iota(jnp.int32, (1, text_len), 1) < info[2]

    pieces = [(own, 0), (own, 1), (other, 0), (other, 1), None, (halo, 0), (halo, 1)]
    pieces += [(own, 2), (other, 2), (halo, 2)]
    ends = [0]
    always, on_halo = [], []
    for i, piece in enumerate(pieces):
        ends.append(ends[-1] + (text_len if piece is None else length))
        for side, text, dst in ((0, text_k, keys), (1, text_v, vals)):
            if piece is None:
                src = text.at[:, pl.ds(head_at, width)]
            else:
                src = piece[0].at[base ^ (piece[1] ^ turn), side]
            copy = pltpu.make_async_copy(src, dst.at[ends[i] : ends[i + 1]], sems.at[side, i])
            (on_halo if piece is not None and piece[0] is halo else always).append(copy)
    for copy in always:
        copy.start()

    @pl.when(info[flag] == 1)
    def _():
        for copy in on_halo:
            copy.start()

    for copy in always:
        copy.wait()

    def run(with_halo):
        main = ends[7] if with_halo else ends[5]
        inner = slice(ends[7], ends[10] if with_halo else ends[9])
        if with_halo:
            for copy in on_halo:
                copy.wait()
        rows = q_a.shape[1]

        def scores_of(q, span, head):
            return lax.dot_general(
                q, keys[span, head], (((1,), (1,)), ((), ())), preferred_element_type=jnp.float32
            )

        for j in range(width // HDIM):
            head = slice(j * HDIM, (j + 1) * HDIM)
            first, second = q_a[0, :, head], q_b[0, :, head]
            q_outer = jnp.where(base == 0, first, second)
            q_inner = jnp.where(base == 0, second, first)
            both = jnp.concatenate([q_outer, q_inner], axis=0)
            s_main = scores_of(both, slice(0, main), head)
            s_inner = scores_of(q_inner, inner, head)
            parts = [
                s_main[:, : ends[4]],
                jnp.where(text_live, s_main[:, ends[4] : ends[5]], masked_score),
            ]
            if with_halo:
                parts.append(s_main[:, ends[5] :])
            tops = [jnp.max(s, axis=-1, keepdims=True) for s in parts]
            top = functools.reduce(jnp.maximum, tops)
            top_inner = jnp.maximum(top[rows:], jnp.max(s_inner, axis=-1, keepdims=True))
            top = jnp.concatenate([top[:rows], top_inner], axis=0) * exp2_scale
            total, summed, at = 0.0, 0.0, 0
            for s in parts:
                w = jnp.exp2(s * exp2_scale - top)
                total = total + jnp.sum(w, axis=-1, keepdims=True)
                summed = summed + jnp.dot(
                    w.astype(jnp.bfloat16),
                    vals[at : at + s.shape[1], head],
                    preferred_element_type=jnp.float32,
                )
                at += s.shape[1]
            w = jnp.exp2(s_inner * exp2_scale - top[rows:])
            total_inner = total[rows:] + jnp.sum(w, axis=-1, keepdims=True)
            summed_inner = summed[rows:] + jnp.dot(
                w.astype(jnp.bfloat16), vals[inner, head], preferred_element_type=jnp.float32
            )
            o_outer = (summed[:rows] / total[:rows]).astype(jnp.bfloat16)
            o_inner = (summed_inner / total_inner).astype(jnp.bfloat16)
            out_a[0, :, head] = jnp.where(base == 0, o_outer, o_inner)
            out_b[0, :, head] = jnp.where(base == 0, o_inner, o_outer)

    pl.when(info[flag] == 1)(lambda: run(True))
    pl.when(info[flag] == 0)(lambda: run(False))


def attend(info, flag, turn, q_a, q_b, text_k, text_v, own, other, halo):
    rows = q_b.shape[1]
    length, width = own.shape[2:]
    heads = width // HDIM
    text_len = text_k.shape[0]
    block = pl.BlockSpec((1, rows, width), lambda _, info: (0, 0, 0))
    mine = pl.BlockSpec((1, rows, width), lambda _, info: (0, 0, info[1] // heads))
    total_keys = 9 * length + text_len
    pairs = heads * 2 * rows * total_keys
    return pl.pallas_call(
        functools.partial(attend_kernel, flag, turn),
        grid_spec=pltpu.PrefetchScalarGridSpec(
            num_scalar_prefetch=1,
            grid=(1,),
            in_specs=[block if q_a.shape[2] == width else mine, block]
            + [pl.BlockSpec(memory_space=pl.ANY)] * 5,
            out_specs=[block, block],
            scratch_shapes=[pltpu.VMEM((total_keys, width), jnp.bfloat16)] * 2
            + [pltpu.SemaphoreType.DMA((2, 10))],
        ),
        out_shape=[jax.ShapeDtypeStruct((1, rows, width), jnp.bfloat16)] * 2,
        cost_estimate=pl.CostEstimate(
            flops=4 * pairs * HDIM,
            bytes_accessed=heads * HDIM * 2 * (2 * total_keys + 4 * rows),
            transcendentals=pairs,
        ),
        compiler_params=pltpu.CompilerParams(vmem_limit_bytes=vmem_limit),
    )(info, q_a, q_b, text_k, text_v, own, other, halo)


def spread_kernel(info, *refs):
    out, width = refs[-1], refs[0].shape[2]
    for k, ref in enumerate(refs[:-1]):
        at = pl.multiple_of((info[0] ^ k) * width, width)
        out[0, :, pl.ds(at, width)] = ref[0]


def spread(place, pieces):
    _, rows, width = pieces[0].shape
    return pl.pallas_call(
        spread_kernel,
        in_specs=[pl.BlockSpec(memory_space=pltpu.SMEM)]
        + [pl.BlockSpec(memory_space=pltpu.VMEM)] * len(pieces),
        out_shape=jax.ShapeDtypeStruct((1, rows, width * len(pieces)), jnp.bfloat16),
        compiler_params=pltpu.CompilerParams(vmem_limit_bytes=vmem_limit),
    )(place, *pieces)


def after(x, *others):
    return lax.optimization_barrier((x, *others))[0]


def body(queries, keys, values, text_keys, text_values, text_count):
    n_seq, n_sp = lax.axis_size("seq"), lax.axis_size("sp")
    tile = lax.axis_index("sp") * n_seq + lax.axis_index("seq")
    n_tiles, span = n_sp * n_seq, 2 * COLS
    col, odd, place, pair = tile % COLS, tile // COLS % 2, tile % span, tile // span
    n_pairs = n_tiles // span
    if lax.axis_size("rep") > 1:
        keys = lax.all_gather(keys, "rep", axis=1, tiled=True)
        values = lax.all_gather(values, "rep", axis=1, tiled=True)
    part = queries.shape[2] // span
    near_slots, far_slots = range(COLS), range(COLS, span)

    def send(x, k):
        return lax.ppermute(x, "seq", [(i, i ^ k) for i in range(n_seq)])

    def to_halo(x, down):
        pairs = [(i, i + span if i // COLS % 2 == down else i - span) for i in range(n_tiles)]
        flat = lambda i: i % n_seq * n_sp + i // n_seq
        pairs = [(flat(i), flat(j)) for i, j in pairs if 0 <= j < n_tiles]
        return lax.ppermute(x, ("seq", "sp"), pairs)

    low_halo, high_halo = pair > 0, pair < n_pairs - 1
    near_halo = jnp.where(odd == 1, low_halo, high_halo)
    far_halo = jnp.where(odd == 1, high_halo, low_halo)
    base = (col == 1) | (col == 2)
    entries = (base, place * (part // HDIM), text_count[0], near_halo, far_halo)
    info = jnp.stack([jnp.asarray(x, jnp.int32) for x in entries])

    def cut(sources, slots):
        return pack([(sources, (place ^ k) * part, part) for k in slots])

    sent = cut([keys, values], far_slots)
    far = {k: send(x, k) for k, x in zip(far_slots, sent)}
    later_k, later_v = after(keys, *sent), after(values, *sent)
    sent = cut([later_k, later_v], near_slots)
    near = {k: send(x, k) if k else x for k, x in zip(near_slots, sent)}
    q_sent = cut([queries], range(1, span))
    q_sent = dict(zip(range(1, span), q_sent))

    own = join([near[k] for k in near_slots])
    q = {k: send(after(q_sent[k], own), k) for k in (4, 5, 1, 2, 3)}
    own_halo = to_halo(own, 1)
    other = join([far[k] for k in far_slots])
    q.update({k: send(after(q_sent[k], other), k) for k in (6, 7)})
    other_halo = to_halo(other, 0)
    o = {}

    def run(flag, a, b, q_a, q_b, mine, theirs, halo):
        turn = 3 if a % COLS else 0
        return attend(info, flag, turn, q_a, q_b, text_keys, text_values, mine, theirs, halo)

    o[4], o[5] = run(3, 4, 5, q[4], q[5], own, other, own_halo)
    for k in (4, 5):
        o[k] = send(o[k], k)
    x7, x6 = run(3, 7, 6, q[7], q[6], own, other, own_halo)
    o[7], o[6] = send(x7, 7), send(x6, 6)
    x3, x2 = run(4, 3, 2, after(q[3], x7), q[2], own, other, other_halo)
    o[3], o[2] = send(x3, 3), send(x2, 2)
    o[0], x1 = run(4, 0, 1, queries, after(q[1], x3), own, other, other_halo)
    o[1] = send(x1, 1)
    return spread(place.reshape(1), [o[k] for k in range(span)])


def solution(mesh):
    in_specs = (
        P(("grp", "sp", "seq"), "rep", None),
        P(("grp", "sp", "seq"), "rep", None),
        P(("grp", "sp", "seq"), "rep", None),
        P("grp", None),
        P("grp", None),
        P("grp"),
    )
    out_specs = P(("grp", "sp", "seq"), "rep", None)
    return jax.shard_map(body, mesh=mesh, in_specs=in_specs, out_specs=out_specs, check_vma=False)
```

```python
import functools
import math

import jax
import jax.numpy as jnp
from jax import lax
from jax.experimental import pallas as pl
from jax.experimental.pallas import tpu as pltpu
from jax.sharding import PartitionSpec as P

HDIM = 128
COLS = 4

masked_score = -1e30
exp2_scale = math.log2(math.e) / math.sqrt(HDIM)
vmem_limit = 20 * 2**20


def pack_kernel(width, slots, at, *refs):
    sources, outs = refs[: -len(slots)], refs[-len(slots) :]
    for k, out in zip(slots, outs):
        head = pl.multiple_of((at[0] ^ k) * width, width)
        for j, source in enumerate(sources):
            out[j] = source[0, :, pl.ds(head, width)]


def pack(place, sources, width, slots):
    shape = (len(sources), sources[0].shape[1], width)
    return pl.pallas_call(
        functools.partial(pack_kernel, width, slots),
        in_specs=[pl.BlockSpec(memory_space=pltpu.SMEM)]
        + [pl.BlockSpec(memory_space=pltpu.VMEM)] * len(sources),
        out_shape=[jax.ShapeDtypeStruct(shape, jnp.bfloat16)] * len(slots),
        cost_estimate=pl.CostEstimate(
            flops=0, bytes_accessed=4 * len(slots) * math.prod(shape), transcendentals=0
        ),
        compiler_params=pltpu.CompilerParams(vmem_limit_bytes=vmem_limit),
    )(place, *sources)


def join_kernel(*refs):
    for j, ref in enumerate(refs[:-1]):
        refs[-1][j] = ref[...]


def join(tiles):
    shape = (len(tiles), *tiles[0].shape)
    return pl.pallas_call(
        join_kernel,
        out_shape=jax.ShapeDtypeStruct(shape, jnp.bfloat16),
        cost_estimate=pl.CostEstimate(
            flops=0, bytes_accessed=4 * math.prod(shape), transcendentals=0
        ),
        compiler_params=pltpu.CompilerParams(vmem_limit_bytes=vmem_limit),
    )(*tiles)


def attend_kernel(flag, turn, info, q_a, q_b, text_k, text_v, own, other, halo, *refs):
    out_a, out_b, queries, keys, vals, sems = refs
    length, width = own.shape[2:]
    text_len = text_k.shape[0]
    base = info[0]
    head_at = pl.multiple_of(info[1] * HDIM, HDIM)
    text_live = lax.broadcasted_iota(jnp.int32, (1, text_len), 1) < info[2]

    pieces = [(own, 0), (own, 1), (other, 0), (other, 1), None, (halo, 0), (halo, 1)]
    pieces += [(own, 2), (other, 2), (halo, 2)]
    ends = [0]
    always, on_halo = [[], []], [[], []]
    for i, (q, place) in enumerate(((q_a, base), (q_b, 1 - base))):
        lanes = slice(None) if q.shape[2] == width else pl.ds(head_at, width)
        always[0].append(
            pltpu.make_async_copy(q.at[0, :, lanes], queries.at[place], sems.at[i, 10])
        )
    for i, piece in enumerate(pieces):
        ends.append(ends[-1] + (text_len if piece is None else length))
        for side, text, dst in ((0, text_k, keys), (1, text_v, vals)):
            if piece is None:
                src = text.at[:, pl.ds(head_at, width)]
            else:
                src = piece[0].at[base ^ (piece[1] ^ turn), side]
            copy = pltpu.make_async_copy(src, dst.at[ends[i] : ends[i + 1]], sems.at[side, i])
            (on_halo if piece is not None and piece[0] is halo else always)[side].append(copy)

    def each(copies, action):
        for copy in copies:
            action(copy)

    each(always[0], lambda copy: copy.start())
    pl.when(info[flag] == 1)(lambda: each(on_halo[0], lambda copy: copy.start()))
    each(always[1], lambda copy: copy.start())
    pl.when(info[flag] == 1)(lambda: each(on_halo[1], lambda copy: copy.start()))
    each(always[0], lambda copy: copy.wait())

    def run(with_halo):
        main = ends[7] if with_halo else ends[5]
        inner = slice(ends[7], ends[10] if with_halo else ends[9])
        if with_halo:
            each(on_halo[0], lambda copy: copy.wait())
        rows = q_a.shape[1]

        def scores_of(q, span, head):
            return lax.dot_general(
                q, keys[span, head], (((1,), (1,)), ((), ())), preferred_element_type=jnp.float32
            )

        for j in range(width // HDIM):
            head = slice(j * HDIM, (j + 1) * HDIM)
            both = queries[:, :, head].reshape(2 * rows, HDIM)
            q_inner = queries[1, :, head]
            s_main = scores_of(both, slice(0, main), head)
            s_inner = scores_of(q_inner, inner, head)
            parts = [
                s_main[:, : ends[4]],
                jnp.where(text_live, s_main[:, ends[4] : ends[5]], masked_score),
            ]
            if with_halo:
                parts.append(s_main[:, ends[5] :])
            tops = [jnp.max(s, axis=-1, keepdims=True) for s in parts]
            top = functools.reduce(jnp.maximum, tops)
            top_inner = jnp.maximum(top[rows:], jnp.max(s_inner, axis=-1, keepdims=True))
            top = jnp.concatenate([top[:rows], top_inner], axis=0) * exp2_scale
            if j == 0:
                each(always[1] + (on_halo[1] if with_halo else []), lambda copy: copy.wait())
            total, summed, at = 0.0, 0.0, 0
            for s in parts:
                w = jnp.exp2(s * exp2_scale - top)
                total = total + jnp.sum(w, axis=-1, keepdims=True)
                summed = summed + jnp.dot(
                    w.astype(jnp.bfloat16),
                    vals[at : at + s.shape[1], head],
                    preferred_element_type=jnp.float32,
                )
                at += s.shape[1]
            w = jnp.exp2(s_inner * exp2_scale - top[rows:])
            total_inner = total[rows:] + jnp.sum(w, axis=-1, keepdims=True)
            summed_inner = summed[rows:] + jnp.dot(
                w.astype(jnp.bfloat16), vals[inner, head], preferred_element_type=jnp.float32
            )
            o_outer = (summed[:rows] / total[:rows]).astype(jnp.bfloat16)
            o_inner = (summed_inner / total_inner).astype(jnp.bfloat16)
            out_a[0, :, head] = jnp.where(base == 0, o_outer, o_inner)
            out_b[0, :, head] = jnp.where(base == 0, o_inner, o_outer)

    pl.when(info[flag] == 1)(lambda: run(True))
    pl.when(info[flag] == 0)(lambda: run(False))


def attend(info, flag, turn, q_a, q_b, text_k, text_v, own, other, halo):
    rows = q_b.shape[1]
    length, width = own.shape[2:]
    heads = width // HDIM
    text_len = text_k.shape[0]
    block = pl.BlockSpec((1, rows, width), lambda _, info: (0, 0, 0))
    total_keys = 9 * length + text_len
    pairs = heads * 2 * rows * total_keys
    return pl.pallas_call(
        functools.partial(attend_kernel, flag, turn),
        grid_spec=pltpu.PrefetchScalarGridSpec(
            num_scalar_prefetch=1,
            grid=(1,),
            in_specs=[pl.BlockSpec(memory_space=pl.ANY)] * 7,
            out_specs=[block, block],
            scratch_shapes=[pltpu.VMEM((2, rows, width), jnp.bfloat16)]
            + [pltpu.VMEM((total_keys, width), jnp.bfloat16)] * 2
            + [pltpu.SemaphoreType.DMA((2, 11))],
        ),
        out_shape=[jax.ShapeDtypeStruct((1, rows, width), jnp.bfloat16)] * 2,
        cost_estimate=pl.CostEstimate(
            flops=4 * pairs * HDIM,
            bytes_accessed=heads * HDIM * 2 * (2 * total_keys + 4 * rows),
            transcendentals=pairs,
        ),
        compiler_params=pltpu.CompilerParams(vmem_limit_bytes=vmem_limit),
    )(info, q_a, q_b, text_k, text_v, own, other, halo)


def spread_kernel(info, *refs):
    out, width = refs[-1], refs[0].shape[2]
    for k, ref in enumerate(refs[:-1]):
        at = pl.multiple_of((info[0] ^ k) * width, width)
        out[0, :, pl.ds(at, width)] = ref[0]


def spread(place, pieces):
    _, rows, width = pieces[0].shape
    return pl.pallas_call(
        spread_kernel,
        in_specs=[pl.BlockSpec(memory_space=pltpu.SMEM)]
        + [pl.BlockSpec(memory_space=pltpu.VMEM)] * len(pieces),
        out_shape=jax.ShapeDtypeStruct((1, rows, width * len(pieces)), jnp.bfloat16),
        compiler_params=pltpu.CompilerParams(vmem_limit_bytes=vmem_limit),
    )(place, *pieces)


def after(x, *others):
    return lax.optimization_barrier((x, *others))[0]


def body(queries, keys, values, text_keys, text_values, text_count):
    n_seq, n_sp = lax.axis_size("seq"), lax.axis_size("sp")
    tile = lax.axis_index("sp") * n_seq + lax.axis_index("seq")
    n_tiles, span = n_sp * n_seq, 2 * COLS
    col, odd, place, pair = tile % COLS, tile // COLS % 2, tile % span, tile // span
    n_pairs = n_tiles // span
    if lax.axis_size("rep") > 1:
        keys = lax.all_gather(keys, "rep", axis=1, tiled=True)
        values = lax.all_gather(values, "rep", axis=1, tiled=True)
    part = queries.shape[2] // span
    near_slots, far_slots = range(COLS), range(COLS, span)

    def send(x, k):
        return lax.ppermute(x, "seq", [(i, i ^ k) for i in range(n_seq)])

    def to_halo(x, down):
        pairs = [(i, i + span if i // COLS % 2 == down else i - span) for i in range(n_tiles)]
        flat = lambda i: i % n_seq * n_sp + i // n_seq
        pairs = [(flat(i), flat(j)) for i, j in pairs if 0 <= j < n_tiles]
        return lax.ppermute(x, ("seq", "sp"), pairs)

    low_halo, high_halo = pair > 0, pair < n_pairs - 1
    near_halo = jnp.where(odd == 1, low_halo, high_halo)
    far_halo = jnp.where(odd == 1, high_halo, low_halo)
    base = (col == 1) | (col == 2)
    entries = (base, place * (part // HDIM), text_count[0], near_halo, far_halo)
    info = jnp.stack([jnp.asarray(x, jnp.int32) for x in entries])

    block = place.reshape(1)
    sent = pack(block, [keys, values], part, [*far_slots, *near_slots])
    sent = dict(zip([*far_slots, *near_slots], sent))
    far = {k: send(sent[k], k) for k in far_slots}
    near = {k: send(sent[k], k) if k else sent[k] for k in near_slots}
    q_sent = pack(block, [queries], part, range(1, span))
    q_sent = dict(zip(range(1, span), q_sent))
    near[1], *_ = lax.optimization_barrier((near[1], *q_sent.values()))

    own = join([near[k] for k in near_slots])
    q = {k: send(after(q_sent[k], own), k) for k in (4, 5, 1, 2, 3)}
    own_halo = to_halo(own, 1)
    other = join([far[k] for k in far_slots])
    q.update({k: send(after(q_sent[k], other), k) for k in (6, 7)})
    other_halo = to_halo(other, 0)
    o = {}

    def run(flag, a, b, q_a, q_b, mine, theirs, halo):
        turn = 3 if a % COLS else 0
        return attend(info, flag, turn, q_a, q_b, text_keys, text_values, mine, theirs, halo)

    o[4], o[5] = run(3, 4, 5, q[4], q[5], own, other, own_halo)
    for k in (4, 5):
        o[k] = send(o[k], k)
    x7, x6 = run(3, 7, 6, q[7], q[6], own, other, own_halo)
    o[7], o[6] = send(x7, 7), send(x6, 6)
    x3, x2 = run(4, 3, 2, after(q[3], x7), q[2], own, other, other_halo)
    o[3], o[2] = send(x3, 3), send(x2, 2)
    o[0], x1 = run(4, 0, 1, queries, after(q[1], x3), own, other, other_halo)
    o[1] = send(x1, 1)
    return spread(block, [o[k] for k in range(span)])


def solution(mesh):
    in_specs = (
        P(("grp", "sp", "seq"), "rep", None),
        P(("grp", "sp", "seq"), "rep", None),
        P(("grp", "sp", "seq"), "rep", None),
        P("grp", None),
        P("grp", None),
        P("grp"),
    )
    out_specs = P(("grp", "sp", "seq"), "rep", None)
    return jax.shard_map(body, mesh=mesh, in_specs=in_specs, out_specs=out_specs, check_vma=False)
```

```python
import functools
import math

import jax
import jax.numpy as jnp
from jax import lax
from jax.experimental import pallas as pl
from jax.experimental.pallas import tpu as pltpu
from jax.sharding import PartitionSpec as P

HDIM = 128
COLS = 4

masked_score = -1e30
exp2_scale = math.log2(math.e) / math.sqrt(HDIM)
vmem_limit = 20 * 2**20


def pack_kernel(width, slots, at, *refs):
    sources, outs = refs[: -len(slots)], refs[-len(slots) :]
    for k, out in zip(slots, outs):
        head = pl.multiple_of((at[0] ^ k) * width, width)
        for j, source in enumerate(sources):
            out[j] = source[0, :, pl.ds(head, width)]


def pack(place, sources, width, slots):
    shape = (len(sources), sources[0].shape[1], width)
    return pl.pallas_call(
        functools.partial(pack_kernel, width, slots),
        in_specs=[pl.BlockSpec(memory_space=pltpu.SMEM)]
        + [pl.BlockSpec(memory_space=pltpu.VMEM)] * len(sources),
        out_shape=[jax.ShapeDtypeStruct(shape, jnp.bfloat16)] * len(slots),
        cost_estimate=pl.CostEstimate(
            flops=0, bytes_accessed=4 * len(slots) * math.prod(shape), transcendentals=0
        ),
        compiler_params=pltpu.CompilerParams(vmem_limit_bytes=vmem_limit),
    )(place, *sources)


def join_kernel(*refs):
    for j, ref in enumerate(refs[:-1]):
        refs[-1][j] = ref[...]


def join(tiles):
    shape = (len(tiles), *tiles[0].shape)
    return pl.pallas_call(
        join_kernel,
        out_shape=jax.ShapeDtypeStruct(shape, jnp.bfloat16),
        cost_estimate=pl.CostEstimate(
            flops=0, bytes_accessed=4 * math.prod(shape), transcendentals=0
        ),
        compiler_params=pltpu.CompilerParams(vmem_limit_bytes=vmem_limit),
    )(*tiles)


def attend_kernel(flag, turns, info, *refs):
    n = 2 * len(turns)
    queries, (text_k, text_v, own, other, halo) = refs[:n], refs[n : n + 5]
    outs, (keys, vals) = refs[n + 5 : 2 * n + 5], refs[2 * n + 5 :]
    length, width = own.shape[2:]
    rows = queries[0].shape[1]
    text_len = text_k.shape[0]
    base = info[0]
    lanes = pl.ds(pl.multiple_of(info[1] * HDIM, HDIM), width)
    text_live = lax.broadcasted_iota(jnp.int32, (1, text_len), 1) < info[2]

    def run(turn, q_refs, out_refs, with_halo):
        pieces = [(own, 0), (own, 1), (other, 0), (other, 1), None]
        pieces += [(halo, 0), (halo, 1)] if with_halo else []
        cut = len(pieces)
        pieces += [(own, 2), (other, 2)] + ([(halo, 2)] if with_halo else [])
        ends = [0]
        for piece in pieces:
            at = slice(ends[-1], ends[-1] + (text_len if piece is None else length))
            for side, text, dst in ((0, text_k, keys), (1, text_v, vals)):
                if piece is None:
                    dst[at] = text[:, lanes]
                else:
                    dst[at] = piece[0][base ^ (piece[1] ^ turn), side]
            ends.append(at.stop)
        main, inner = ends[cut], slice(ends[cut], ends[-1])
        first, second = [
            ref[0] if ref.shape[2] == width else ref[0, :, lanes] for ref in q_refs
        ]
        q_outer = jnp.where(base == 0, first, second)
        q_inner = jnp.where(base == 0, second, first)
        q_both = jnp.concatenate([q_outer, q_inner], axis=0)

        def scores_of(q, span, head):
            return lax.dot_general(
                q[:, head],
                keys[span, head],
                (((1,), (1,)), ((), ())),
                preferred_element_type=jnp.float32,
            )

        for j in range(width // HDIM):
            head = slice(j * HDIM, (j + 1) * HDIM)
            s_main = scores_of(q_both, slice(0, main), head)
            s_inner = scores_of(q_inner, inner, head)
            parts = [
                s_main[:, : ends[4]],
                jnp.where(text_live, s_main[:, ends[4] : ends[5]], masked_score),
            ]
            if with_halo:
                parts.append(s_main[:, ends[5] :])
            tops = [jnp.max(s, axis=-1, keepdims=True) for s in parts]
            top = functools.reduce(jnp.maximum, tops)
            top_inner = jnp.maximum(top[rows:], jnp.max(s_inner, axis=-1, keepdims=True))
            top = jnp.concatenate([top[:rows], top_inner], axis=0) * exp2_scale
            total, summed, at = 0.0, 0.0, 0
            for s in parts:
                w = jnp.exp2(s * exp2_scale - top)
                total = total + jnp.sum(w, axis=-1, keepdims=True)
                summed = summed + jnp.dot(
                    w.astype(jnp.bfloat16),
                    vals[at : at + s.shape[1], head],
                    preferred_element_type=jnp.float32,
                )
                at += s.shape[1]
            w = jnp.exp2(s_inner * exp2_scale - top[rows:])
            total_inner = total[rows:] + jnp.sum(w, axis=-1, keepdims=True)
            summed_inner = summed[rows:] + jnp.dot(
                w.astype(jnp.bfloat16), vals[inner, head], preferred_element_type=jnp.float32
            )
            o_outer = (summed[:rows] / total[:rows]).astype(jnp.bfloat16)
            o_inner = (summed_inner / total_inner).astype(jnp.bfloat16)
            out_refs[0][0, :, head] = jnp.where(base == 0, o_outer, o_inner)
            out_refs[1][0, :, head] = jnp.where(base == 0, o_inner, o_outer)

    for with_halo in (True, False):

        @pl.when(info[flag] == int(with_halo))
        def _():
            for t, turn in enumerate(turns):
                pair = slice(2 * t, 2 * t + 2)
                run(turn, queries[pair], outs[pair], with_halo)


def attend(info, flag, turns, queries, text_k, text_v, own, other, halo):
    rows = queries[-1].shape[1]
    length, width = own.shape[2:]
    total_keys = 9 * length + text_k.shape[0]
    pairs = len(queries) * width // HDIM * rows * total_keys
    return pl.pallas_call(
        functools.partial(attend_kernel, flag, turns),
        in_specs=[pl.BlockSpec(memory_space=pltpu.SMEM)]
        + [pl.BlockSpec(memory_space=pltpu.VMEM)] * (len(queries) + 5),
        scratch_shapes=[pltpu.VMEM((total_keys, width), jnp.bfloat16)] * 2,
        out_shape=[jax.ShapeDtypeStruct((1, rows, width), jnp.bfloat16)] * len(queries),
        cost_estimate=pl.CostEstimate(
            flops=4 * pairs * HDIM,
            bytes_accessed=width * 4 * (total_keys + rows * len(queries)),
            transcendentals=pairs,
        ),
        compiler_params=pltpu.CompilerParams(vmem_limit_bytes=vmem_limit),
    )(info, *queries, text_k, text_v, own, other, halo)


def spread_kernel(slots, place, *refs):
    out, sems = refs[-2:]
    width = refs[0].shape[2]
    copies = []
    for i, (k, ref) in enumerate(zip(slots, refs)):
        at = pl.multiple_of((place[0] ^ k) * width, width)
        copies.append(pltpu.make_async_copy(ref, out.at[:, :, pl.ds(at, width)], sems.at[i]))
    for copy in copies:
        copy.start()
    for copy in copies:
        copy.wait()


def spread(place, pieces, out_width, into=None):
    slots = sorted(pieces)
    shape = (*pieces[slots[0]].shape[:2], out_width)
    extra = [] if into is None else [into]
    return pl.pallas_call(
        functools.partial(spread_kernel, slots),
        in_specs=[pl.BlockSpec(memory_space=pltpu.SMEM)]
        + [pl.BlockSpec(memory_space=pltpu.VMEM)] * len(slots)
        + [pl.BlockSpec(memory_space=pl.ANY)] * len(extra),
        out_specs=pl.BlockSpec(memory_space=pl.ANY),
        out_shape=jax.ShapeDtypeStruct(shape, jnp.bfloat16),
        input_output_aliases={1 + len(slots): 0} if extra else {},
        scratch_shapes=[pltpu.SemaphoreType.DMA((len(slots),))],
        cost_estimate=pl.CostEstimate(
            flops=0, bytes_accessed=4 * math.prod(shape), transcendentals=0
        ),
        compiler_params=pltpu.CompilerParams(vmem_limit_bytes=vmem_limit),
    )(place, *[pieces[k] for k in slots], *extra)


def after(x, *others):
    return lax.optimization_barrier((x, *others))[0]


def body(queries, keys, values, text_keys, text_values, text_count):
    n_seq, n_sp = lax.axis_size("seq"), lax.axis_size("sp")
    tile = lax.axis_index("sp") * n_seq + lax.axis_index("seq")
    n_tiles, span = n_sp * n_seq, 2 * COLS
    col, odd, place, pair = tile % COLS, tile // COLS % 2, tile % span, tile // span
    n_pairs = n_tiles // span
    if lax.axis_size("rep") > 1:
        keys = lax.all_gather(keys, "rep", axis=1, tiled=True)
        values = lax.all_gather(values, "rep", axis=1, tiled=True)
    part = queries.shape[2] // span
    near_slots, far_slots = range(COLS), range(COLS, span)

    def send(x, k):
        return lax.ppermute(x, "seq", [(i, i ^ k) for i in range(n_seq)])

    def to_halo(x, down):
        pairs = [(i, i + span if i // COLS % 2 == down else i - span) for i in range(n_tiles)]
        flat = lambda i: i % n_seq * n_sp + i // n_seq
        pairs = [(flat(i), flat(j)) for i, j in pairs if 0 <= j < n_tiles]
        return lax.ppermute(x, ("seq", "sp"), pairs)

    low_halo, high_halo = pair > 0, pair < n_pairs - 1
    near_halo = jnp.where(odd == 1, low_halo, high_halo)
    far_halo = jnp.where(odd == 1, high_halo, low_halo)
    base = (col == 1) | (col == 2)
    entries = (base, place * (part // HDIM), text_count[0], near_halo, far_halo)
    info = jnp.stack([jnp.asarray(x, jnp.int32) for x in entries])

    block = place.reshape(1)
    sent = pack(block, [keys, values], part, [*far_slots, *near_slots])
    sent = dict(zip([*far_slots, *near_slots], sent))
    far = {k: send(sent[k], k) for k in far_slots}
    near = {k: send(sent[k], k) if k else sent[k] for k in near_slots}
    q_sent = pack(block, [queries], part, range(1, span))
    q_sent = dict(zip(range(1, span), q_sent))
    near[1], *_ = lax.optimization_barrier((near[1], *q_sent.values()))

    own = join([near[k] for k in near_slots])
    q = {k: send(after(q_sent[k], own), k) for k in (4, 5, 1, 2, 3)}
    own_halo = to_halo(own, 1)
    far[7] = after(far[7], q[4], q[5])
    other = join([far[k] for k in far_slots])
    q.update({k: send(after(q_sent[k], other), k) for k in (6, 7)})
    other_halo = to_halo(other, 0)
    texts = (text_keys, text_values)
    o = {}
    x4, x5 = attend(info, 3, [0], [q[4], q[5]], *texts, own, other, own_halo)
    o[4], o[5] = send(x4, 4), send(x5, 5)
    x7, x6 = attend(info, 3, [3], [q[7], q[6]], *texts, own, other, own_halo)
    o[7], o[6] = send(x7, 7), send(x6, 6)
    pieces = [queries, q[1], after(q[3], x7), q[2]]
    o[0], x1, x3, x2 = attend(info, 4, [0, 3], pieces, *texts, own, other, other_halo)
    o[3], o[2], o[1] = send(x3, 3), send(x2, 2), send(x1, 1)
    out = spread(block, {k: o[k] for k in far_slots}, queries.shape[2])
    return spread(block, {k: o[k] for k in near_slots}, queries.shape[2], into=out)


def solution(mesh):
    in_specs = (
        P(("grp", "sp", "seq"), "rep", None),
        P(("grp", "sp", "seq"), "rep", None),
        P(("grp", "sp", "seq"), "rep", None),
        P("grp", None),
        P("grp", None),
        P("grp"),
    )
    out_specs = P(("grp", "sp", "seq"), "rep", None)
    return jax.shard_map(body, mesh=mesh, in_specs=in_specs, out_specs=out_specs, check_vma=False)
```

```python
import functools
import math

import jax
import jax.numpy as jnp
from jax import lax
from jax.experimental import pallas as pl
from jax.experimental.pallas import tpu as pltpu
from jax.sharding import PartitionSpec as P

HDIM = 128
COLS = 4

masked_score = -1e30
exp2_scale = math.log2(math.e) / math.sqrt(HDIM)
vmem_limit = 20 * 2**20


def pack_kernel(width, slots, at, *refs):
    sources, outs = refs[: -len(slots)], refs[-len(slots) :]
    for (k, chosen), out in zip(slots, outs):
        head = pl.multiple_of((at[0] ^ k) * width, width)
        for j, i in enumerate(chosen):
            out[j] = sources[i][0, :, pl.ds(head, width)]


def pack(place, sources, width, slots):
    shapes = [(len(chosen), sources[chosen[0]].shape[1], width) for _, chosen in slots]
    return pl.pallas_call(
        functools.partial(pack_kernel, width, slots),
        in_specs=[pl.BlockSpec(memory_space=pltpu.SMEM)]
        + [pl.BlockSpec(memory_space=pltpu.VMEM)] * len(sources),
        out_shape=[jax.ShapeDtypeStruct(shape, jnp.bfloat16) for shape in shapes],
        cost_estimate=pl.CostEstimate(
            flops=0, bytes_accessed=4 * sum(map(math.prod, shapes)), transcendentals=0
        ),
        compiler_params=pltpu.CompilerParams(vmem_limit_bytes=vmem_limit),
    )(place, *sources)


def join_kernel(*refs):
    for j, ref in enumerate(refs[:-1]):
        refs[-1][j] = ref[...]


def join(tiles):
    shape = (len(tiles), *tiles[0].shape)
    return pl.pallas_call(
        join_kernel,
        out_shape=jax.ShapeDtypeStruct(shape, jnp.bfloat16),
        cost_estimate=pl.CostEstimate(
            flops=0, bytes_accessed=4 * math.prod(shape), transcendentals=0
        ),
        compiler_params=pltpu.CompilerParams(vmem_limit_bytes=vmem_limit),
    )(*tiles)


def attend_kernel(flag, turns, info, *refs):
    n = 2 * len(turns)
    queries, (text_k, text_v, own, other, halo) = refs[:n], refs[n : n + 5]
    outs, (keys, vals) = refs[n + 5 : 2 * n + 5], refs[2 * n + 5 :]
    length, width = own.shape[2:]
    rows = queries[0].shape[1]
    text_len = text_k.shape[0]
    base = info[0]
    lanes = pl.ds(pl.multiple_of(info[1] * HDIM, HDIM), width)
    text_live = lax.broadcasted_iota(jnp.int32, (1, text_len), 1) < info[2]

    def run(turn, q_refs, out_refs, with_halo):
        pieces = [(own, 0), (own, 1), (other, 0), (other, 1), None]
        pieces += [(halo, 0), (halo, 1)] if with_halo else []
        cut = len(pieces)
        pieces += [(own, 2), (other, 2)] + ([(halo, 2)] if with_halo else [])
        ends = [0]
        for piece in pieces:
            at = slice(ends[-1], ends[-1] + (text_len if piece is None else length))
            for side, text, dst in ((0, text_k, keys), (1, text_v, vals)):
                if piece is None:
                    dst[at] = text[:, lanes]
                else:
                    dst[at] = piece[0][base ^ (piece[1] ^ turn), side]
            ends.append(at.stop)
        main, inner = ends[cut], slice(ends[cut], ends[-1])
        first, second = [
            ref[0] if ref.shape[2] == width else ref[0, :, lanes] for ref in q_refs
        ]
        q_outer = jnp.where(base == 0, first, second)
        q_inner = jnp.where(base == 0, second, first)
        q_both = jnp.concatenate([q_outer, q_inner], axis=0)

        def scores_of(q, span, head):
            return lax.dot_general(
                q[:, head],
                keys[span, head],
                (((1,), (1,)), ((), ())),
                preferred_element_type=jnp.float32,
            )

        for j in range(width // HDIM):
            head = slice(j * HDIM, (j + 1) * HDIM)
            s_main = scores_of(q_both, slice(0, main), head)
            s_inner = scores_of(q_inner, inner, head)
            parts = [
                s_main[:, : ends[4]],
                jnp.where(text_live, s_main[:, ends[4] : ends[5]], masked_score),
            ]
            if with_halo:
                parts.append(s_main[:, ends[5] :])
            tops = [jnp.max(s, axis=-1, keepdims=True) for s in parts]
            top = functools.reduce(jnp.maximum, tops)
            top_inner = jnp.maximum(top[rows:], jnp.max(s_inner, axis=-1, keepdims=True))
            top = jnp.concatenate([top[:rows], top_inner], axis=0) * exp2_scale
            total, summed, at = 0.0, 0.0, 0
            for s in parts:
                w = jnp.exp2(s * exp2_scale - top)
                total = total + jnp.sum(w, axis=-1, keepdims=True)
                summed = summed + jnp.dot(
                    w.astype(jnp.bfloat16),
                    vals[at : at + s.shape[1], head],
                    preferred_element_type=jnp.float32,
                )
                at += s.shape[1]
            w = jnp.exp2(s_inner * exp2_scale - top[rows:])
            total_inner = total[rows:] + jnp.sum(w, axis=-1, keepdims=True)
            summed_inner = summed[rows:] + jnp.dot(
                w.astype(jnp.bfloat16), vals[inner, head], preferred_element_type=jnp.float32
            )
            o_outer = (summed[:rows] / total[:rows]).astype(jnp.bfloat16)
            o_inner = (summed_inner / total_inner).astype(jnp.bfloat16)
            out_refs[0][0, :, head] = jnp.where(base == 0, o_outer, o_inner)
            out_refs[1][0, :, head] = jnp.where(base == 0, o_inner, o_outer)

    for with_halo in (True, False):

        @pl.when(info[flag] == int(with_halo))
        def _():
            for t, turn in enumerate(turns):
                pair = slice(2 * t, 2 * t + 2)
                run(turn, queries[pair], outs[pair], with_halo)


def attend(info, flag, turns, queries, text_k, text_v, own, other, halo):
    rows = queries[-1].shape[1]
    length, width = own.shape[2:]
    total_keys = 9 * length + text_k.shape[0]
    pairs = len(queries) * width // HDIM * rows * total_keys
    return pl.pallas_call(
        functools.partial(attend_kernel, flag, turns),
        in_specs=[pl.BlockSpec(memory_space=pltpu.SMEM)]
        + [pl.BlockSpec(memory_space=pltpu.VMEM)] * (len(queries) + 5),
        scratch_shapes=[pltpu.VMEM((total_keys, width), jnp.bfloat16)] * 2,
        out_shape=[jax.ShapeDtypeStruct((1, rows, width), jnp.bfloat16)] * len(queries),
        cost_estimate=pl.CostEstimate(
            flops=4 * pairs * HDIM,
            bytes_accessed=width * 4 * (total_keys + rows * len(queries)),
            transcendentals=pairs,
        ),
        compiler_params=pltpu.CompilerParams(vmem_limit_bytes=vmem_limit),
    )(info, *queries, text_k, text_v, own, other, halo)


def spread_kernel(slots, place, *refs):
    out, sems = refs[-2:]
    width = refs[0].shape[2]
    copies = []
    for i, (k, ref) in enumerate(zip(slots, refs)):
        at = pl.multiple_of((place[0] ^ k) * width, width)
        copies.append(pltpu.make_async_copy(ref, out.at[:, :, pl.ds(at, width)], sems.at[i]))
    for copy in copies:
        copy.start()
    for copy in copies:
        copy.wait()


def spread(place, pieces, out_width, into=None):
    slots = sorted(pieces)
    shape = (*pieces[slots[0]].shape[:2], out_width)
    extra = [] if into is None else [into]
    return pl.pallas_call(
        functools.partial(spread_kernel, slots),
        in_specs=[pl.BlockSpec(memory_space=pltpu.SMEM)]
        + [pl.BlockSpec(memory_space=pltpu.VMEM)] * len(slots)
        + [pl.BlockSpec(memory_space=pl.ANY)] * len(extra),
        out_specs=pl.BlockSpec(memory_space=pl.ANY),
        out_shape=jax.ShapeDtypeStruct(shape, jnp.bfloat16),
        input_output_aliases={1 + len(slots): 0} if extra else {},
        scratch_shapes=[pltpu.SemaphoreType.DMA((len(slots),))],
        cost_estimate=pl.CostEstimate(
            flops=0, bytes_accessed=4 * math.prod(shape), transcendentals=0
        ),
        compiler_params=pltpu.CompilerParams(vmem_limit_bytes=vmem_limit),
    )(place, *[pieces[k] for k in slots], *extra)


def after(x, *others):
    return lax.optimization_barrier((x, *others))[0]


def body(queries, keys, values, text_keys, text_values, text_count):
    n_seq, n_sp = lax.axis_size("seq"), lax.axis_size("sp")
    tile = lax.axis_index("sp") * n_seq + lax.axis_index("seq")
    n_tiles, span = n_sp * n_seq, 2 * COLS
    col, odd, place, pair = tile % COLS, tile // COLS % 2, tile % span, tile // span
    n_pairs = n_tiles // span
    if lax.axis_size("rep") > 1:
        keys = lax.all_gather(keys, "rep", axis=1, tiled=True)
        values = lax.all_gather(values, "rep", axis=1, tiled=True)
    part = queries.shape[2] // span
    near_slots, far_slots = range(COLS), range(COLS, span)

    def send(x, k):
        return lax.ppermute(x, "seq", [(i, i ^ k) for i in range(n_seq)])

    def to_halo(x, down):
        pairs = [(i, i + span if i // COLS % 2 == down else i - span) for i in range(n_tiles)]
        flat = lambda i: i % n_seq * n_sp + i // n_seq
        pairs = [(flat(i), flat(j)) for i, j in pairs if 0 <= j < n_tiles]
        return lax.ppermute(x, ("seq", "sp"), pairs)

    low_halo, high_halo = pair > 0, pair < n_pairs - 1
    near_halo = jnp.where(odd == 1, low_halo, high_halo)
    far_halo = jnp.where(odd == 1, high_halo, low_halo)
    base = (col == 1) | (col == 2)
    entries = (base, place * (part // HDIM), text_count[0], near_halo, far_halo)
    info = jnp.stack([jnp.asarray(x, jnp.int32) for x in entries])

    block = place.reshape(1)
    sent = pack(block, [keys, values], part, [(k, (0, 1)) for k in range(span)])
    q_sent = pack(block, [queries], part, [(k, (0,)) for k in range(1, span)])
    q_sent = dict(zip(range(1, span), q_sent))
    far = {k: send(sent[k], k) for k in (4, 5)}
    near = {k: send(sent[k], k) if k else sent[k] for k in near_slots}
    near[1], *_ = lax.optimization_barrier((near[1], *q_sent.values()))
    near[3] = after(near[3], far[4])
    own = join([near[k] for k in near_slots])

    own_halo = to_halo(after(own, far[5]), 1)
    far[6] = send(after(sent[6], own), 6)
    q = {4: send(after(q_sent[4], far[4]), 4)}
    far[7] = send(after(sent[7], far[5], q[4]), 7)
    halos = {k: to_halo(far[k], 0) for k in (4, 5)}
    q[5] = send(after(q_sent[5], far[6]), 5)
    halos[6] = to_halo(far[6], 0)
    q.update({k: send(after(q_sent[k], far[5]), k) for k in (1, 2, 3)})
    q.update({k: send(after(q_sent[k], far[7]), k) for k in (6, 7)})
    far[7] = after(far[7], q[5], q[1], q[2], q[3])
    halos[7] = to_halo(far[7], 0)
    other = join([far[k] for k in far_slots])
    texts = (text_keys, text_values)
    o = {}
    x4, x5 = attend(info, 3, [0], [q[4], q[5]], *texts, own, other, own_halo)
    o[4], o[5] = send(x4, 4), send(x5, 5)
    x7, x6 = attend(info, 3, [3], [after(q[7], x4), q[6]], *texts, own, other, own_halo)
    o[7], o[6] = send(x7, 7), send(x6, 6)
    halos[7] = after(halos[7], x7)
    other_halo = join([halos[k] for k in far_slots])
    pieces = [queries, q[1], after(q[3], x7), q[2]]
    o[0], x1, x3, x2 = attend(info, 4, [0, 3], pieces, *texts, own, other, other_halo)
    for k, x in ((3, x3), (2, x2), (1, x1)):
        o[k] = send(after(x, o[4], o[5]), k)
    out = spread(block, {k: o[k] for k in far_slots}, queries.shape[2])
    return spread(block, {k: o[k] for k in near_slots}, queries.shape[2], into=out)


def solution(mesh):
    in_specs = (
        P(("grp", "sp", "seq"), "rep", None),
        P(("grp", "sp", "seq"), "rep", None),
        P(("grp", "sp", "seq"), "rep", None),
        P("grp", None),
        P("grp", None),
        P("grp"),
    )
    out_specs = P(("grp", "sp", "seq"), "rep", None)
    return jax.shard_map(body, mesh=mesh, in_specs=in_specs, out_specs=out_specs, check_vma=False)
```

```python
import functools
import math

import jax
import jax.numpy as jnp
from jax import lax
from jax.experimental import pallas as pl
from jax.experimental.pallas import tpu as pltpu
from jax.sharding import PartitionSpec as P

HDIM = 128
COLS = 4

masked_score = -1e30
exp2_scale = math.log2(math.e) / math.sqrt(HDIM)
vmem_limit = 12 * 2**20


def pack_kernel(slots, at, *refs):
    n = len(refs) - len(slots) - 1
    sources, outs, sems = refs[:n], refs[n:-1], refs[-1]
    copies = []
    for (k, chosen), out in zip(slots, outs):
        width = out.shape[2]
        head = pl.multiple_of((at[0] ^ k) * width, width)
        for j, i in enumerate(chosen):
            source = sources[i].at[0, :, pl.ds(head, width)]
            copies.append(pltpu.make_async_copy(source, out.at[j], sems.at[len(copies)]))
    for copy in copies:
        copy.start()
    for copy in copies:
        copy.wait()


def pack(place, sources, width, slots):
    shapes = [(len(chosen), sources[chosen[0]].shape[1], width) for _, chosen in slots]
    return pl.pallas_call(
        functools.partial(pack_kernel, slots),
        in_specs=[pl.BlockSpec(memory_space=pltpu.SMEM)]
        + [pl.BlockSpec(memory_space=pltpu.HBM)] * len(sources),
        out_specs=[pl.BlockSpec(memory_space=pltpu.VMEM)] * len(slots),
        out_shape=[jax.ShapeDtypeStruct(shape, jnp.bfloat16) for shape in shapes],
        scratch_shapes=[pltpu.SemaphoreType.DMA((sum(shape[0] for shape in shapes),))],
        cost_estimate=pl.CostEstimate(
            flops=0, bytes_accessed=4 * sum(map(math.prod, shapes)), transcendentals=0
        ),
        compiler_params=pltpu.CompilerParams(vmem_limit_bytes=vmem_limit),
    )(place, *sources)


def join_kernel(tiles, *refs):
    at = 0
    for ref in refs[:-1]:
        if tiles:
            refs[-1][at] = ref[:2]
            at += 1
        else:
            refs[-1][at : at + ref.shape[0]] = ref[...]
            at += ref.shape[0]


def join(parts):
    tiles = parts[0].ndim == 3
    count = len(parts) if tiles else sum(part.shape[0] for part in parts)
    shape = (count, 2, *parts[0].shape[-2:])
    return pl.pallas_call(
        functools.partial(join_kernel, tiles),
        out_shape=jax.ShapeDtypeStruct(shape, jnp.bfloat16),
        cost_estimate=pl.CostEstimate(
            flops=0, bytes_accessed=4 * math.prod(shape), transcendentals=0
        ),
        compiler_params=pltpu.CompilerParams(vmem_limit_bytes=vmem_limit),
    )(*parts)


def attend_kernel(flag, turns, info, *refs):
    n = 2 * len(turns)
    queries, (text, own, other, halo) = refs[:n], refs[n : n + 4]
    outs, (keys, vals) = refs[n + 4 : 2 * n + 4], refs[2 * n + 4 :]
    length, width = own.shape[2:]
    rows = queries[0].shape[1]
    text_len = text.shape[1]
    base = info[0]
    text_live = lax.broadcasted_iota(jnp.int32, (1, text_len), 1) < info[1]

    def run(turn, q_refs, out_refs, with_halo):
        pieces = [(own, 0), (own, 1), (other, 0), (other, 1), None]
        pieces += [(halo, 0), (halo, 1)] if with_halo else []
        cut = len(pieces)
        pieces += [(own, 2), (other, 2)] + ([(halo, 2)] if with_halo else [])
        ends = [0]
        for piece in pieces:
            at = slice(ends[-1], ends[-1] + (text_len if piece is None else length))
            for side, dst in enumerate((keys, vals)):
                if piece is None:
                    dst[at] = text[side]
                else:
                    dst[at] = piece[0][base ^ (piece[1] ^ turn), side]
            ends.append(at.stop)
        main, inner = ends[cut], slice(ends[cut], ends[-1])
        first, second = [ref[ref.shape[0] - 1] for ref in q_refs]
        q_outer = jnp.where(base == 0, first, second)
        q_inner = jnp.where(base == 0, second, first)
        q_both = jnp.concatenate([q_outer, q_inner], axis=0)

        def scores_of(q, span, head):
            return lax.dot_general(
                q[:, head],
                keys[span, head],
                (((1,), (1,)), ((), ())),
                preferred_element_type=jnp.float32,
            )

        for j in range(width // HDIM):
            head = slice(j * HDIM, (j + 1) * HDIM)
            s_main = scores_of(q_both, slice(0, main), head)
            s_inner = scores_of(q_inner, inner, head)
            parts = [
                s_main[:, : ends[4]],
                jnp.where(text_live, s_main[:, ends[4] : ends[5]], masked_score),
            ]
            if with_halo:
                parts.append(s_main[:, ends[5] :])
            tops = [jnp.max(s, axis=-1, keepdims=True) for s in parts]
            top = functools.reduce(jnp.maximum, tops)
            top_inner = jnp.maximum(top[rows:], jnp.max(s_inner, axis=-1, keepdims=True))
            top = jnp.concatenate([top[:rows], top_inner], axis=0) * exp2_scale
            total, summed, at = 0.0, 0.0, 0
            for s in parts:
                w = jnp.exp2(s * exp2_scale - top)
                total = total + jnp.sum(w, axis=-1, keepdims=True)
                summed = summed + jnp.dot(
                    w.astype(jnp.bfloat16),
                    vals[at : at + s.shape[1], head],
                    preferred_element_type=jnp.float32,
                )
                at += s.shape[1]
            w = jnp.exp2(s_inner * exp2_scale - top[rows:])
            total_inner = total[rows:] + jnp.sum(w, axis=-1, keepdims=True)
            summed_inner = summed[rows:] + jnp.dot(
                w.astype(jnp.bfloat16), vals[inner, head], preferred_element_type=jnp.float32
            )
            o_outer = (summed[:rows] / total[:rows]).astype(jnp.bfloat16)
            o_inner = (summed_inner / total_inner).astype(jnp.bfloat16)
            out_refs[0][0, :, head] = jnp.where(base == 0, o_outer, o_inner)
            out_refs[1][0, :, head] = jnp.where(base == 0, o_inner, o_outer)

    for with_halo in (True, False):

        @pl.when(info[flag] == int(with_halo))
        def _():
            for t, turn in enumerate(turns):
                pair = slice(2 * t, 2 * t + 2)
                run(turn, queries[pair], outs[pair], with_halo)


def attend(info, flag, turns, queries, text, own, other, halo):
    rows = queries[-1].shape[1]
    length, width = own.shape[2:]
    total_keys = 9 * length + text.shape[1]
    pairs = len(queries) * width // HDIM * rows * total_keys
    return pl.pallas_call(
        functools.partial(attend_kernel, flag, turns),
        in_specs=[pl.BlockSpec(memory_space=pltpu.SMEM)]
        + [pl.BlockSpec(memory_space=pltpu.VMEM)] * (len(queries) + 4),
        scratch_shapes=[pltpu.VMEM((total_keys, width), jnp.bfloat16)] * 2,
        out_shape=[jax.ShapeDtypeStruct((1, rows, width), jnp.bfloat16)] * len(queries),
        cost_estimate=pl.CostEstimate(
            flops=4 * pairs * HDIM,
            bytes_accessed=width * 4 * (total_keys + rows * len(queries)),
            transcendentals=pairs,
        ),
        compiler_params=pltpu.CompilerParams(vmem_limit_bytes=vmem_limit),
    )(info, *queries, text, own, other, halo)


def spread_kernel(slots, place, *refs):
    out, sems = refs[-2:]
    width = refs[0].shape[2]
    copies = []
    for i, (k, ref) in enumerate(zip(slots, refs)):
        at = pl.multiple_of((place[0] ^ k) * width, width)
        copies.append(pltpu.make_async_copy(ref, out.at[:, :, pl.ds(at, width)], sems.at[i]))
    for copy in copies:
        copy.start()
    for copy in copies:
        copy.wait()


def spread(place, pieces, out_width, into=None):
    slots = sorted(pieces)
    shape = (*pieces[slots[0]].shape[:2], out_width)
    extra = [] if into is None else [into]
    return pl.pallas_call(
        functools.partial(spread_kernel, slots),
        in_specs=[pl.BlockSpec(memory_space=pltpu.SMEM)]
        + [pl.BlockSpec(memory_space=pltpu.VMEM)] * len(slots)
        + [pl.BlockSpec(memory_space=pl.ANY)] * len(extra),
        out_specs=pl.BlockSpec(memory_space=pl.ANY),
        out_shape=jax.ShapeDtypeStruct(shape, jnp.bfloat16),
        input_output_aliases={1 + len(slots): 0} if extra else {},
        scratch_shapes=[pltpu.SemaphoreType.DMA((len(slots),))],
        cost_estimate=pl.CostEstimate(
            flops=0, bytes_accessed=4 * math.prod(shape), transcendentals=0
        ),
        compiler_params=pltpu.CompilerParams(vmem_limit_bytes=vmem_limit),
    )(place, *[pieces[k] for k in slots], *extra)


def after(x, *others):
    return lax.optimization_barrier((x, *others))[0]


def body(queries, keys, values, text_keys, text_values, text_count):
    n_seq, n_sp = lax.axis_size("seq"), lax.axis_size("sp")
    tile = lax.axis_index("sp") * n_seq + lax.axis_index("seq")
    n_tiles, span = n_sp * n_seq, 2 * COLS
    col, odd, place, pair = tile % COLS, tile // COLS % 2, tile % span, tile // span
    n_pairs = n_tiles // span
    if lax.axis_size("rep") > 1:
        keys = lax.all_gather(keys, "rep", axis=1, tiled=True)
        values = lax.all_gather(values, "rep", axis=1, tiled=True)
    part = queries.shape[2] // span
    near_slots, far_slots = range(COLS), range(COLS, span)

    def send(x, k):
        return lax.ppermute(x, "seq", [(i, i ^ k) for i in range(n_seq)])

    def to_halo(x, down):
        pairs = [(i, i + span if i // COLS % 2 == down else i - span) for i in range(n_tiles)]
        flat = lambda i: i % n_seq * n_sp + i // n_seq
        pairs = [(flat(i), flat(j)) for i, j in pairs if 0 <= j < n_tiles]
        return lax.ppermute(x, ("seq", "sp"), pairs)

    low_halo, high_halo = pair > 0, pair < n_pairs - 1
    near_halo = jnp.where(odd == 1, low_halo, high_halo)
    far_halo = jnp.where(odd == 1, high_halo, low_halo)
    base = (col == 1) | (col == 2)
    entries = (base, text_count[0], near_halo, far_halo)
    info = jnp.stack([jnp.asarray(x, jnp.int32) for x in entries])

    block = place.reshape(1)
    sources = [keys, values, queries]
    kinds = [(0, 1, 2)] if queries.shape == keys.shape else [(0, 1), (2,)]

    def cut(inputs, slots, extra=()):
        wanted = [(k, kind) for k in slots for kind in kinds]
        parts = pack(block, inputs, part, [*wanted, *extra])
        pieces = iter(parts)
        return {k: [next(pieces) for _ in kinds] for k in slots}, parts[len(wanted) :]

    def post(x, k, *others):
        return [send(after(piece, *others), k) for piece in x]

    sent, _ = cut(sources, (4, 5, 6))
    first = [piece for k in sent for piece in sent[k]]
    texts = [text_keys[None], text_values[None]]
    inputs = [*(after(x, *first) for x in sources), *texts]
    more, (text,) = cut(inputs, (0, 1, 2, 3, 7), [(0, (3, 4))])
    sent.update(more)
    got = {k: post(sent[k], k) for k in (4, 5)}
    got[0] = sent[0]
    got.update({k: post(sent[k], k) for k in (1, 2, 3)})
    got[6] = post(sent[6], 6, got[1][0])
    got[7] = post(sent[7], 7, *(got[k][0] for k in (4, 5, 6)))
    kv = {k: got[k][0] for k in got}
    q = {k: got[k][-1] for k in got}
    own = join([kv[k] for k in near_slots])
    own_halo = to_halo(own, 1)
    first_halo = to_halo(join([kv[4], kv[5]]), 0)
    kv[7] = after(kv[7], first_halo)
    last_halo = to_halo(join([kv[6], kv[7]]), 0)
    other = join([kv[k] for k in far_slots])
    o = {}
    x4, x5 = attend(info, 2, [0], [q[4], q[5]], text, own, other, own_halo)
    o[4], o[5] = send(x4, 4), send(x5, 5)
    x7, x6 = attend(info, 2, [3], [after(q[7], x4), q[6]], text, own, other, own_halo)
    o[7], o[6] = send(x7, 7), send(x6, 6)
    other_halo = join([first_halo, after(last_halo, x7)])
    pieces = [q[0], q[1], q[3], q[2]]
    o[0], x1, x3, x2 = attend(info, 3, [0, 3], pieces, text, own, other, other_halo)
    for k, x in ((3, x3), (2, x2), (1, x1)):
        o[k] = send(after(x, o[4], o[5]), k)
    out = spread(block, {k: o[k] for k in far_slots}, queries.shape[2])
    return spread(block, {k: o[k] for k in near_slots}, queries.shape[2], into=out)


def solution(mesh):
    in_specs = (
        P(("grp", "sp", "seq"), "rep", None),
        P(("grp", "sp", "seq"), "rep", None),
        P(("grp", "sp", "seq"), "rep", None),
        P("grp", None),
        P("grp", None),
        P("grp"),
    )
    out_specs = P(("grp", "sp", "seq"), "rep", None)
    return jax.shard_map(body, mesh=mesh, in_specs=in_specs, out_specs=out_specs, check_vma=False)
```

```python
import functools
import math

import jax
import jax.numpy as jnp
from jax import lax
from jax.experimental import pallas as pl
from jax.experimental.pallas import tpu as pltpu
from jax.sharding import PartitionSpec as P

HDIM = 128
COLS = 4

masked_score = -1e30
exp2_scale = math.log2(math.e) / math.sqrt(HDIM)
vmem_limit = 12 * 2**20


def pack_kernel(slots, at, *refs):
    n = len(refs) - len(slots) - 1
    sources, outs, sems = refs[:n], refs[n:-1], refs[-1]
    copies = []
    for (k, chosen), out in zip(slots, outs):
        width = out.shape[2]
        head = pl.multiple_of((at[0] ^ k) * width, width)
        for j, i in enumerate(chosen):
            source = sources[i].at[0, :, pl.ds(head, width)]
            copies.append(pltpu.make_async_copy(source, out.at[j], sems.at[len(copies)]))
    for copy in copies:
        copy.start()
    for copy in copies:
        copy.wait()


def pack(place, sources, width, slots):
    shapes = [(len(chosen), sources[chosen[0]].shape[1], width) for _, chosen in slots]
    return pl.pallas_call(
        functools.partial(pack_kernel, slots),
        in_specs=[pl.BlockSpec(memory_space=pltpu.SMEM)]
        + [pl.BlockSpec(memory_space=pltpu.HBM)] * len(sources),
        out_specs=[pl.BlockSpec(memory_space=pltpu.VMEM)] * len(slots),
        out_shape=[jax.ShapeDtypeStruct(shape, jnp.bfloat16) for shape in shapes],
        scratch_shapes=[pltpu.SemaphoreType.DMA((sum(shape[0] for shape in shapes),))],
        cost_estimate=pl.CostEstimate(
            flops=0, bytes_accessed=4 * sum(map(math.prod, shapes)), transcendentals=0
        ),
        compiler_params=pltpu.CompilerParams(vmem_limit_bytes=vmem_limit),
    )(place, *sources)


def join_kernel(tiles, *refs):
    at = 0
    for ref in refs[:-1]:
        if tiles:
            refs[-1][at] = ref[:2]
            at += 1
        else:
            refs[-1][at : at + ref.shape[0]] = ref[...]
            at += ref.shape[0]


def join(parts):
    tiles = parts[0].ndim == 3
    count = len(parts) if tiles else sum(part.shape[0] for part in parts)
    shape = (count, 2, *parts[0].shape[-2:])
    return pl.pallas_call(
        functools.partial(join_kernel, tiles),
        out_shape=jax.ShapeDtypeStruct(shape, jnp.bfloat16),
        cost_estimate=pl.CostEstimate(
            flops=0, bytes_accessed=4 * math.prod(shape), transcendentals=0
        ),
        compiler_params=pltpu.CompilerParams(vmem_limit_bytes=vmem_limit),
    )(*parts)


def attend_kernel(flag, turns, info, *refs):
    n = 2 * len(turns)
    queries, (text, own, other, halo) = refs[:n], refs[n : n + 4]
    outs, (keys, vals) = refs[n + 4 : 2 * n + 4], refs[2 * n + 4 :]
    length, width = own.shape[2:]
    rows = queries[0].shape[1]
    text_len = text.shape[1]
    base = info[0]
    text_live = lax.broadcasted_iota(jnp.int32, (1, text_len), 1) < info[1]

    def run(turn, q_refs, out_refs, with_halo):
        pieces = [(own, 0), (own, 1), (other, 0), (other, 1), None]
        pieces += [(halo, 0), (halo, 1)] if with_halo else []
        cut = len(pieces)
        pieces += [(own, 2), (other, 2)] + ([(halo, 2)] if with_halo else [])
        ends = [0]
        for piece in pieces:
            at = slice(ends[-1], ends[-1] + (text_len if piece is None else length))
            for side, dst in enumerate((keys, vals)):
                if piece is None:
                    dst[at] = text[side]
                else:
                    dst[at] = piece[0][base ^ (piece[1] ^ turn), side]
            ends.append(at.stop)
        main, inner = ends[cut], slice(ends[cut], ends[-1])
        first, second = [ref[ref.shape[0] - 1] for ref in q_refs]
        q_outer = jnp.where(base == 0, first, second)
        q_inner = jnp.where(base == 0, second, first)
        q_both = jnp.concatenate([q_outer, q_inner], axis=0)

        def scores_of(q, span, head):
            return lax.dot_general(
                q[:, head],
                keys[span, head],
                (((1,), (1,)), ((), ())),
                preferred_element_type=jnp.float32,
            )

        for j in range(width // HDIM):
            head = slice(j * HDIM, (j + 1) * HDIM)
            s_main = scores_of(q_both, slice(0, main), head)
            s_inner = scores_of(q_inner, inner, head)
            parts = [
                s_main[:, : ends[4]],
                jnp.where(text_live, s_main[:, ends[4] : ends[5]], masked_score),
            ]
            if with_halo:
                parts.append(s_main[:, ends[5] :])
            tops = [jnp.max(s, axis=-1, keepdims=True) for s in parts]
            top = functools.reduce(jnp.maximum, tops)
            top_inner = jnp.maximum(top[rows:], jnp.max(s_inner, axis=-1, keepdims=True))
            top = jnp.concatenate([top[:rows], top_inner], axis=0) * exp2_scale
            total, summed, at = 0.0, 0.0, 0
            for s in parts:
                w = jnp.exp2(s * exp2_scale - top)
                total = total + jnp.sum(w, axis=-1, keepdims=True)
                summed = summed + jnp.dot(
                    w.astype(jnp.bfloat16),
                    vals[at : at + s.shape[1], head],
                    preferred_element_type=jnp.float32,
                )
                at += s.shape[1]
            w = jnp.exp2(s_inner * exp2_scale - top[rows:])
            total_inner = total[rows:] + jnp.sum(w, axis=-1, keepdims=True)
            summed_inner = summed[rows:] + jnp.dot(
                w.astype(jnp.bfloat16), vals[inner, head], preferred_element_type=jnp.float32
            )
            o_outer = (summed[:rows] / total[:rows]).astype(jnp.bfloat16)
            o_inner = (summed_inner / total_inner).astype(jnp.bfloat16)
            out_refs[0][0, :, head] = jnp.where(base == 0, o_outer, o_inner)
            out_refs[1][0, :, head] = jnp.where(base == 0, o_inner, o_outer)

    for with_halo in (True, False):

        @pl.when(info[flag] == int(with_halo))
        def _():
            for t, turn in enumerate(turns):
                pair = slice(2 * t, 2 * t + 2)
                run(turn, queries[pair], outs[pair], with_halo)


def attend(info, flag, turns, queries, text, own, other, halo):
    rows = queries[-1].shape[1]
    length, width = own.shape[2:]
    total_keys = 9 * length + text.shape[1]
    pairs = len(queries) * width // HDIM * rows * total_keys
    return pl.pallas_call(
        functools.partial(attend_kernel, flag, turns),
        in_specs=[pl.BlockSpec(memory_space=pltpu.SMEM)]
        + [pl.BlockSpec(memory_space=pltpu.VMEM)] * (len(queries) + 4),
        scratch_shapes=[pltpu.VMEM((total_keys, width), jnp.bfloat16)] * 2,
        out_shape=[jax.ShapeDtypeStruct((1, rows, width), jnp.bfloat16)] * len(queries),
        cost_estimate=pl.CostEstimate(
            flops=4 * pairs * HDIM,
            bytes_accessed=width * 4 * (total_keys + rows * len(queries)),
            transcendentals=pairs,
        ),
        compiler_params=pltpu.CompilerParams(vmem_limit_bytes=vmem_limit),
    )(info, *queries, text, own, other, halo)


def spread_kernel(slots, place, *refs):
    out, sems = refs[-2:]
    width = refs[0].shape[2]
    copies = []
    for i, (k, ref) in enumerate(zip(slots, refs)):
        at = pl.multiple_of((place[0] ^ k) * width, width)
        copies.append(pltpu.make_async_copy(ref, out.at[:, :, pl.ds(at, width)], sems.at[i]))
    for copy in copies:
        copy.start()
    for copy in copies:
        copy.wait()


def spread(place, pieces, out_width, into=None):
    slots = sorted(pieces)
    shape = (*pieces[slots[0]].shape[:2], out_width)
    extra = [] if into is None else [into]
    return pl.pallas_call(
        functools.partial(spread_kernel, slots),
        in_specs=[pl.BlockSpec(memory_space=pltpu.SMEM)]
        + [pl.BlockSpec(memory_space=pltpu.VMEM)] * len(slots)
        + [pl.BlockSpec(memory_space=pl.ANY)] * len(extra),
        out_specs=pl.BlockSpec(memory_space=pl.ANY),
        out_shape=jax.ShapeDtypeStruct(shape, jnp.bfloat16),
        input_output_aliases={1 + len(slots): 0} if extra else {},
        scratch_shapes=[pltpu.SemaphoreType.DMA((len(slots),))],
        cost_estimate=pl.CostEstimate(
            flops=0, bytes_accessed=4 * math.prod(shape), transcendentals=0
        ),
        compiler_params=pltpu.CompilerParams(vmem_limit_bytes=vmem_limit),
    )(place, *[pieces[k] for k in slots], *extra)


def after(x, *others):
    return lax.optimization_barrier((x, *others))[0]


def body(queries, keys, values, text_keys, text_values, text_count):
    n_seq, n_sp = lax.axis_size("seq"), lax.axis_size("sp")
    tile = lax.axis_index("sp") * n_seq + lax.axis_index("seq")
    n_tiles, span = n_sp * n_seq, 2 * COLS
    col, odd, place, pair = tile % COLS, tile // COLS % 2, tile % span, tile // span
    n_pairs = n_tiles // span
    if lax.axis_size("rep") > 1:
        keys = lax.all_gather(keys, "rep", axis=1, tiled=True)
        values = lax.all_gather(values, "rep", axis=1, tiled=True)
    part = queries.shape[2] // span
    near_slots, far_slots = range(COLS), range(COLS, span)

    def send(x, k):
        return lax.ppermute(x, "seq", [(i, i ^ k) for i in range(n_seq)])

    def to_halo(x, down):
        pairs = [(i, i + span if i // COLS % 2 == down else i - span) for i in range(n_tiles)]
        flat = lambda i: i % n_seq * n_sp + i // n_seq
        pairs = [(flat(i), flat(j)) for i, j in pairs if 0 <= j < n_tiles]
        return lax.ppermute(x, ("seq", "sp"), pairs)

    low_halo, high_halo = pair > 0, pair < n_pairs - 1
    near_halo = jnp.where(odd == 1, low_halo, high_halo)
    far_halo = jnp.where(odd == 1, high_halo, low_halo)
    base = (col == 1) | (col == 2)
    entries = (base, text_count[0], near_halo, far_halo)
    info = jnp.stack([jnp.asarray(x, jnp.int32) for x in entries])

    block = place.reshape(1)
    sources = [keys, values, queries]
    kinds = [(0, 1, 2)] if queries.shape == keys.shape else [(0, 1), (2,)]

    sent = dict(zip(far_slots, pack(block, sources[:2], part, [(k, (0, 1)) for k in far_slots])))
    kv = {k: send(sent[k], k) for k in (4, 5)}
    inputs = [after(x, *sent.values()) for x in sources]
    wanted = [(k, kind) for k in near_slots for kind in kinds]
    near_sent = pack(block, inputs, part, wanted)
    near_sent = [near_sent[k * len(kinds) : (k + 1) * len(kinds)] for k in near_slots]
    near = [near_sent[0]] + [[send(x, k) for x in near_sent[k]] for k in (1, 2, 3)]
    inputs = [after(x, near[1][0]) for x in (queries, text_keys[None], text_values[None])]
    wanted = [(k, (0,)) for k in far_slots] + [(0, (1, 2))]
    q4, q5, q6, q7, text = pack(block, inputs, part, wanted)
    kv[6] = send(after(sent[6], near[1][0]), 6)
    kv[7] = send(after(sent[7], text, *(near[k][0] for k in (1, 2, 3))), 7)
    kv.update({k: near[k][0] for k in near_slots})
    q = {k: near[k][-1] for k in near_slots}
    own = join([kv[k] for k in near_slots])
    own_halo = to_halo(own, 1)
    other = join([kv[k] for k in far_slots])
    other_halo = to_halo(other, 0)
    q4, q5 = after(q4, other), after(q5, other)
    q[4], q[5] = send(q4, 4), send(q5, 5)
    q[6], q[7] = send(after(q6, q[4]), 6), send(after(q7, q[5]), 7)
    o = {}
    x4, x5 = attend(info, 2, [0], [q[4], q[5]], text, own, other, own_halo)
    o[4], o[5] = send(x4, 4), send(x5, 5)
    x7, x6 = attend(info, 2, [3], [after(q[7], x4), q[6]], text, own, other, own_halo)
    o[7], o[6] = send(x7, 7), send(x6, 6)
    pieces = [q[0], q[1], after(q[3], x7), q[2]]
    o[0], x1, x3, x2 = attend(info, 3, [0, 3], pieces, text, own, other, other_halo)
    o[3], o[2], o[1] = send(x3, 3), send(x2, 2), send(x1, 1)
    out = spread(block, {k: o[k] for k in far_slots}, queries.shape[2])
    return spread(block, {k: o[k] for k in near_slots}, queries.shape[2], into=out)


def solution(mesh):
    in_specs = (
        P(("grp", "sp", "seq"), "rep", None),
        P(("grp", "sp", "seq"), "rep", None),
        P(("grp", "sp", "seq"), "rep", None),
        P("grp", None),
        P("grp", None),
        P("grp"),
    )
    out_specs = P(("grp", "sp", "seq"), "rep", None)
    return jax.shard_map(body, mesh=mesh, in_specs=in_specs, out_specs=out_specs, check_vma=False)
```

```python
import functools
import math

import jax
import jax.numpy as jnp
from jax import lax
from jax.experimental import pallas as pl
from jax.experimental.pallas import tpu as pltpu
from jax.sharding import PartitionSpec as P

HDIM = 128
COLS = 4

masked_score = -1e30
exp2_scale = math.log2(math.e) / math.sqrt(HDIM)
vmem_limit = 12 * 2**20


def pack_kernel(slots, at, *refs):
    n = len(refs) - len(slots) - 1
    sources, outs, sems = refs[:n], refs[n:-1], refs[-1]
    copies = []
    for (k, chosen), out in zip(slots, outs):
        width = out.shape[2]
        head = pl.multiple_of((at[0] ^ k) * width, width)
        for j, i in enumerate(chosen):
            source = sources[i].at[0, :, pl.ds(head, width)]
            copies.append(pltpu.make_async_copy(source, out.at[j], sems.at[len(copies)]))
    for copy in copies:
        copy.start()
    for copy in copies:
        copy.wait()


def pack(place, sources, width, slots):
    shapes = [(len(chosen), sources[chosen[0]].shape[1], width) for _, chosen in slots]
    return pl.pallas_call(
        functools.partial(pack_kernel, slots),
        in_specs=[pl.BlockSpec(memory_space=pltpu.SMEM)]
        + [pl.BlockSpec(memory_space=pltpu.HBM)] * len(sources),
        out_specs=[pl.BlockSpec(memory_space=pltpu.VMEM)] * len(slots),
        out_shape=[jax.ShapeDtypeStruct(shape, jnp.bfloat16) for shape in shapes],
        scratch_shapes=[pltpu.SemaphoreType.DMA((sum(shape[0] for shape in shapes),))],
        cost_estimate=pl.CostEstimate(
            flops=0, bytes_accessed=4 * sum(map(math.prod, shapes)), transcendentals=0
        ),
        compiler_params=pltpu.CompilerParams(vmem_limit_bytes=vmem_limit),
    )(place, *sources)


def join_kernel(tiles, *refs):
    at = 0
    for ref in refs[:-1]:
        if tiles:
            refs[-1][at] = ref[:2]
            at += 1
        else:
            refs[-1][at : at + ref.shape[0]] = ref[...]
            at += ref.shape[0]


def join(parts):
    tiles = parts[0].ndim == 3
    count = len(parts) if tiles else sum(part.shape[0] for part in parts)
    shape = (count, 2, *parts[0].shape[-2:])
    return pl.pallas_call(
        functools.partial(join_kernel, tiles),
        out_shape=jax.ShapeDtypeStruct(shape, jnp.bfloat16),
        cost_estimate=pl.CostEstimate(
            flops=0, bytes_accessed=4 * math.prod(shape), transcendentals=0
        ),
        compiler_params=pltpu.CompilerParams(vmem_limit_bytes=vmem_limit),
    )(*parts)


def attend_kernel(flag, turns, info, *refs):
    n = 2 * len(turns)
    queries, (text, own, other, halo) = refs[:n], refs[n : n + 4]
    outs, (keys, vals) = refs[n + 4 : 2 * n + 4], refs[2 * n + 4 :]
    length, width = own.shape[2:]
    rows = queries[0].shape[1]
    text_len = text.shape[1]
    base = info[0]
    text_live = lax.broadcasted_iota(jnp.int32, (1, text_len), 1) < info[1]

    def run(turn, q_refs, out_refs, with_halo):
        pieces = [(own, 0), (own, 1), (other, 0), (other, 1), None]
        pieces += [(halo, 0), (halo, 1)] if with_halo else []
        cut = len(pieces)
        pieces += [(own, 2), (other, 2)] + ([(halo, 2)] if with_halo else [])
        ends = [0]
        for piece in pieces:
            at = slice(ends[-1], ends[-1] + (text_len if piece is None else length))
            for side, dst in enumerate((keys, vals)):
                if piece is None:
                    dst[at] = text[side]
                else:
                    dst[at] = piece[0][base ^ (piece[1] ^ turn), side]
            ends.append(at.stop)
        main, inner = ends[cut], slice(ends[cut], ends[-1])
        first, second = [ref[ref.shape[0] - 1] for ref in q_refs]
        q_outer = jnp.where(base == 0, first, second)
        q_inner = jnp.where(base == 0, second, first)
        q_both = jnp.concatenate([q_outer, q_inner], axis=0)

        def scores_of(q, span, head):
            return lax.dot_general(
                q[:, head],
                keys[span, head],
                (((1,), (1,)), ((), ())),
                preferred_element_type=jnp.float32,
            )

        for j in range(width // HDIM):
            head = slice(j * HDIM, (j + 1) * HDIM)
            s_main = scores_of(q_both, slice(0, main), head)
            s_inner = scores_of(q_inner, inner, head)
            parts = [
                s_main[:, : ends[4]],
                jnp.where(text_live, s_main[:, ends[4] : ends[5]], masked_score),
            ]
            if with_halo:
                parts.append(s_main[:, ends[5] :])
            tops = [jnp.max(s, axis=-1, keepdims=True) for s in parts]
            top = functools.reduce(jnp.maximum, tops)
            top_inner = jnp.maximum(top[rows:], jnp.max(s_inner, axis=-1, keepdims=True))
            top = jnp.concatenate([top[:rows], top_inner], axis=0) * exp2_scale
            total, summed, at = 0.0, 0.0, 0
            for s in parts:
                w = jnp.exp2(s * exp2_scale - top)
                total = total + jnp.sum(w, axis=-1, keepdims=True)
                summed = summed + jnp.dot(
                    w.astype(jnp.bfloat16),
                    vals[at : at + s.shape[1], head],
                    preferred_element_type=jnp.float32,
                )
                at += s.shape[1]
            w = jnp.exp2(s_inner * exp2_scale - top[rows:])
            total_inner = total[rows:] + jnp.sum(w, axis=-1, keepdims=True)
            summed_inner = summed[rows:] + jnp.dot(
                w.astype(jnp.bfloat16), vals[inner, head], preferred_element_type=jnp.float32
            )
            o_outer = (summed[:rows] / total[:rows]).astype(jnp.bfloat16)
            o_inner = (summed_inner / total_inner).astype(jnp.bfloat16)
            out_refs[0][0, :, head] = jnp.where(base == 0, o_outer, o_inner)
            out_refs[1][0, :, head] = jnp.where(base == 0, o_inner, o_outer)

    for with_halo in (True, False):

        @pl.when(info[flag] == int(with_halo))
        def _():
            for t, turn in enumerate(turns):
                pair = slice(2 * t, 2 * t + 2)
                run(turn, queries[pair], outs[pair], with_halo)


def attend(info, flag, turns, queries, text, own, other, halo):
    rows = queries[-1].shape[1]
    length, width = own.shape[2:]
    total_keys = 9 * length + text.shape[1]
    pairs = len(queries) * width // HDIM * rows * total_keys
    return pl.pallas_call(
        functools.partial(attend_kernel, flag, turns),
        in_specs=[pl.BlockSpec(memory_space=pltpu.SMEM)]
        + [pl.BlockSpec(memory_space=pltpu.VMEM)] * (len(queries) + 4),
        scratch_shapes=[pltpu.VMEM((total_keys, width), jnp.bfloat16)] * 2,
        out_shape=[jax.ShapeDtypeStruct((1, rows, width), jnp.bfloat16)] * len(queries),
        cost_estimate=pl.CostEstimate(
            flops=4 * pairs * HDIM,
            bytes_accessed=width * 4 * (total_keys + rows * len(queries)),
            transcendentals=pairs,
        ),
        compiler_params=pltpu.CompilerParams(vmem_limit_bytes=vmem_limit),
    )(info, *queries, text, own, other, halo)


def spread_kernel(slots, place, *refs):
    out, sems = refs[-2:]
    width = refs[0].shape[2]
    copies = []
    for i, (k, ref) in enumerate(zip(slots, refs)):
        at = pl.multiple_of((place[0] ^ k) * width, width)
        copies.append(pltpu.make_async_copy(ref, out.at[:, :, pl.ds(at, width)], sems.at[i]))
    for copy in copies:
        copy.start()
    for copy in copies:
        copy.wait()


def spread(place, pieces, out_width, into=None):
    slots = sorted(pieces)
    shape = (*pieces[slots[0]].shape[:2], out_width)
    extra = [] if into is None else [into]
    return pl.pallas_call(
        functools.partial(spread_kernel, slots),
        in_specs=[pl.BlockSpec(memory_space=pltpu.SMEM)]
        + [pl.BlockSpec(memory_space=pltpu.VMEM)] * len(slots)
        + [pl.BlockSpec(memory_space=pl.ANY)] * len(extra),
        out_specs=pl.BlockSpec(memory_space=pl.ANY),
        out_shape=jax.ShapeDtypeStruct(shape, jnp.bfloat16),
        input_output_aliases={1 + len(slots): 0} if extra else {},
        scratch_shapes=[pltpu.SemaphoreType.DMA((len(slots),))],
        cost_estimate=pl.CostEstimate(
            flops=0, bytes_accessed=4 * math.prod(shape), transcendentals=0
        ),
        compiler_params=pltpu.CompilerParams(vmem_limit_bytes=vmem_limit),
    )(place, *[pieces[k] for k in slots], *extra)


def after(x, *others):
    return lax.optimization_barrier((x, *others))[0]


def body(queries, keys, values, text_keys, text_values, text_count):
    n_seq, n_sp = lax.axis_size("seq"), lax.axis_size("sp")
    tile = lax.axis_index("sp") * n_seq + lax.axis_index("seq")
    n_tiles, span = n_sp * n_seq, 2 * COLS
    col, odd, place, pair = tile % COLS, tile // COLS % 2, tile % span, tile // span
    n_pairs = n_tiles // span
    if lax.axis_size("rep") > 1:
        keys = lax.all_gather(keys, "rep", axis=1, tiled=True)
        values = lax.all_gather(values, "rep", axis=1, tiled=True)
    part = queries.shape[2] // span
    near_slots, far_slots = range(COLS), range(COLS, span)

    def send(x, k):
        return lax.ppermute(x, "seq", [(i, i ^ k) for i in range(n_seq)])

    def to_halo(x, down):
        pairs = [(i, i + span if i // COLS % 2 == down else i - span) for i in range(n_tiles)]
        flat = lambda i: i % n_seq * n_sp + i // n_seq
        pairs = [(flat(i), flat(j)) for i, j in pairs if 0 <= j < n_tiles]
        return lax.ppermute(x, ("seq", "sp"), pairs)

    low_halo, high_halo = pair > 0, pair < n_pairs - 1
    near_halo = jnp.where(odd == 1, low_halo, high_halo)
    far_halo = jnp.where(odd == 1, high_halo, low_halo)
    base = (col == 1) | (col == 2)
    entries = (base, text_count[0], near_halo, far_halo)
    info = jnp.stack([jnp.asarray(x, jnp.int32) for x in entries])

    block = place.reshape(1)
    sources = [keys, values, queries]
    kinds = [(0, 1, 2)] if queries.shape == keys.shape else [(0, 1), (2,)]

    sent = dict(zip(far_slots, pack(block, sources[:2], part, [(k, (0, 1)) for k in far_slots])))
    kv = {k: send(sent[k], k) for k in (4, 5)}
    inputs = [after(x, *sent.values()) for x in sources]
    wanted = [(k, kind) for k in near_slots for kind in kinds]
    near_sent = pack(block, inputs, part, wanted)
    near_sent = [near_sent[k * len(kinds) : (k + 1) * len(kinds)] for k in near_slots]
    near = [near_sent[0]] + [[send(x, k) for x in near_sent[k]] for k in (1, 2, 3)]
    inputs = [after(x, near[1][0]) for x in (queries, text_keys[None], text_values[None])]
    wanted = [(k, (0,)) for k in far_slots] + [(0, (1, 2))]
    q4, q5, q6, q7, text = pack(block, inputs, part, wanted)
    kv[6] = send(after(sent[6], near[1][0]), 6)
    kv[7] = send(after(sent[7], text, *(near[k][0] for k in (1, 2, 3))), 7)
    kv.update({k: near[k][0] for k in near_slots})
    q = {k: near[k][-1] for k in near_slots}
    own = join([kv[k] for k in near_slots])
    own_halo = to_halo(own, 1)
    q[4], q[5] = send(after(q4, kv[4]), 4), send(after(q5, kv[5]), 5)
    q[6], q[7] = send(after(q6, kv[6]), 6), send(after(q7, kv[7]), 7)
    kv[7] = after(kv[7], q[4], q[5])
    other = join([kv[k] for k in far_slots])
    other_halo = to_halo(other, 0)
    o = {}
    x4, x5 = attend(info, 2, [0], [q[4], q[5]], text, own, other, own_halo)
    o[4], o[5] = send(x4, 4), send(x5, 5)
    x7, x6 = attend(info, 2, [3], [after(q[7], x4), q[6]], text, own, other, own_halo)
    o[7], o[6] = send(x7, 7), send(x6, 6)
    pieces = [q[0], q[1], after(q[3], x7), q[2]]
    o[0], x1, x3, x2 = attend(info, 3, [0, 3], pieces, text, own, other, other_halo)
    o[3], o[2], o[1] = send(x3, 3), send(x2, 2), send(x1, 1)
    out = spread(block, {k: o[k] for k in far_slots}, queries.shape[2])
    return spread(block, {k: o[k] for k in near_slots}, queries.shape[2], into=out)


def solution(mesh):
    in_specs = (
        P(("grp", "sp", "seq"), "rep", None),
        P(("grp", "sp", "seq"), "rep", None),
        P(("grp", "sp", "seq"), "rep", None),
        P("grp", None),
        P("grp", None),
        P("grp"),
    )
    out_specs = P(("grp", "sp", "seq"), "rep", None)
    return jax.shard_map(body, mesh=mesh, in_specs=in_specs, out_specs=out_specs, check_vma=False)
```

```python
import functools
import math

import jax
import jax.numpy as jnp
from jax import lax
from jax.experimental import pallas as pl
from jax.experimental.pallas import tpu as pltpu
from jax.sharding import PartitionSpec as P

HDIM = 128
COLS = 4

masked_score = -1e30
exp2_scale = math.log2(math.e) / math.sqrt(HDIM)
vmem_limit = 12 * 2**20
move_limit = 2 * 2**20


def pack_kernel(slots, at, *refs):
    n = len(refs) - len(slots) - 1
    sources, outs, sems = refs[:n], refs[n:-1], refs[-1]
    copies = []
    for (k, chosen), out in zip(slots, outs):
        width = out.shape[2]
        head = pl.multiple_of((at[0] ^ k) * width, width)
        for j, i in enumerate(chosen):
            source = sources[i].at[0, :, pl.ds(head, width)]
            copies.append(pltpu.make_async_copy(source, out.at[j], sems.at[len(copies)]))
    for copy in copies:
        copy.start()
    for copy in copies:
        copy.wait()


def pack(place, sources, width, slots):
    shapes = [(len(chosen), sources[chosen[0]].shape[1], width) for _, chosen in slots]
    return pl.pallas_call(
        functools.partial(pack_kernel, slots),
        in_specs=[pl.BlockSpec(memory_space=pltpu.SMEM)]
        + [pl.BlockSpec(memory_space=pltpu.HBM)] * len(sources),
        out_specs=[pl.BlockSpec(memory_space=pltpu.VMEM)] * len(slots),
        out_shape=[jax.ShapeDtypeStruct(shape, jnp.bfloat16) for shape in shapes],
        scratch_shapes=[pltpu.SemaphoreType.DMA((sum(shape[0] for shape in shapes),))],
        cost_estimate=pl.CostEstimate(
            flops=0, bytes_accessed=4 * sum(map(math.prod, shapes)), transcendentals=0
        ),
        compiler_params=pltpu.CompilerParams(vmem_limit_bytes=move_limit),
    )(place, *sources)


def join_kernel(tiles, *refs):
    at = 0
    for ref in refs[:-1]:
        if tiles:
            refs[-1][at] = ref[:2]
            at += 1
        else:
            refs[-1][at : at + ref.shape[0]] = ref[...]
            at += ref.shape[0]


def join(parts):
    tiles = parts[0].ndim == 3
    count = len(parts) if tiles else sum(part.shape[0] for part in parts)
    shape = (count, 2, *parts[0].shape[-2:])
    return pl.pallas_call(
        functools.partial(join_kernel, tiles),
        out_shape=jax.ShapeDtypeStruct(shape, jnp.bfloat16),
        cost_estimate=pl.CostEstimate(
            flops=0, bytes_accessed=4 * math.prod(shape), transcendentals=0
        ),
        compiler_params=pltpu.CompilerParams(vmem_limit_bytes=move_limit),
    )(*parts)


def attend_kernel(flag, turns, info, *refs):
    n = 2 * len(turns)
    queries, (text, own, other, halo) = refs[:n], refs[n : n + 4]
    outs, (keys, vals) = refs[n + 4 : 2 * n + 4], refs[2 * n + 4 :]
    length, width = own.shape[2:]
    rows = queries[0].shape[1]
    text_len = text.shape[1]
    base = info[0]
    text_live = lax.broadcasted_iota(jnp.int32, (1, text_len), 1) < info[1]

    def run(turn, q_refs, out_refs, with_halo):
        pieces = [(own, 0), (own, 1), (other, 0), (other, 1), None]
        pieces += [(halo, 0), (halo, 1)] if with_halo else []
        cut = len(pieces)
        pieces += [(own, 2), (other, 2)] + ([(halo, 2)] if with_halo else [])
        ends = [0]
        for piece in pieces:
            at = slice(ends[-1], ends[-1] + (text_len if piece is None else length))
            for side, dst in enumerate((keys, vals)):
                if piece is None:
                    dst[at] = text[side]
                else:
                    dst[at] = piece[0][base ^ (piece[1] ^ turn), side]
            ends.append(at.stop)
        main, inner = ends[cut], slice(ends[cut], ends[-1])
        first, second = [ref[ref.shape[0] - 1] for ref in q_refs]
        q_outer = jnp.where(base == 0, first, second)
        q_inner = jnp.where(base == 0, second, first)
        q_both = jnp.concatenate([q_outer, q_inner], axis=0)

        def scores_of(q, span, head):
            return lax.dot_general(
                q[:, head],
                keys[span, head],
                (((1,), (1,)), ((), ())),
                preferred_element_type=jnp.float32,
            )

        for j in range(width // HDIM):
            head = slice(j * HDIM, (j + 1) * HDIM)
            s_main = scores_of(q_both, slice(0, main), head)
            s_inner = scores_of(q_inner, inner, head)
            parts = [
                s_main[:, : ends[4]],
                jnp.where(text_live, s_main[:, ends[4] : ends[5]], masked_score),
            ]
            if with_halo:
                parts.append(s_main[:, ends[5] :])
            tops = [jnp.max(s, axis=-1, keepdims=True) for s in parts]
            top = functools.reduce(jnp.maximum, tops)
            top_inner = jnp.maximum(top[rows:], jnp.max(s_inner, axis=-1, keepdims=True))
            top = jnp.concatenate([top[:rows], top_inner], axis=0) * exp2_scale
            total, summed, at = 0.0, 0.0, 0
            for s in parts:
                w = jnp.exp2(s * exp2_scale - top)
                total = total + jnp.sum(w, axis=-1, keepdims=True)
                summed = summed + jnp.dot(
                    w.astype(jnp.bfloat16),
                    vals[at : at + s.shape[1], head],
                    preferred_element_type=jnp.float32,
                )
                at += s.shape[1]
            w = jnp.exp2(s_inner * exp2_scale - top[rows:])
            total_inner = total[rows:] + jnp.sum(w, axis=-1, keepdims=True)
            summed_inner = summed[rows:] + jnp.dot(
                w.astype(jnp.bfloat16), vals[inner, head], preferred_element_type=jnp.float32
            )
            o_outer = (summed[:rows] / total[:rows]).astype(jnp.bfloat16)
            o_inner = (summed_inner / total_inner).astype(jnp.bfloat16)
            out_refs[0][0, :, head] = jnp.where(base == 0, o_outer, o_inner)
            out_refs[1][0, :, head] = jnp.where(base == 0, o_inner, o_outer)

    for with_halo in (True, False):

        @pl.when(info[flag] == int(with_halo))
        def _():
            for t, turn in enumerate(turns):
                pair = slice(2 * t, 2 * t + 2)
                run(turn, queries[pair], outs[pair], with_halo)


def attend(info, flag, turns, queries, text, own, other, halo):
    rows = queries[-1].shape[1]
    length, width = own.shape[2:]
    total_keys = 9 * length + text.shape[1]
    pairs = len(queries) * width // HDIM * rows * total_keys
    return pl.pallas_call(
        functools.partial(attend_kernel, flag, turns),
        in_specs=[pl.BlockSpec(memory_space=pltpu.SMEM)]
        + [pl.BlockSpec(memory_space=pltpu.VMEM)] * (len(queries) + 4),
        scratch_shapes=[pltpu.VMEM((total_keys, width), jnp.bfloat16)] * 2,
        out_shape=[jax.ShapeDtypeStruct((1, rows, width), jnp.bfloat16)] * len(queries),
        cost_estimate=pl.CostEstimate(
            flops=4 * pairs * HDIM,
            bytes_accessed=width * 4 * (total_keys + rows * len(queries)),
            transcendentals=pairs,
        ),
        compiler_params=pltpu.CompilerParams(vmem_limit_bytes=vmem_limit),
    )(info, *queries, text, own, other, halo)


def spread_kernel(slots, place, *refs):
    out, sems = refs[-2:]
    width = refs[0].shape[2]
    copies = []
    for i, (k, ref) in enumerate(zip(slots, refs)):
        at = pl.multiple_of((place[0] ^ k) * width, width)
        copies.append(pltpu.make_async_copy(ref, out.at[:, :, pl.ds(at, width)], sems.at[i]))
    for copy in copies:
        copy.start()
    for copy in copies:
        copy.wait()


def spread(place, pieces, out_width, into=None):
    slots = sorted(pieces)
    shape = (*pieces[slots[0]].shape[:2], out_width)
    extra = [] if into is None else [into]
    return pl.pallas_call(
        functools.partial(spread_kernel, slots),
        in_specs=[pl.BlockSpec(memory_space=pltpu.SMEM)]
        + [pl.BlockSpec(memory_space=pltpu.VMEM)] * len(slots)
        + [pl.BlockSpec(memory_space=pl.ANY)] * len(extra),
        out_specs=pl.BlockSpec(memory_space=pl.ANY),
        out_shape=jax.ShapeDtypeStruct(shape, jnp.bfloat16),
        input_output_aliases={1 + len(slots): 0} if extra else {},
        scratch_shapes=[pltpu.SemaphoreType.DMA((len(slots),))],
        cost_estimate=pl.CostEstimate(
            flops=0, bytes_accessed=4 * math.prod(shape), transcendentals=0
        ),
        compiler_params=pltpu.CompilerParams(vmem_limit_bytes=move_limit),
    )(place, *[pieces[k] for k in slots], *extra)


def after(x, *others):
    return lax.optimization_barrier((x, *others))[0]


def body(queries, keys, values, text_keys, text_values, text_count):
    n_seq, n_sp = lax.axis_size("seq"), lax.axis_size("sp")
    tile = lax.axis_index("sp") * n_seq + lax.axis_index("seq")
    n_tiles, span = n_sp * n_seq, 2 * COLS
    col, odd, place, pair = tile % COLS, tile // COLS % 2, tile % span, tile // span
    n_pairs = n_tiles // span
    if lax.axis_size("rep") > 1:
        keys = lax.all_gather(keys, "rep", axis=1, tiled=True)
        values = lax.all_gather(values, "rep", axis=1, tiled=True)
    part = queries.shape[2] // span
    near_slots, far_slots = range(COLS), range(COLS, span)

    def send(x, k):
        return lax.ppermute(x, "seq", [(i, i ^ k) for i in range(n_seq)])

    def to_halo(x, down):
        pairs = [(i, i + span if i // COLS % 2 == down else i - span) for i in range(n_tiles)]
        flat = lambda i: i % n_seq * n_sp + i // n_seq
        pairs = [(flat(i), flat(j)) for i, j in pairs if 0 <= j < n_tiles]
        return lax.ppermute(x, ("seq", "sp"), pairs)

    low_halo, high_halo = pair > 0, pair < n_pairs - 1
    near_halo = jnp.where(odd == 1, low_halo, high_halo)
    far_halo = jnp.where(odd == 1, high_halo, low_halo)
    base = (col == 1) | (col == 2)
    entries = (base, text_count[0], near_halo, far_halo)
    info = jnp.stack([jnp.asarray(x, jnp.int32) for x in entries])

    block = place.reshape(1)
    sources = [keys, values, queries]
    kinds = [(0, 1, 2)] if queries.shape == keys.shape else [(0, 1), (2,)]

    sent = dict(zip(far_slots, pack(block, sources[:2], part, [(k, (0, 1)) for k in far_slots])))
    kv = {k: send(sent[k], k) for k in (4, 5)}
    inputs = [after(x, *sent.values()) for x in sources]
    wanted = [(k, kind) for k in near_slots for kind in kinds]
    near_sent = pack(block, inputs, part, wanted)
    near_sent = [near_sent[k * len(kinds) : (k + 1) * len(kinds)] for k in near_slots]
    near = [near_sent[0]] + [[send(x, k) for x in near_sent[k]] for k in (1, 2, 3)]
    inputs = [after(x, near[1][0]) for x in (queries, text_keys[None], text_values[None])]
    wanted = [(k, (0,)) for k in far_slots] + [(0, (1, 2))]
    q4, q5, q6, q7, text = pack(block, inputs, part, wanted)
    kv[6] = send(after(sent[6], near[1][0]), 6)
    kv[7] = send(after(sent[7], text, *(near[k][0] for k in (1, 2, 3))), 7)
    kv.update({k: near[k][0] for k in near_slots})
    q = {k: near[k][-1] for k in near_slots}
    own = join([kv[k] for k in near_slots])
    own_halo = to_halo(own, 1)
    q[4], q[5] = [send(after(x, kv[4], kv[5], kv[6]), k) for k, x in ((4, q4), (5, q5))]
    q[6], q[7] = send(after(q6, kv[6]), 6), send(after(q7, kv[7]), 7)
    kv[7] = after(kv[7], q[4], q[5])
    other = join([kv[k] for k in far_slots])
    other_halo = to_halo(other, 0)
    o = {}
    x4, x5 = attend(info, 2, [0], [q[4], q[5]], text, own, other, own_halo)
    o[4], o[5] = send(x4, 4), send(x5, 5)
    x7, x6 = attend(info, 2, [3], [after(q[7], x4), q[6]], text, own, other, own_halo)
    o[7], o[6] = send(x7, 7), send(x6, 6)
    pieces = [q[0], q[1], after(q[3], x7), q[2]]
    o[0], x1, x3, x2 = attend(info, 3, [0, 3], pieces, text, own, other, other_halo)
    o[3], o[2], o[1] = send(x3, 3), send(x2, 2), send(x1, 1)
    out = spread(block, {k: o[k] for k in far_slots}, queries.shape[2])
    return spread(block, {k: o[k] for k in near_slots}, queries.shape[2], into=out)


def solution(mesh):
    in_specs = (
        P(("grp", "sp", "seq"), "rep", None),
        P(("grp", "sp", "seq"), "rep", None),
        P(("grp", "sp", "seq"), "rep", None),
        P("grp", None),
        P("grp", None),
        P("grp"),
    )
    out_specs = P(("grp", "sp", "seq"), "rep", None)
    return jax.shard_map(body, mesh=mesh, in_specs=in_specs, out_specs=out_specs, check_vma=False)
```

```python
import functools
import math

import jax
import jax.numpy as jnp
from jax import lax
from jax.experimental import pallas as pl
from jax.experimental.pallas import tpu as pltpu
from jax.sharding import PartitionSpec as P

HDIM = 128
COLS = 4

masked_score = -1e30
exp2_scale = math.log2(math.e) / math.sqrt(HDIM)
vmem_limit = 12 * 2**20
move_limit = 2 * 2**20


def pack_kernel(wanted, at, *refs):
    n = len(refs) - len(wanted) - 1
    sources, outs, sems = refs[:n], refs[n:-1], refs[-1]
    copies = []
    for (k, chosen), out in zip(wanted, outs):
        width = out.shape[-1]
        if k is None:
            blocks = [(out.at[c], at[0] // COLS * COLS + c) for c in range(COLS)]
        else:
            blocks = [(out, at[0] ^ k)]
        for dst, block in blocks:
            lanes = pl.ds(pl.multiple_of(block * width, width), width)
            for j, i in enumerate(chosen):
                sem = sems.at[len(copies)]
                copies.append(pltpu.make_async_copy(sources[i].at[0, :, lanes], dst.at[j], sem))
    for copy in copies:
        copy.start()
    for copy in copies:
        copy.wait()


def pack(place, sources, width, wanted):
    shapes = []
    for k, chosen in wanted:
        shape = (len(chosen), sources[chosen[0]].shape[1], width)
        shapes.append((COLS, *shape) if k is None else shape)
    count = sum(math.prod(shape[:-2]) for shape in shapes)
    return pl.pallas_call(
        functools.partial(pack_kernel, wanted),
        in_specs=[pl.BlockSpec(memory_space=pltpu.SMEM)]
        + [pl.BlockSpec(memory_space=pl.ANY)] * len(sources),
        out_specs=[pl.BlockSpec(memory_space=pltpu.VMEM)] * len(wanted),
        out_shape=[jax.ShapeDtypeStruct(shape, jnp.bfloat16) for shape in shapes],
        scratch_shapes=[pltpu.SemaphoreType.DMA((count,))],
        cost_estimate=pl.CostEstimate(
            flops=0, bytes_accessed=4 * sum(map(math.prod, shapes)), transcendentals=0
        ),
        compiler_params=pltpu.CompilerParams(vmem_limit_bytes=move_limit),
    )(place, *sources)


def join_kernel(tiles, *refs):
    at = 0
    for ref in refs[:-1]:
        if tiles:
            refs[-1][at] = ref[:2]
            at += 1
        else:
            refs[-1][at : at + ref.shape[0]] = ref[...]
            at += ref.shape[0]


def join(parts):
    tiles = parts[0].ndim == 3
    count = len(parts) if tiles else sum(part.shape[0] for part in parts)
    shape = (count, 2, *parts[0].shape[-2:])
    return pl.pallas_call(
        functools.partial(join_kernel, tiles),
        out_shape=jax.ShapeDtypeStruct(shape, jnp.bfloat16),
        cost_estimate=pl.CostEstimate(
            flops=0, bytes_accessed=4 * math.prod(shape), transcendentals=0
        ),
        compiler_params=pltpu.CompilerParams(vmem_limit_bytes=move_limit),
    )(*parts)


def first_two_kernel(src, dst):
    dst[...] = src[:, :2]


def first_two(x):
    if x.shape[1] == 2:
        return x
    return pl.pallas_call(
        first_two_kernel,
        out_shape=jax.ShapeDtypeStruct((x.shape[0], 2, *x.shape[2:]), jnp.bfloat16),
        compiler_params=pltpu.CompilerParams(vmem_limit_bytes=move_limit),
    )(x)


def attend_kernel(flag, turns, halo_by_column, info, *refs):
    n = 1 if turns == [False] else 2
    queries, (text, own, other, halo) = refs[:n], refs[n : n + 4]
    outs, (keys, vals) = refs[n + 4 : 2 * n + 4], refs[2 * n + 4 :]
    length, width = own.shape[2:]
    rows = queries[0].shape[-2]
    text_len = text.shape[1]
    col, flip = info[4], info[5]
    base = info[0]
    text_live = lax.broadcasted_iota(jnp.int32, (1, text_len), 1) < info[1]
    by_column = {id(own), id(halo)} if halo_by_column else {id(own)}

    def run(turn, q_outer, q_inner, put, with_halo):
        pieces = [(own, 0), (own, 1), (other, 0), (other, 1), None]
        pieces += [(halo, 0), (halo, 1)] if with_halo else []
        cut = len(pieces)
        pieces += [(own, 2), (other, 2)] + ([(halo, 2)] if with_halo else [])
        ends = [0]
        for piece in pieces:
            at = slice(ends[-1], ends[-1] + (text_len if piece is None else length))
            for side, dst in enumerate((keys, vals)):
                if piece is None:
                    dst[at] = text[side]
                else:
                    ref, column = piece[0], turn ^ piece[1]
                    dst[at] = ref[column if id(ref) in by_column else col ^ column, side]
            ends.append(at.stop)
        main, inner = ends[cut], slice(ends[cut], ends[-1])
        q_both = jnp.concatenate([q_outer, q_inner], axis=0)

        def scores_of(q, span, head):
            return lax.dot_general(
                q[:, head],
                keys[span, head],
                (((1,), (1,)), ((), ())),
                preferred_element_type=jnp.float32,
            )

        for j in range(width // HDIM):
            head = slice(j * HDIM, (j + 1) * HDIM)
            s_main = scores_of(q_both, slice(0, main), head)
            s_inner = scores_of(q_inner, inner, head)
            parts = [
                s_main[:, : ends[4]],
                jnp.where(text_live, s_main[:, ends[4] : ends[5]], masked_score),
            ]
            if with_halo:
                parts.append(s_main[:, ends[5] :])
            tops = [jnp.max(s, axis=-1, keepdims=True) for s in parts]
            top = functools.reduce(jnp.maximum, tops)
            top_inner = jnp.maximum(top[rows:], jnp.max(s_inner, axis=-1, keepdims=True))
            top = jnp.concatenate([top[:rows], top_inner], axis=0) * exp2_scale
            total, summed, at = 0.0, 0.0, 0
            for s in parts:
                w = jnp.exp2(s * exp2_scale - top)
                total = total + jnp.sum(w, axis=-1, keepdims=True)
                summed = summed + jnp.dot(
                    w.astype(jnp.bfloat16),
                    vals[at : at + s.shape[1], head],
                    preferred_element_type=jnp.float32,
                )
                at += s.shape[1]
            w = jnp.exp2(s_inner * exp2_scale - top[rows:])
            total_inner = total[rows:] + jnp.sum(w, axis=-1, keepdims=True)
            summed_inner = summed[rows:] + jnp.dot(
                w.astype(jnp.bfloat16), vals[inner, head], preferred_element_type=jnp.float32
            )
            o_outer = (summed[:rows] / total[:rows]).astype(jnp.bfloat16)
            o_inner = (summed_inner / total_inner).astype(jnp.bfloat16)
            put(head, o_outer, o_inner)

    def one_pair(turn, with_halo):
        first, second = [ref[0] for ref in queries]

        def put(head, o_outer, o_inner):
            outs[0][0, :, head] = jnp.where(base == 0, o_outer, o_inner)
            outs[1][0, :, head] = jnp.where(base == 0, o_inner, o_outer)

        q_outer = jnp.where(base == 0, first, second)
        q_inner = jnp.where(base == 0, second, first)
        run(turn, q_outer, q_inner, put, with_halo)

    def both_pairs(with_halo):
        for turn in (0, COLS - 1):

            def put(head, o_outer, o_inner):
                outs[0][turn, 0, :, head] = o_outer
                outs[0][turn ^ 1, 0, :, head] = o_inner

            q = queries[0]
            last = q.shape[1] - 1
            run(turn, q[turn, last], q[turn ^ 1, last], put, with_halo)

    for with_halo in (True, False):

        @pl.when(info[flag] == int(with_halo))
        def _():
            if turns == [False]:
                both_pairs(with_halo)
            else:
                one_pair(flip ^ (COLS - 1) if turns[0] else flip, with_halo)


def attend(info, flag, turns, queries, text, own, other, halo, halo_by_column):
    rows = queries[0].shape[-2]
    length, width = own.shape[2:]
    total_keys = 9 * length + text.shape[1]
    pairs = (4 if turns == [False] else 2) * width // HDIM * rows * total_keys
    out = (COLS, 1, rows, width) if turns == [False] else (1, rows, width)
    return pl.pallas_call(
        functools.partial(attend_kernel, flag, turns, halo_by_column),
        in_specs=[pl.BlockSpec(memory_space=pltpu.SMEM)]
        + [pl.BlockSpec(memory_space=pltpu.VMEM)] * (len(queries) + 4),
        scratch_shapes=[pltpu.VMEM((total_keys, width), jnp.bfloat16)] * 2,
        out_shape=[jax.ShapeDtypeStruct(out, jnp.bfloat16)] * len(queries),
        cost_estimate=pl.CostEstimate(
            flops=4 * pairs * HDIM,
            bytes_accessed=width * 4 * (total_keys + rows * len(queries)),
            transcendentals=pairs,
        ),
        compiler_params=pltpu.CompilerParams(vmem_limit_bytes=vmem_limit),
    )(info, *queries, text, own, other, halo)


def spread_kernel(slots, place, *refs):
    out, sems = refs[-2:]
    width = refs[0].shape[-1]
    if slots is None:
        pieces = [(refs[0].at[c], place[0] // COLS * COLS + c) for c in range(COLS)]
    else:
        pieces = [(ref, place[0] ^ k) for k, ref in zip(slots, refs)]
    copies = []
    for i, (piece, at) in enumerate(pieces):
        lanes = pl.ds(pl.multiple_of(at * width, width), width)
        copies.append(pltpu.make_async_copy(piece, out.at[:, :, lanes], sems.at[i]))
    for copy in copies:
        copy.start()
    for copy in copies:
        copy.wait()


def spread(place, pieces, out_width, slots=None, into=None):
    shape = (1, pieces[0].shape[-2], out_width)
    extra = [] if into is None else [into]
    return pl.pallas_call(
        functools.partial(spread_kernel, slots),
        in_specs=[pl.BlockSpec(memory_space=pltpu.SMEM)]
        + [pl.BlockSpec(memory_space=pltpu.VMEM)] * len(pieces)
        + [pl.BlockSpec(memory_space=pl.ANY)] * len(extra),
        out_specs=pl.BlockSpec(memory_space=pl.ANY),
        out_shape=jax.ShapeDtypeStruct(shape, jnp.bfloat16),
        input_output_aliases={1 + len(pieces): 0} if extra else {},
        scratch_shapes=[pltpu.SemaphoreType.DMA((COLS,))],
        cost_estimate=pl.CostEstimate(
            flops=0, bytes_accessed=4 * math.prod(shape), transcendentals=0
        ),
        compiler_params=pltpu.CompilerParams(vmem_limit_bytes=move_limit),
    )(place, *pieces, *extra)


def after(x, *others):
    return lax.optimization_barrier((x, *others))[0]


def body(queries, keys, values, text_keys, text_values, text_count):
    n_seq, n_sp = lax.axis_size("seq"), lax.axis_size("sp")
    tile = lax.axis_index("sp") * n_seq + lax.axis_index("seq")
    n_tiles, span = n_sp * n_seq, 2 * COLS
    col, odd, place, pair = tile % COLS, tile // COLS % 2, tile % span, tile // span
    n_pairs = n_tiles // span
    if lax.axis_size("rep") > 1:
        keys = lax.all_gather(keys, "rep", axis=1, tiled=True)
        values = lax.all_gather(values, "rep", axis=1, tiled=True)
    part = queries.shape[2] // span
    far_slots = range(COLS, span)

    def send(x, k):
        return lax.ppermute(x, "seq", [(i, i ^ k) for i in range(n_seq)])

    def to_halo(x, down):
        pairs = [(i, i + span if i // COLS % 2 == down else i - span) for i in range(n_tiles)]
        flat = lambda i: i % n_seq * n_sp + i // n_seq
        pairs = [(flat(i), flat(j)) for i, j in pairs if 0 <= j < n_tiles]
        return lax.ppermute(x, ("seq", "sp"), pairs)

    low_halo, high_halo = pair > 0, pair < n_pairs - 1
    near_halo = jnp.where(odd == 1, low_halo, high_halo)
    far_halo = jnp.where(odd == 1, high_halo, low_halo)
    base = (col == 1) | (col == 2)
    flip = jnp.where(col >= COLS // 2, COLS - 1, 0)
    entries = (base, text_count[0], near_halo, far_halo, col, flip)
    info = jnp.stack([jnp.asarray(x, jnp.int32) for x in entries])

    block = place.reshape(1)

    def exchange(x):
        groups = [[i + c for c in range(COLS)] for i in range(0, n_seq, COLS)]
        return lax.all_to_all(x, "seq", 0, 0, axis_index_groups=groups, tiled=True)

    same_rows = queries.shape == keys.shape
    sent = pack(block, [keys, values], part, [(k, (0, 1)) for k in far_slots])
    far = [send(x, k) for k, x in zip(far_slots, sent)]
    inputs = [after(x, *sent) for x in (keys, values, queries)]
    wanted = [(None, (0, 1, 2))] if same_rows else [(None, (0, 1)), (None, (2,))]
    near = [exchange(x) for x in pack(block, inputs, part, wanted)]
    own = first_two(near[0])
    own_halo = to_halo(after(own, far[0]), 1)
    inputs = [after(x, far[2]) for x in (queries, text_keys[None], text_values[None])]
    wanted = [(k, (0,)) for k in far_slots] + [(0, (1, 2))]
    q4, q5, q6, q7, text = pack(block, inputs, part, wanted)
    q4, q5 = send(after(q4, *far[:3]), 4), send(after(q5, *far[:3]), 5)
    first_halo = to_halo(join([after(far[0], far[2]), far[1]]), 0)
    far[3] = after(far[3], q4, q5, first_halo)
    other = join(far)
    last_halo = to_halo(join(far[2:]), 0)
    q6, q7 = send(after(q6, far[3]), 6), send(after(q7, far[3]), 7)
    keyed = (text, own, other)
    x4, x5 = attend(info, 2, [None], [q4, q5], *keyed, own_halo, True)
    o4, o5 = send(x4, 4), send(x5, 5)
    x7, x6 = attend(info, 2, [True], [after(q7, x4), q6], *keyed, own_halo, True)
    o7, o6 = send(x7, 7), send(x6, 6)
    other_halo = join([first_halo, after(last_halo, x7)])
    (x,) = attend(info, 3, [False], [after(near[-1], x7, o4, o5)], *keyed, other_halo, False)
    back = exchange(x)
    out = spread(block, [o4, o5, o6, o7], queries.shape[2], slots=list(far_slots))
    return spread(block, [back], queries.shape[2], into=out)


def solution(mesh):
    in_specs = (
        P(("grp", "sp", "seq"), "rep", None),
        P(("grp", "sp", "seq"), "rep", None),
        P(("grp", "sp", "seq"), "rep", None),
        P("grp", None),
        P("grp", None),
        P("grp"),
    )
    out_specs = P(("grp", "sp", "seq"), "rep", None)
    return jax.shard_map(body, mesh=mesh, in_specs=in_specs, out_specs=out_specs, check_vma=False)
```

```python
import functools
import math

import jax
import jax.numpy as jnp
from jax import lax
from jax.experimental import pallas as pl
from jax.experimental.pallas import tpu as pltpu
from jax.sharding import PartitionSpec as P

HDIM = 128
COLS = 4

masked_score = -1e30
exp2_scale = math.log2(math.e) / math.sqrt(HDIM)
vmem_limit = 14 * 2**20
move_limit = 2 * 2**20


def pack_kernel(slots, at, *refs):
    n = len(refs) - len(slots) - 1
    sources, outs, sems = refs[:n], refs[n:-1], refs[-1]
    copies = []
    for (k, chosen), out in zip(slots, outs):
        width = out.shape[2]
        head = pl.multiple_of((at[0] ^ k) * width, width)
        for j, i in enumerate(chosen):
            source = sources[i].at[0, :, pl.ds(head, width)]
            copies.append(pltpu.make_async_copy(source, out.at[j], sems.at[len(copies)]))
    for copy in copies:
        copy.start()
    for copy in copies:
        copy.wait()


def pack(place, sources, width, slots):
    shapes = [(len(chosen), sources[chosen[0]].shape[1], width) for _, chosen in slots]
    return pl.pallas_call(
        functools.partial(pack_kernel, slots),
        in_specs=[pl.BlockSpec(memory_space=pltpu.SMEM)]
        + [pl.BlockSpec(memory_space=pltpu.HBM)] * len(sources),
        out_specs=[pl.BlockSpec(memory_space=pltpu.VMEM)] * len(slots),
        out_shape=[jax.ShapeDtypeStruct(shape, jnp.bfloat16) for shape in shapes],
        scratch_shapes=[pltpu.SemaphoreType.DMA((sum(shape[0] for shape in shapes),))],
        cost_estimate=pl.CostEstimate(
            flops=0, bytes_accessed=4 * sum(map(math.prod, shapes)), transcendentals=0
        ),
        compiler_params=pltpu.CompilerParams(vmem_limit_bytes=move_limit),
    )(place, *sources)


def join_kernel(tiles, *refs):
    at = 0
    for ref in refs[:-1]:
        if tiles:
            refs[-1][at] = ref[:2]
            at += 1
        else:
            refs[-1][at : at + ref.shape[0]] = ref[...]
            at += ref.shape[0]


def join(parts):
    tiles = parts[0].ndim == 3
    count = len(parts) if tiles else sum(part.shape[0] for part in parts)
    shape = (count, 2, *parts[0].shape[-2:])
    return pl.pallas_call(
        functools.partial(join_kernel, tiles),
        out_shape=jax.ShapeDtypeStruct(shape, jnp.bfloat16),
        cost_estimate=pl.CostEstimate(
            flops=0, bytes_accessed=4 * math.prod(shape), transcendentals=0
        ),
        compiler_params=pltpu.CompilerParams(vmem_limit_bytes=move_limit),
    )(*parts)


def attend_kernel(flag, turns, info, *refs):
    n = 2 * len(turns)
    queries, (text, own, other, halo) = refs[:n], refs[n : n + 4]
    outs, (keys, vals) = refs[n + 4 : 2 * n + 4], refs[2 * n + 4 :]
    length, width = own.shape[2:]
    rows = queries[0].shape[1]
    text_len = text.shape[1]
    base = info[0]
    text_live = lax.broadcasted_iota(jnp.int32, (1, text_len), 1) < info[1]

    def run(turn, q_refs, out_refs, with_halo):
        pieces = [(own, 0), (own, 1), (other, 0), (other, 1), None]
        pieces += [(halo, 0), (halo, 1)] if with_halo else []
        cut = len(pieces)
        pieces += [(own, 2), (other, 2)] + ([(halo, 2)] if with_halo else [])
        ends = [0]
        for piece in pieces:
            at = slice(ends[-1], ends[-1] + (text_len if piece is None else length))
            for side, dst in enumerate((keys, vals)):
                if piece is None:
                    dst[at] = text[side]
                else:
                    dst[at] = piece[0][base ^ (piece[1] ^ turn), side]
            ends.append(at.stop)
        main, inner = ends[cut], slice(ends[cut], ends[-1])
        first, second = [ref[ref.shape[0] - 1] for ref in q_refs]
        q_outer = jnp.where(base == 0, first, second)
        q_inner = jnp.where(base == 0, second, first)
        q_both = jnp.concatenate([q_outer, q_inner], axis=0)

        def scores_of(q, span, head):
            return lax.dot_general(
                q[:, head],
                keys[span, head],
                (((1,), (1,)), ((), ())),
                preferred_element_type=jnp.float32,
            )

        heads = [slice(at, at + HDIM) for at in range(0, width, HDIM)]
        scores = [
            (scores_of(q_both, slice(0, main), head), scores_of(q_inner, inner, head))
            for head in heads
        ]
        for head, (s_main, s_inner) in zip(heads, scores):
            parts = [
                s_main[:, : ends[4]],
                jnp.where(text_live, s_main[:, ends[4] : ends[5]], masked_score),
            ]
            if with_halo:
                parts.append(s_main[:, ends[5] :])
            tops = [jnp.max(s, axis=-1, keepdims=True) for s in parts]
            top = functools.reduce(jnp.maximum, tops)
            top_inner = jnp.maximum(top[rows:], jnp.max(s_inner, axis=-1, keepdims=True))
            top = jnp.concatenate([top[:rows], top_inner], axis=0) * exp2_scale
            total, summed, at = 0.0, 0.0, 0
            for s in parts:
                w = jnp.exp2(s * exp2_scale - top)
                total = total + jnp.sum(w, axis=-1, keepdims=True)
                summed = summed + jnp.dot(
                    w.astype(jnp.bfloat16),
                    vals[at : at + s.shape[1], head],
                    preferred_element_type=jnp.float32,
                )
                at += s.shape[1]
            w = jnp.exp2(s_inner * exp2_scale - top[rows:])
            total_inner = total[rows:] + jnp.sum(w, axis=-1, keepdims=True)
            summed_inner = summed[rows:] + jnp.dot(
                w.astype(jnp.bfloat16), vals[inner, head], preferred_element_type=jnp.float32
            )
            o_outer = (summed[:rows] / total[:rows]).astype(jnp.bfloat16)
            o_inner = (summed_inner / total_inner).astype(jnp.bfloat16)
            out_refs[0][0, :, head] = jnp.where(base == 0, o_outer, o_inner)
            out_refs[1][0, :, head] = jnp.where(base == 0, o_inner, o_outer)

    for with_halo in (True, False):

        @pl.when(info[flag] == int(with_halo))
        def _():
            for t, turn in enumerate(turns):
                pair = slice(2 * t, 2 * t + 2)
                run(turn, queries[pair], outs[pair], with_halo)


def attend(info, flag, turns, queries, text, own, other, halo):
    rows = queries[-1].shape[1]
    length, width = own.shape[2:]
    total_keys = 9 * length + text.shape[1]
    pairs = len(queries) * width // HDIM * rows * total_keys
    return pl.pallas_call(
        functools.partial(attend_kernel, flag, turns),
        in_specs=[pl.BlockSpec(memory_space=pltpu.SMEM)]
        + [pl.BlockSpec(memory_space=pltpu.VMEM)] * (len(queries) + 4),
        scratch_shapes=[pltpu.VMEM((total_keys, width), jnp.bfloat16)] * 2,
        out_shape=[jax.ShapeDtypeStruct((1, rows, width), jnp.bfloat16)] * len(queries),
        cost_estimate=pl.CostEstimate(
            flops=4 * pairs * HDIM,
            bytes_accessed=width * 4 * (total_keys + rows * len(queries)),
            transcendentals=pairs,
        ),
        compiler_params=pltpu.CompilerParams(vmem_limit_bytes=vmem_limit),
    )(info, *queries, text, own, other, halo)


def spread_kernel(slots, place, *refs):
    out, sems = refs[-2:]
    width = refs[0].shape[2]
    copies = []
    for i, (k, ref) in enumerate(zip(slots, refs)):
        at = pl.multiple_of((place[0] ^ k) * width, width)
        copies.append(pltpu.make_async_copy(ref, out.at[:, :, pl.ds(at, width)], sems.at[i]))
    for copy in copies:
        copy.start()
    for copy in copies:
        copy.wait()


def spread(place, pieces, out_width, into=None):
    slots = sorted(pieces)
    shape = (*pieces[slots[0]].shape[:2], out_width)
    extra = [] if into is None else [into]
    return pl.pallas_call(
        functools.partial(spread_kernel, slots),
        in_specs=[pl.BlockSpec(memory_space=pltpu.SMEM)]
        + [pl.BlockSpec(memory_space=pltpu.VMEM)] * len(slots)
        + [pl.BlockSpec(memory_space=pl.ANY)] * len(extra),
        out_specs=pl.BlockSpec(memory_space=pl.ANY),
        out_shape=jax.ShapeDtypeStruct(shape, jnp.bfloat16),
        input_output_aliases={1 + len(slots): 0} if extra else {},
        scratch_shapes=[pltpu.SemaphoreType.DMA((len(slots),))],
        cost_estimate=pl.CostEstimate(
            flops=0, bytes_accessed=4 * math.prod(shape), transcendentals=0
        ),
        compiler_params=pltpu.CompilerParams(vmem_limit_bytes=move_limit),
    )(place, *[pieces[k] for k in slots], *extra)


def after(x, *others):
    return lax.optimization_barrier((x, *others))[0]


def body(queries, keys, values, text_keys, text_values, text_count):
    n_seq, n_sp = lax.axis_size("seq"), lax.axis_size("sp")
    tile = lax.axis_index("sp") * n_seq + lax.axis_index("seq")
    n_tiles, span = n_sp * n_seq, 2 * COLS
    col, odd, place, pair = tile % COLS, tile // COLS % 2, tile % span, tile // span
    n_pairs = n_tiles // span
    if lax.axis_size("rep") > 1:
        keys = lax.all_gather(keys, "rep", axis=1, tiled=True)
        values = lax.all_gather(values, "rep", axis=1, tiled=True)
    part = queries.shape[2] // span
    near_slots, far_slots = range(COLS), range(COLS, span)

    def send(x, k):
        return lax.ppermute(x, "seq", [(i, i ^ k) for i in range(n_seq)])

    def to_halo(x, down):
        pairs = [(i, i + span if i // COLS % 2 == down else i - span) for i in range(n_tiles)]
        flat = lambda i: i % n_seq * n_sp + i // n_seq
        pairs = [(flat(i), flat(j)) for i, j in pairs if 0 <= j < n_tiles]
        return lax.ppermute(x, ("seq", "sp"), pairs)

    low_halo, high_halo = pair > 0, pair < n_pairs - 1
    near_halo = jnp.where(odd == 1, low_halo, high_halo)
    far_halo = jnp.where(odd == 1, high_halo, low_halo)
    base = (col == 1) | (col == 2)
    entries = (base, text_count[0], near_halo, far_halo)
    info = jnp.stack([jnp.asarray(x, jnp.int32) for x in entries])

    block = place.reshape(1)
    sources = [keys, values, queries]
    kinds = [(0, 1, 2)] if queries.shape == keys.shape else [(0, 1), (2,)]

    sent = dict(zip(far_slots, pack(block, sources[:2], part, [(k, (0, 1)) for k in far_slots])))
    kv = {k: send(sent[k], k) for k in (4, 5)}
    inputs = [after(x, *sent.values()) for x in sources]
    wanted = [(k, kind) for k in near_slots for kind in kinds]
    near_sent = pack(block, inputs, part, wanted)
    near_sent = [near_sent[k * len(kinds) : (k + 1) * len(kinds)] for k in near_slots]
    near = [near_sent[0]] + [[send(x, k) for x in near_sent[k]] for k in (1, 2, 3)]
    inputs = [after(x, near[1][0]) for x in (queries, text_keys[None], text_values[None])]
    wanted = [(k, (0,)) for k in far_slots] + [(0, (1, 2))]
    q4, q5, q6, q7, text = pack(block, inputs, part, wanted)
    kv[6] = send(after(sent[6], near[1][0]), 6)
    kv[7] = send(after(sent[7], text, *(near[k][0] for k in (1, 2, 3))), 7)
    kv.update({k: near[k][0] for k in near_slots})
    q = {k: near[k][-1] for k in near_slots}
    own = join([kv[k] for k in near_slots])
    own_halo = to_halo(own, 1)
    other = join([kv[k] for k in far_slots])
    other_halo = to_halo(other, 0)
    q4, q5 = after(q4, other), after(q5, other)
    q[4], q[5] = send(q4, 4), send(q5, 5)
    q[6], q[7] = send(after(q6, other), 6), send(after(q7, other), 7)
    o = {}
    x4, x5 = attend(info, 2, [0], [q[4], q[5]], text, own, other, own_halo)
    o[4], o[5] = send(x4, 4), send(x5, 5)
    x7, x6 = attend(info, 2, [3], [after(q[7], x4), q[6]], text, own, other, own_halo)
    o[7], o[6] = send(x7, 7), send(x6, 6)
    pieces = [q[0], q[1], after(q[3], x7), q[2]]
    o[0], x1, x3, x2 = attend(info, 3, [0, 3], pieces, text, own, other, other_halo)
    o[3], o[2], o[1] = send(x3, 3), send(x2, 2), send(x1, 1)
    out = spread(block, {k: o[k] for k in far_slots}, queries.shape[2])
    return spread(block, {k: o[k] for k in near_slots}, queries.shape[2], into=out)


def solution(mesh):
    in_specs = (
        P(("grp", "sp", "seq"), "rep", None),
        P(("grp", "sp", "seq"), "rep", None),
        P(("grp", "sp", "seq"), "rep", None),
        P("grp", None),
        P("grp", None),
        P("grp"),
    )
    out_specs = P(("grp", "sp", "seq"), "rep", None)
    return jax.shard_map(body, mesh=mesh, in_specs=in_specs, out_specs=out_specs, check_vma=False)
```

```python
import functools
import math

import jax
import jax.numpy as jnp
from jax import lax
from jax.experimental import pallas as pl
from jax.experimental.pallas import tpu as pltpu
from jax.sharding import PartitionSpec as P

HDIM = 128
COLS = 4

masked_score = -1e30
exp2_scale = math.log2(math.e) / math.sqrt(HDIM)
vmem_limit = 14 * 2**20
move_limit = 2 * 2**20


def pack_kernel(slots, at, *refs):
    n = len(refs) - len(slots) - 1
    sources, outs, sems = refs[:n], refs[n:-1], refs[-1]
    copies = []
    for (k, chosen), out in zip(slots, outs):
        width = out.shape[2]
        head = pl.multiple_of((at[0] ^ k) * width, width)
        for j, i in enumerate(chosen):
            source = sources[i].at[0, :, pl.ds(head, width)]
            copies.append(pltpu.make_async_copy(source, out.at[j], sems.at[len(copies)]))
    for copy in copies:
        copy.start()
    for copy in copies:
        copy.wait()


def pack(place, sources, width, slots):
    shapes = [(len(chosen), sources[chosen[0]].shape[1], width) for _, chosen in slots]
    return pl.pallas_call(
        functools.partial(pack_kernel, slots),
        in_specs=[pl.BlockSpec(memory_space=pltpu.SMEM)]
        + [pl.BlockSpec(memory_space=pltpu.HBM)] * len(sources),
        out_specs=[pl.BlockSpec(memory_space=pltpu.VMEM)] * len(slots),
        out_shape=[jax.ShapeDtypeStruct(shape, jnp.bfloat16) for shape in shapes],
        scratch_shapes=[pltpu.SemaphoreType.DMA((sum(shape[0] for shape in shapes),))],
        cost_estimate=pl.CostEstimate(
            flops=0, bytes_accessed=4 * sum(map(math.prod, shapes)), transcendentals=0
        ),
        compiler_params=pltpu.CompilerParams(vmem_limit_bytes=move_limit),
    )(place, *sources)


def join_kernel(tiles, *refs):
    at = 0
    for ref in refs[:-1]:
        if tiles:
            refs[-1][at] = ref[:2]
            at += 1
        else:
            refs[-1][at : at + ref.shape[0]] = ref[...]
            at += ref.shape[0]


def join(parts):
    tiles = parts[0].ndim == 3
    count = len(parts) if tiles else sum(part.shape[0] for part in parts)
    shape = (count, 2, *parts[0].shape[-2:])
    return pl.pallas_call(
        functools.partial(join_kernel, tiles),
        out_shape=jax.ShapeDtypeStruct(shape, jnp.bfloat16),
        cost_estimate=pl.CostEstimate(
            flops=0, bytes_accessed=4 * math.prod(shape), transcendentals=0
        ),
        compiler_params=pltpu.CompilerParams(vmem_limit_bytes=move_limit),
    )(*parts)


def attend_kernel(flag, turns, begin, info, *refs):
    n = 2 * len(turns)
    queries, (text, own, other, halo) = refs[:n], refs[n : n + 4]
    outs, (keys, vals) = refs[n + 4 : -2], refs[-2:]
    length, width = own.shape[2:]
    rows = queries[0].shape[1]
    text_len = text.shape[1]
    base = info[0]
    text_live = lax.broadcasted_iota(jnp.int32, (1, text_len), 1) < info[1]

    def run(turn, at_query, with_halo):
        q_refs, out_refs = queries[at_query : at_query + 2], outs[at_query : at_query + 2]
        pieces = [(own, 0), (own, 1), (other, 0), (other, 1), None]
        pieces += [(halo, 0), (halo, 1)] if with_halo else []
        cut = len(pieces)
        pieces += [(own, 2), (other, 2)] + ([(halo, 2)] if with_halo else [])
        ends = [0]
        for piece in pieces:
            at = slice(ends[-1], ends[-1] + (text_len if piece is None else length))
            for side, dst in enumerate((keys, vals)):
                if piece is None:
                    dst[at] = text[side]
                else:
                    dst[at] = piece[0][base ^ (piece[1] ^ turn), side]
            ends.append(at.stop)
        main, inner = ends[cut], slice(ends[cut], ends[-1])
        first, second = [ref[ref.shape[0] - 1] for ref in q_refs]
        q_outer = jnp.where(base == 0, first, second)
        q_inner = jnp.where(base == 0, second, first)
        q_both = jnp.concatenate([q_outer, q_inner], axis=0)

        def scores_of(q, span, head):
            return lax.dot_general(
                q[:, head],
                keys[span, head],
                (((1,), (1,)), ((), ())),
                preferred_element_type=jnp.float32,
            )

        heads = [slice(at, at + HDIM) for at in range(0, width, HDIM)]
        scores = [
            (scores_of(q_both, slice(0, main), head), scores_of(q_inner, inner, head))
            for head in heads
        ]
        for head, (s_main, s_inner) in zip(heads, scores):
            parts = [
                s_main[:, : ends[4]],
                jnp.where(text_live, s_main[:, ends[4] : ends[5]], masked_score),
            ]
            if with_halo:
                parts.append(s_main[:, ends[5] :])
            tops = [jnp.max(s, axis=-1, keepdims=True) for s in parts]
            top = functools.reduce(jnp.maximum, tops)
            top_inner = jnp.maximum(top[rows:], jnp.max(s_inner, axis=-1, keepdims=True))
            top = jnp.concatenate([top[:rows], top_inner], axis=0) * exp2_scale
            total, summed, at = 0.0, 0.0, 0
            for s in parts:
                w = jnp.exp2(s * exp2_scale - top)
                total = total + jnp.sum(w, axis=-1, keepdims=True)
                summed = summed + jnp.dot(
                    w.astype(jnp.bfloat16),
                    vals[at : at + s.shape[1], head],
                    preferred_element_type=jnp.float32,
                )
                at += s.shape[1]
            w = jnp.exp2(s_inner * exp2_scale - top[rows:])
            total_inner = total[rows:] + jnp.sum(w, axis=-1, keepdims=True)
            summed_inner = summed[rows:] + jnp.dot(
                w.astype(jnp.bfloat16), vals[inner, head], preferred_element_type=jnp.float32
            )
            if begin:
                for i, row in (
                    (at_query + base, (summed[:rows], top[:rows], total[:rows])),
                    (at_query + 1 - base, (summed_inner, top[rows:], total_inner)),
                ):
                    for out, x in zip(outs, row):
                        out[i, :, head] = jnp.broadcast_to(x, (rows, HDIM))
                continue
            o_outer = (summed[:rows] / total[:rows]).astype(jnp.bfloat16)
            o_inner = (summed_inner / total_inner).astype(jnp.bfloat16)
            out_refs[0][0, :, head] = jnp.where(base == 0, o_outer, o_inner)
            out_refs[1][0, :, head] = jnp.where(base == 0, o_inner, o_outer)

    def run_all(with_halo):
        for t, turn in enumerate(turns):
            run(turn, 2 * t, with_halo)

    if begin:
        run_all(False)
    else:
        pl.when(info[flag] == 1)(lambda: run_all(True))
        pl.when(info[flag] == 0)(lambda: run_all(False))


def finish_kernel(flag, turns, info, *refs):
    n = 2 * len(turns)
    queries, (halo, sums, tops, totals), outs = refs[:n], refs[n : n + 4], refs[n + 4 :]
    rows, width = sums.shape[1:]
    base = info[0]

    def run(with_halo):
        for t, turn in enumerate(turns):
            outer, inner = 2 * t + base, 2 * t + 1 - base
            first, second = [ref[ref.shape[0] - 1] for ref in queries[2 * t : 2 * t + 2]]
            q_inner = jnp.where(base == 0, second, first)
            q_both = jnp.concatenate([jnp.where(base == 0, first, second), q_inner], axis=0)
            slots = [base ^ (place ^ turn) for place in range(3)]
            for at in range(0, width, HDIM):
                head = slice(at, at + HDIM)
                both = [
                    jnp.concatenate([ref[outer, :, head], ref[inner, :, head]], axis=0)
                    for ref in (sums, tops, totals)
                ]
                summed, old_top, total = both
                if with_halo:
                    pair, third = [
                        [jnp.concatenate([halo[j, side, :, head] for j in js], axis=0) for side in (0, 1)]
                        for js in (slots[:2], slots[2:])
                    ]
                    s_pair, s_third = [
                        lax.dot_general(
                            q, key, (((1,), (1,)), ((), ())), preferred_element_type=jnp.float32
                        )
                        for q, key in ((q_both[:, head], pair[0]), (q_inner[:, head], third[0]))
                    ]
                    top = jnp.max(s_pair, axis=-1, keepdims=True)
                    top_third = jnp.max(s_third, axis=-1, keepdims=True)
                    top = jnp.concatenate(
                        [top[:rows], jnp.maximum(top[rows:], top_third)], axis=0
                    )
                    top = jnp.maximum(top * exp2_scale, old_top[:, :1])
                    keep = jnp.exp2(old_top - top)
                    w = jnp.exp2(s_pair * exp2_scale - top)
                    w_third = jnp.exp2(s_third * exp2_scale - top[rows:])
                    added, added_third = [
                        jnp.dot(x.astype(jnp.bfloat16), val, preferred_element_type=jnp.float32)
                        for x, val in ((w, pair[1]), (w_third, third[1]))
                    ]
                    more = jnp.sum(w, axis=-1, keepdims=True)
                    more_third = jnp.sum(w_third, axis=-1, keepdims=True)
                    summed = summed * keep + jnp.concatenate(
                        [added[:rows], added[rows:] + added_third], axis=0
                    )
                    total = total * keep + jnp.concatenate(
                        [more[:rows], more[rows:] + more_third], axis=0
                    )
                result = (summed / total).astype(jnp.bfloat16)
                o_outer, o_inner = result[:rows], result[rows:]
                outs[2 * t][0, :, head] = jnp.where(base == 0, o_outer, o_inner)
                outs[2 * t + 1][0, :, head] = jnp.where(base == 0, o_inner, o_outer)

    pl.when(info[flag] == 1)(lambda: run(True))
    pl.when(info[flag] == 0)(lambda: run(False))


def finish(info, flag, turns, queries, halo, began):
    _, rows, width = began[0].shape
    length = halo.shape[2]
    pairs = len(queries) * width // HDIM * rows * 3 * length
    return pl.pallas_call(
        functools.partial(finish_kernel, flag, turns),
        in_specs=[pl.BlockSpec(memory_space=pltpu.SMEM)]
        + [pl.BlockSpec(memory_space=pltpu.VMEM)] * (len(queries) + 4),
        out_shape=[jax.ShapeDtypeStruct((1, rows, width), jnp.bfloat16)] * len(queries),
        cost_estimate=pl.CostEstimate(
            flops=4 * pairs * HDIM,
            bytes_accessed=width * (4 * 3 * length + 16 * rows * len(queries)),
            transcendentals=pairs,
        ),
        compiler_params=pltpu.CompilerParams(vmem_limit_bytes=vmem_limit),
    )(info, *queries, halo, *began)


def attend(info, flag, turns, queries, text, own, other, halo=None):
    rows = queries[-1].shape[1]
    length, width = own.shape[2:]
    total_keys = 9 * length + text.shape[1]
    pairs = len(queries) * width // HDIM * rows * total_keys
    if halo is None:
        out_shape = [jax.ShapeDtypeStruct((len(queries), rows, width), jnp.float32)] * 3
    else:
        out_shape = [jax.ShapeDtypeStruct((1, rows, width), jnp.bfloat16)] * len(queries)
    begin, halo = halo is None, own if halo is None else halo
    return pl.pallas_call(
        functools.partial(attend_kernel, flag, turns, begin),
        in_specs=[pl.BlockSpec(memory_space=pltpu.SMEM)]
        + [pl.BlockSpec(memory_space=pltpu.VMEM)] * (len(queries) + 4),
        scratch_shapes=[pltpu.VMEM((total_keys, width), jnp.bfloat16)] * 2,
        out_shape=out_shape,
        cost_estimate=pl.CostEstimate(
            flops=4 * pairs * HDIM,
            bytes_accessed=width * 4 * (total_keys + rows * len(queries)),
            transcendentals=pairs,
        ),
        compiler_params=pltpu.CompilerParams(vmem_limit_bytes=vmem_limit),
    )(info, *queries, text, own, other, halo)


def spread_kernel(slots, place, *refs):
    out, sems = refs[-2:]
    width = refs[0].shape[2]
    copies = []
    for i, (k, ref) in enumerate(zip(slots, refs)):
        at = pl.multiple_of((place[0] ^ k) * width, width)
        copies.append(pltpu.make_async_copy(ref, out.at[:, :, pl.ds(at, width)], sems.at[i]))
    for copy in copies:
        copy.start()
    for copy in copies:
        copy.wait()


def spread(place, pieces, out_width, into=None):
    slots = sorted(pieces)
    shape = (*pieces[slots[0]].shape[:2], out_width)
    extra = [] if into is None else [into]
    return pl.pallas_call(
        functools.partial(spread_kernel, slots),
        in_specs=[pl.BlockSpec(memory_space=pltpu.SMEM)]
        + [pl.BlockSpec(memory_space=pltpu.VMEM)] * len(slots)
        + [pl.BlockSpec(memory_space=pl.ANY)] * len(extra),
        out_specs=pl.BlockSpec(memory_space=pl.ANY),
        out_shape=jax.ShapeDtypeStruct(shape, jnp.bfloat16),
        input_output_aliases={1 + len(slots): 0} if extra else {},
        scratch_shapes=[pltpu.SemaphoreType.DMA((len(slots),))],
        cost_estimate=pl.CostEstimate(
            flops=0, bytes_accessed=4 * math.prod(shape), transcendentals=0
        ),
        compiler_params=pltpu.CompilerParams(vmem_limit_bytes=move_limit),
    )(place, *[pieces[k] for k in slots], *extra)


def after(x, *others):
    return lax.optimization_barrier((x, *others))[0]


def body(queries, keys, values, text_keys, text_values, text_count):
    n_seq, n_sp = lax.axis_size("seq"), lax.axis_size("sp")
    tile = lax.axis_index("sp") * n_seq + lax.axis_index("seq")
    n_tiles, span = n_sp * n_seq, 2 * COLS
    col, odd, place, pair = tile % COLS, tile // COLS % 2, tile % span, tile // span
    n_pairs = n_tiles // span
    if lax.axis_size("rep") > 1:
        keys = lax.all_gather(keys, "rep", axis=1, tiled=True)
        values = lax.all_gather(values, "rep", axis=1, tiled=True)
    part = queries.shape[2] // span
    near_slots, far_slots = range(COLS), range(COLS, span)

    def send(x, k):
        return lax.ppermute(x, "seq", [(i, i ^ k) for i in range(n_seq)])

    def to_halo(x, down):
        pairs = [(i, i + span if i // COLS % 2 == down else i - span) for i in range(n_tiles)]
        flat = lambda i: i % n_seq * n_sp + i // n_seq
        pairs = [(flat(i), flat(j)) for i, j in pairs if 0 <= j < n_tiles]
        return lax.ppermute(x, ("seq", "sp"), pairs)

    low_halo, high_halo = pair > 0, pair < n_pairs - 1
    near_halo = jnp.where(odd == 1, low_halo, high_halo)
    far_halo = jnp.where(odd == 1, high_halo, low_halo)
    base = (col == 1) | (col == 2)
    entries = (base, text_count[0], near_halo, far_halo)
    info = jnp.stack([jnp.asarray(x, jnp.int32) for x in entries])

    block = place.reshape(1)
    sources = [keys, values, queries]
    kinds = [(0, 1, 2)] if queries.shape == keys.shape else [(0, 1), (2,)]

    sent = dict(zip(far_slots, pack(block, sources[:2], part, [(k, (0, 1)) for k in far_slots])))
    kv = {k: send(sent[k], k) for k in (4, 5)}
    inputs = [after(x, *sent.values()) for x in sources]
    wanted = [(k, kind) for k in near_slots for kind in kinds]
    near_sent = pack(block, inputs, part, wanted)
    near_sent = [near_sent[k * len(kinds) : (k + 1) * len(kinds)] for k in near_slots]
    near = [near_sent[0]] + [[send(x, k) for x in near_sent[k]] for k in (1, 2, 3)]
    inputs = [after(x, near[1][0]) for x in (queries, text_keys[None], text_values[None])]
    wanted = [(k, (0,)) for k in far_slots] + [(0, (1, 2))]
    q4, q5, q6, q7, text = pack(block, inputs, part, wanted)
    kv[6] = send(after(sent[6], near[1][0]), 6)
    kv[7] = send(after(sent[7], near[1][0], text), 7)
    kv.update({k: near[k][0] for k in near_slots})
    q = {k: near[k][-1] for k in near_slots}
    own = join([kv[k] for k in near_slots])
    own_halo = to_halo(after(own, kv[4], kv[5], kv[6]), 1)
    other = join([kv[k] for k in far_slots])
    other_halo = to_halo(other, 0)
    q4, q5 = after(q4, other), after(q5, other)
    q[4], q[5] = send(q4, 4), send(q5, 5)
    q[6], q[7] = send(after(q6, q[4]), 6), send(after(q7, q[5]), 7)
    o = {}
    pieces = [q[0], q[1], q[3], q[2]]
    began = attend(info, 3, [0, 3], pieces, text, own, other)
    x4, x5 = attend(info, 2, [0], [after(q[4], began[0]), q[5]], text, own, other, own_halo)
    o[4], o[5] = send(x4, 4), send(x5, 5)
    x7, x6 = attend(info, 2, [3], [after(q[7], x4), q[6]], text, own, other, own_halo)
    o[7], o[6] = send(x7, 7), send(x6, 6)
    other_halo = after(other_halo, x7, o[4], o[5])
    o[0], x1, x3, x2 = finish(info, 3, [0, 3], pieces, other_halo, began)
    o[3], o[2], o[1] = send(x3, 3), send(x2, 2), send(x1, 1)
    out = spread(block, {k: o[k] for k in far_slots}, queries.shape[2])
    return spread(block, {k: o[k] for k in near_slots}, queries.shape[2], into=out)


def solution(mesh):
    in_specs = (
        P(("grp", "sp", "seq"), "rep", None),
        P(("grp", "sp", "seq"), "rep", None),
        P(("grp", "sp", "seq"), "rep", None),
        P("grp", None),
        P("grp", None),
        P("grp"),
    )
    out_specs = P(("grp", "sp", "seq"), "rep", None)
    return jax.shard_map(body, mesh=mesh, in_specs=in_specs, out_specs=out_specs, check_vma=False)
```

```python
import functools
import math

import jax
import jax.numpy as jnp
from jax import lax
from jax.experimental import pallas as pl
from jax.experimental.pallas import tpu as pltpu
from jax.sharding import PartitionSpec as P

HDIM = 128
COLS = 4

masked_score = -1e30
exp2_scale = math.log2(math.e) / math.sqrt(HDIM)
vmem_limit = 14 * 2**20
move_limit = 2 * 2**20


def pack_kernel(slots, at, *refs):
    n = len(refs) - len(slots) - 1
    sources, outs, sems = refs[:n], refs[n:-1], refs[-1]
    copies = []
    for (k, chosen), out in zip(slots, outs):
        width = out.shape[2]
        head = pl.multiple_of((at[0] ^ k) * width, width)
        for j, i in enumerate(chosen):
            source = sources[i].at[0, :, pl.ds(head, width)]
            copies.append(pltpu.make_async_copy(source, out.at[j], sems.at[len(copies)]))
    for copy in copies:
        copy.start()
    for copy in copies:
        copy.wait()


def pack(place, sources, width, slots):
    shapes = [(len(chosen), sources[chosen[0]].shape[1], width) for _, chosen in slots]
    return pl.pallas_call(
        functools.partial(pack_kernel, slots),
        in_specs=[pl.BlockSpec(memory_space=pltpu.SMEM)]
        + [pl.BlockSpec(memory_space=pltpu.HBM)] * len(sources),
        out_specs=[pl.BlockSpec(memory_space=pltpu.VMEM)] * len(slots),
        out_shape=[jax.ShapeDtypeStruct(shape, jnp.bfloat16) for shape in shapes],
        scratch_shapes=[pltpu.SemaphoreType.DMA((sum(shape[0] for shape in shapes),))],
        cost_estimate=pl.CostEstimate(
            flops=0, bytes_accessed=4 * sum(map(math.prod, shapes)), transcendentals=0
        ),
        compiler_params=pltpu.CompilerParams(vmem_limit_bytes=move_limit),
    )(place, *sources)


def join_kernel(tiles, *refs):
    at = 0
    for ref in refs[:-1]:
        if tiles:
            refs[-1][at] = ref[:2]
            at += 1
        else:
            refs[-1][at : at + ref.shape[0]] = ref[...]
            at += ref.shape[0]


def join(parts):
    tiles = parts[0].ndim == 3
    count = len(parts) if tiles else sum(part.shape[0] for part in parts)
    shape = (count, 2, *parts[0].shape[-2:])
    return pl.pallas_call(
        functools.partial(join_kernel, tiles),
        out_shape=jax.ShapeDtypeStruct(shape, jnp.bfloat16),
        cost_estimate=pl.CostEstimate(
            flops=0, bytes_accessed=4 * math.prod(shape), transcendentals=0
        ),
        compiler_params=pltpu.CompilerParams(vmem_limit_bytes=move_limit),
    )(*parts)


def attend_kernel(flag, turns, begin, info, *refs):
    n = 2 * len(turns)
    queries, (text, own, other, halo) = refs[:n], refs[n : n + 4]
    outs, (keys, vals) = refs[n + 4 : -2], refs[-2:]
    length, width = own.shape[2:]
    rows = queries[0].shape[1]
    text_len = text.shape[1]
    base = info[0]
    text_live = lax.broadcasted_iota(jnp.int32, (1, text_len), 1) < info[1]

    def run(turn, at_query, with_halo):
        q_refs, out_refs = queries[at_query : at_query + 2], outs[at_query : at_query + 2]
        pieces = [(own, 0), (own, 1), (other, 0), (other, 1), None]
        pieces += [(halo, 0), (halo, 1)] if with_halo else []
        cut = len(pieces)
        pieces += [(own, 2), (other, 2)] + ([(halo, 2)] if with_halo else [])
        ends = [0]
        for piece in pieces:
            at = slice(ends[-1], ends[-1] + (text_len if piece is None else length))
            for side, dst in enumerate((keys, vals)):
                if piece is None:
                    dst[at] = text[side]
                else:
                    dst[at] = piece[0][base ^ (piece[1] ^ turn), side]
            ends.append(at.stop)
        main, inner = ends[cut], slice(ends[cut], ends[-1])
        first, second = [ref[ref.shape[0] - 1] for ref in q_refs]
        q_outer = jnp.where(base == 0, first, second)
        q_inner = jnp.where(base == 0, second, first)
        q_both = jnp.concatenate([q_outer, q_inner], axis=0)

        def scores_of(q, span, head):
            return lax.dot_general(
                q[:, head],
                keys[span, head],
                (((1,), (1,)), ((), ())),
                preferred_element_type=jnp.float32,
            )

        heads = [slice(at, at + HDIM) for at in range(0, width, HDIM)]
        scores = [
            (scores_of(q_both, slice(0, main), head), scores_of(q_inner, inner, head))
            for head in heads
        ]
        for head, (s_main, s_inner) in zip(heads, scores):
            parts = [
                s_main[:, : ends[4]],
                jnp.where(text_live, s_main[:, ends[4] : ends[5]], masked_score),
            ]
            if with_halo:
                parts.append(s_main[:, ends[5] :])
            tops = [jnp.max(s, axis=-1, keepdims=True) for s in parts]
            top = functools.reduce(jnp.maximum, tops)
            top_inner = jnp.maximum(top[rows:], jnp.max(s_inner, axis=-1, keepdims=True))
            top = jnp.concatenate([top[:rows], top_inner], axis=0) * exp2_scale
            total, summed, at = 0.0, 0.0, 0
            for s in parts:
                w = jnp.exp2(s * exp2_scale - top)
                total = total + jnp.sum(w, axis=-1, keepdims=True)
                summed = summed + jnp.dot(
                    w.astype(jnp.bfloat16),
                    vals[at : at + s.shape[1], head],
                    preferred_element_type=jnp.float32,
                )
                at += s.shape[1]
            w = jnp.exp2(s_inner * exp2_scale - top[rows:])
            total_inner = total[rows:] + jnp.sum(w, axis=-1, keepdims=True)
            summed_inner = summed[rows:] + jnp.dot(
                w.astype(jnp.bfloat16), vals[inner, head], preferred_element_type=jnp.float32
            )
            if begin:
                for i, row in (
                    (at_query + base, (summed[:rows], top[:rows], total[:rows])),
                    (at_query + 1 - base, (summed_inner, top[rows:], total_inner)),
                ):
                    for out, x in zip(outs, row):
                        out[i, :, head] = jnp.broadcast_to(x, (rows, HDIM))
                continue
            o_outer = (summed[:rows] / total[:rows]).astype(jnp.bfloat16)
            o_inner = (summed_inner / total_inner).astype(jnp.bfloat16)
            out_refs[0][0, :, head] = jnp.where(base == 0, o_outer, o_inner)
            out_refs[1][0, :, head] = jnp.where(base == 0, o_inner, o_outer)

    def run_all(with_halo):
        for t, turn in enumerate(turns):
            run(turn, 2 * t, with_halo)

    if begin:
        run_all(False)
    else:
        pl.when(info[flag] == 1)(lambda: run_all(True))
        pl.when(info[flag] == 0)(lambda: run_all(False))


def finish_kernel(flag, turns, info, *refs):
    n = 2 * len(turns)
    queries, (halo, sums, tops, totals), outs = refs[:n], refs[n : n + 4], refs[n + 4 :]
    rows, width = sums.shape[1:]
    base = info[0]

    def run(with_halo):
        for t, turn in enumerate(turns):
            outer, inner = 2 * t + base, 2 * t + 1 - base
            first, second = [ref[ref.shape[0] - 1] for ref in queries[2 * t : 2 * t + 2]]
            q_inner = jnp.where(base == 0, second, first)
            q_both = jnp.concatenate([jnp.where(base == 0, first, second), q_inner], axis=0)
            slots = [base ^ (place ^ turn) for place in range(3)]
            for at in range(0, width, HDIM):
                head = slice(at, at + HDIM)
                both = [
                    jnp.concatenate([ref[outer, :, head], ref[inner, :, head]], axis=0)
                    for ref in (sums, tops, totals)
                ]
                summed, old_top, total = both
                if with_halo:
                    pair, third = [
                        [jnp.concatenate([halo[j, side, :, head] for j in js], axis=0) for side in (0, 1)]
                        for js in (slots[:2], slots[2:])
                    ]
                    s_pair, s_third = [
                        lax.dot_general(
                            q, key, (((1,), (1,)), ((), ())), preferred_element_type=jnp.float32
                        )
                        for q, key in ((q_both[:, head], pair[0]), (q_inner[:, head], third[0]))
                    ]
                    top = jnp.max(s_pair, axis=-1, keepdims=True)
                    top_third = jnp.max(s_third, axis=-1, keepdims=True)
                    top = jnp.concatenate(
                        [top[:rows], jnp.maximum(top[rows:], top_third)], axis=0
                    )
                    top = jnp.maximum(top * exp2_scale, old_top[:, :1])
                    keep = jnp.exp2(old_top - top)
                    w = jnp.exp2(s_pair * exp2_scale - top)
                    w_third = jnp.exp2(s_third * exp2_scale - top[rows:])
                    added, added_third = [
                        jnp.dot(x.astype(jnp.bfloat16), val, preferred_element_type=jnp.float32)
                        for x, val in ((w, pair[1]), (w_third, third[1]))
                    ]
                    more = jnp.sum(w, axis=-1, keepdims=True)
                    more_third = jnp.sum(w_third, axis=-1, keepdims=True)
                    summed = summed * keep + jnp.concatenate(
                        [added[:rows], added[rows:] + added_third], axis=0
                    )
                    total = total * keep + jnp.concatenate(
                        [more[:rows], more[rows:] + more_third], axis=0
                    )
                result = (summed / total).astype(jnp.bfloat16)
                o_outer, o_inner = result[:rows], result[rows:]
                outs[2 * t][0, :, head] = jnp.where(base == 0, o_outer, o_inner)
                outs[2 * t + 1][0, :, head] = jnp.where(base == 0, o_inner, o_outer)

    pl.when(info[flag] == 1)(lambda: run(True))
    pl.when(info[flag] == 0)(lambda: run(False))


def finish(info, flag, turns, queries, halo, began):
    _, rows, width = began[0].shape
    length = halo.shape[2]
    pairs = len(queries) * width // HDIM * rows * 3 * length
    return pl.pallas_call(
        functools.partial(finish_kernel, flag, turns),
        in_specs=[pl.BlockSpec(memory_space=pltpu.SMEM)]
        + [pl.BlockSpec(memory_space=pltpu.VMEM)] * (len(queries) + 4),
        out_shape=[jax.ShapeDtypeStruct((1, rows, width), jnp.bfloat16)] * len(queries),
        cost_estimate=pl.CostEstimate(
            flops=4 * pairs * HDIM,
            bytes_accessed=width * (4 * 3 * length + 16 * rows * len(queries)),
            transcendentals=pairs,
        ),
        compiler_params=pltpu.CompilerParams(vmem_limit_bytes=vmem_limit),
    )(info, *queries, halo, *began)


def attend(info, flag, turns, queries, text, own, other, halo=None):
    rows = queries[-1].shape[1]
    length, width = own.shape[2:]
    total_keys = 9 * length + text.shape[1]
    pairs = len(queries) * width // HDIM * rows * total_keys
    if halo is None:
        out_shape = [jax.ShapeDtypeStruct((len(queries), rows, width), jnp.float32)] * 3
    else:
        out_shape = [jax.ShapeDtypeStruct((1, rows, width), jnp.bfloat16)] * len(queries)
    begin, halo = halo is None, own if halo is None else halo
    return pl.pallas_call(
        functools.partial(attend_kernel, flag, turns, begin),
        in_specs=[pl.BlockSpec(memory_space=pltpu.SMEM)]
        + [pl.BlockSpec(memory_space=pltpu.VMEM)] * (len(queries) + 4),
        scratch_shapes=[pltpu.VMEM((total_keys, width), jnp.bfloat16)] * 2,
        out_shape=out_shape,
        cost_estimate=pl.CostEstimate(
            flops=4 * pairs * HDIM,
            bytes_accessed=width * 4 * (total_keys + rows * len(queries)),
            transcendentals=pairs,
        ),
        compiler_params=pltpu.CompilerParams(vmem_limit_bytes=vmem_limit),
    )(info, *queries, text, own, other, halo)


def spread_kernel(slots, place, *refs):
    out, sems = refs[-2:]
    width = refs[0].shape[2]
    copies = []
    for i, (k, ref) in enumerate(zip(slots, refs)):
        at = pl.multiple_of((place[0] ^ k) * width, width)
        copies.append(pltpu.make_async_copy(ref, out.at[:, :, pl.ds(at, width)], sems.at[i]))
    for copy in copies:
        copy.start()
    for copy in copies:
        copy.wait()


def spread(place, pieces, out_width, into=None):
    slots = sorted(pieces)
    shape = (*pieces[slots[0]].shape[:2], out_width)
    extra = [] if into is None else [into]
    return pl.pallas_call(
        functools.partial(spread_kernel, slots),
        in_specs=[pl.BlockSpec(memory_space=pltpu.SMEM)]
        + [pl.BlockSpec(memory_space=pltpu.VMEM)] * len(slots)
        + [pl.BlockSpec(memory_space=pl.ANY)] * len(extra),
        out_specs=pl.BlockSpec(memory_space=pl.ANY),
        out_shape=jax.ShapeDtypeStruct(shape, jnp.bfloat16),
        input_output_aliases={1 + len(slots): 0} if extra else {},
        scratch_shapes=[pltpu.SemaphoreType.DMA((len(slots),))],
        cost_estimate=pl.CostEstimate(
            flops=0, bytes_accessed=4 * math.prod(shape), transcendentals=0
        ),
        compiler_params=pltpu.CompilerParams(vmem_limit_bytes=move_limit),
    )(place, *[pieces[k] for k in slots], *extra)


def after(x, *others):
    return lax.optimization_barrier((x, *others))[0]


def body(queries, keys, values, text_keys, text_values, text_count):
    n_seq, n_sp = lax.axis_size("seq"), lax.axis_size("sp")
    tile = lax.axis_index("sp") * n_seq + lax.axis_index("seq")
    n_tiles, span = n_sp * n_seq, 2 * COLS
    col, odd, place, pair = tile % COLS, tile // COLS % 2, tile % span, tile // span
    n_pairs = n_tiles // span
    if lax.axis_size("rep") > 1:
        keys = lax.all_gather(keys, "rep", axis=1, tiled=True)
        values = lax.all_gather(values, "rep", axis=1, tiled=True)
    part = queries.shape[2] // span
    near_slots, far_slots = range(COLS), range(COLS, span)

    def send(x, k):
        return lax.ppermute(x, "seq", [(i, i ^ k) for i in range(n_seq)])

    def to_halo(x, down):
        pairs = [(i, i + span if i // COLS % 2 == down else i - span) for i in range(n_tiles)]
        flat = lambda i: i % n_seq * n_sp + i // n_seq
        pairs = [(flat(i), flat(j)) for i, j in pairs if 0 <= j < n_tiles]
        return lax.ppermute(x, ("seq", "sp"), pairs)

    low_halo, high_halo = pair > 0, pair < n_pairs - 1
    near_halo = jnp.where(odd == 1, low_halo, high_halo)
    far_halo = jnp.where(odd == 1, high_halo, low_halo)
    base = (col == 1) | (col == 2)
    entries = (base, text_count[0], near_halo, far_halo)
    info = jnp.stack([jnp.asarray(x, jnp.int32) for x in entries])

    block = place.reshape(1)
    sources = [keys, values, queries]
    kinds = [(0, 1, 2)] if queries.shape == keys.shape else [(0, 1), (2,)]

    sent = dict(zip(far_slots, pack(block, sources[:2], part, [(k, (0, 1)) for k in far_slots])))
    kv = {k: send(sent[k], k) for k in (4, 5)}
    inputs = [after(x, *sent.values()) for x in sources]
    wanted = [(k, kind) for k in near_slots for kind in kinds]
    near_sent = pack(block, inputs, part, wanted)
    near_sent = [near_sent[k * len(kinds) : (k + 1) * len(kinds)] for k in near_slots]
    near = [near_sent[0]] + [[send(x, k) for x in near_sent[k]] for k in (1, 2, 3)]
    inputs = [after(x, near[1][0]) for x in (queries, text_keys[None], text_values[None])]
    wanted = [(k, (0,)) for k in far_slots] + [(0, (1, 2))]
    q4, q5, q6, q7, text = pack(block, inputs, part, wanted)
    kv[6] = send(after(sent[6], near[1][0]), 6)
    kv[7] = send(after(sent[7], near[1][0], text), 7)
    kv.update({k: near[k][0] for k in near_slots})
    q = {k: near[k][-1] for k in near_slots}
    own = join([kv[k] for k in near_slots])
    own_halo = to_halo(after(own, kv[4], kv[5], kv[6]), 1)
    other = join([kv[k] for k in far_slots])
    other_halo = to_halo(other, 0)
    q4, q5 = after(q4, other), after(q5, other)
    q[4], q[5] = send(q4, 4), send(q5, 5)
    q[6], q[7] = send(after(q6, own_halo), 6), send(after(q7, other), 7)
    o = {}
    pieces = [q[0], q[1], q[3], q[2]]
    began = attend(info, 3, [0, 3], pieces, text, own, other)
    x4, x5 = attend(info, 2, [0], [after(q[4], began[0]), q[5]], text, own, other, own_halo)
    o[4], o[5] = send(x4, 4), send(x5, 5)
    x7, x6 = attend(info, 2, [3], [after(q[7], x4), q[6]], text, own, other, own_halo)
    o[7], o[6] = send(x7, 7), send(x6, 6)
    other_halo = after(other_halo, x7, o[4])
    o[0], x1, x3, x2 = finish(info, 3, [0, 3], pieces, other_halo, began)
    o[3], o[2], o[1] = send(x3, 3), send(x2, 2), send(x1, 1)
    out = spread(block, {k: o[k] for k in far_slots}, queries.shape[2])
    return spread(block, {k: o[k] for k in near_slots}, queries.shape[2], into=out)


def solution(mesh):
    in_specs = (
        P(("grp", "sp", "seq"), "rep", None),
        P(("grp", "sp", "seq"), "rep", None),
        P(("grp", "sp", "seq"), "rep", None),
        P("grp", None),
        P("grp", None),
        P("grp"),
    )
    out_specs = P(("grp", "sp", "seq"), "rep", None)
    return jax.shard_map(body, mesh=mesh, in_specs=in_specs, out_specs=out_specs, check_vma=False)
```

```python
import functools
import math

import jax
import jax.numpy as jnp
from jax import lax
from jax.experimental import pallas as pl
from jax.experimental.pallas import tpu as pltpu
from jax.sharding import PartitionSpec as P

HDIM = 128
COLS = 4

masked_score = -1e30
exp2_scale = math.log2(math.e) / math.sqrt(HDIM)
vmem_limit = 14 * 2**20
move_limit = 2 * 2**20


def pack_kernel(slots, at, *refs):
    n = len(refs) - len(slots) - 1
    sources, outs, sems = refs[:n], refs[n:-1], refs[-1]
    copies = []
    for (k, chosen), out in zip(slots, outs):
        width = out.shape[2]
        head = pl.multiple_of((at[0] ^ k) * width, width)
        for j, i in enumerate(chosen):
            source = sources[i].at[0, :, pl.ds(head, width)]
            copies.append(pltpu.make_async_copy(source, out.at[j], sems.at[len(copies)]))
    for copy in copies:
        copy.start()
    for copy in copies:
        copy.wait()


def pack(place, sources, width, slots):
    shapes = [(len(chosen), sources[chosen[0]].shape[1], width) for _, chosen in slots]
    return pl.pallas_call(
        functools.partial(pack_kernel, slots),
        in_specs=[pl.BlockSpec(memory_space=pltpu.SMEM)]
        + [pl.BlockSpec(memory_space=pltpu.HBM)] * len(sources),
        out_specs=[pl.BlockSpec(memory_space=pltpu.VMEM)] * len(slots),
        out_shape=[jax.ShapeDtypeStruct(shape, jnp.bfloat16) for shape in shapes],
        scratch_shapes=[pltpu.SemaphoreType.DMA((sum(shape[0] for shape in shapes),))],
        cost_estimate=pl.CostEstimate(
            flops=0, bytes_accessed=4 * sum(map(math.prod, shapes)), transcendentals=0
        ),
        compiler_params=pltpu.CompilerParams(vmem_limit_bytes=move_limit),
    )(place, *sources)


def join_kernel(tiles, *refs):
    at = 0
    for ref in refs[:-1]:
        if tiles:
            refs[-1][at] = ref[:2]
            at += 1
        else:
            refs[-1][at : at + ref.shape[0]] = ref[...]
            at += ref.shape[0]


def join(parts):
    tiles = parts[0].ndim == 3
    count = len(parts) if tiles else sum(part.shape[0] for part in parts)
    shape = (count, 2, *parts[0].shape[-2:])
    return pl.pallas_call(
        functools.partial(join_kernel, tiles),
        out_shape=jax.ShapeDtypeStruct(shape, jnp.bfloat16),
        cost_estimate=pl.CostEstimate(
            flops=0, bytes_accessed=4 * math.prod(shape), transcendentals=0
        ),
        compiler_params=pltpu.CompilerParams(vmem_limit_bytes=move_limit),
    )(*parts)


def attend_kernel(flag, turns, begin, info, *refs):
    n = 2 * len(turns)
    queries, (text, own, other, halo) = refs[:n], refs[n : n + 4]
    outs, (keys, vals) = refs[n + 4 : -2], refs[-2:]
    length, width = own.shape[2:]
    rows = queries[0].shape[1]
    text_len = text.shape[1]
    base = info[0]
    text_live = lax.broadcasted_iota(jnp.int32, (1, text_len), 1) < info[1]

    def run(turn, at_query, with_halo):
        q_refs, out_refs = queries[at_query : at_query + 2], outs[at_query : at_query + 2]
        pieces = [(own, 0), (own, 1), (other, 0), (other, 1), None]
        pieces += [(halo, 0), (halo, 1)] if with_halo else []
        cut = len(pieces)
        pieces += [(own, 2), (other, 2)] + ([(halo, 2)] if with_halo else [])
        ends = [0]
        for piece in pieces:
            at = slice(ends[-1], ends[-1] + (text_len if piece is None else length))
            for side, dst in enumerate((keys, vals)):
                if piece is None:
                    dst[at] = text[side]
                else:
                    dst[at] = piece[0][base ^ (piece[1] ^ turn), side]
            ends.append(at.stop)
        main, inner = ends[cut], slice(ends[cut], ends[-1])
        first, second = [ref[ref.shape[0] - 1] for ref in q_refs]
        q_outer = jnp.where(base == 0, first, second)
        q_inner = jnp.where(base == 0, second, first)
        q_both = jnp.concatenate([q_outer, q_inner], axis=0)

        def scores_of(q, span, head):
            return lax.dot_general(
                q[:, head],
                keys[span, head],
                (((1,), (1,)), ((), ())),
                preferred_element_type=jnp.float32,
            )

        heads = [slice(at, at + HDIM) for at in range(0, width, HDIM)]
        scores = [
            (scores_of(q_both, slice(0, main), head), scores_of(q_inner, inner, head))
            for head in heads
        ]
        for head, (s_main, s_inner) in zip(heads, scores):
            parts = [
                s_main[:, : ends[4]],
                jnp.where(text_live, s_main[:, ends[4] : ends[5]], masked_score),
            ]
            if with_halo:
                parts.append(s_main[:, ends[5] :])
            tops = [jnp.max(s, axis=-1, keepdims=True) for s in parts]
            top = functools.reduce(jnp.maximum, tops)
            top_inner = jnp.maximum(top[rows:], jnp.max(s_inner, axis=-1, keepdims=True))
            top = jnp.concatenate([top[:rows], top_inner], axis=0) * exp2_scale
            total, summed, at = 0.0, 0.0, 0
            for s in parts:
                w = jnp.exp2(s * exp2_scale - top)
                total = total + jnp.sum(w, axis=-1, keepdims=True)
                summed = summed + jnp.dot(
                    w.astype(jnp.bfloat16),
                    vals[at : at + s.shape[1], head],
                    preferred_element_type=jnp.float32,
                )
                at += s.shape[1]
            w = jnp.exp2(s_inner * exp2_scale - top[rows:])
            total_inner = total[rows:] + jnp.sum(w, axis=-1, keepdims=True)
            summed_inner = summed[rows:] + jnp.dot(
                w.astype(jnp.bfloat16), vals[inner, head], preferred_element_type=jnp.float32
            )
            if begin:
                for i, row in (
                    (at_query + base, (summed[:rows], top[:rows], total[:rows])),
                    (at_query + 1 - base, (summed_inner, top[rows:], total_inner)),
                ):
                    for out, x in zip(outs, row):
                        out[i, :, head] = jnp.broadcast_to(x, (rows, HDIM))
                continue
            o_outer = (summed[:rows] / total[:rows]).astype(jnp.bfloat16)
            o_inner = (summed_inner / total_inner).astype(jnp.bfloat16)
            out_refs[0][0, :, head] = jnp.where(base == 0, o_outer, o_inner)
            out_refs[1][0, :, head] = jnp.where(base == 0, o_inner, o_outer)

    def run_all(with_halo):
        for t, turn in enumerate(turns):
            run(turn, 2 * t, with_halo)

    if begin:
        run_all(False)
    else:
        pl.when(info[flag] == 1)(lambda: run_all(True))
        pl.when(info[flag] == 0)(lambda: run_all(False))


def finish_kernel(flag, turns, info, *refs):
    n = 2 * len(turns)
    queries, (halo, sums, tops, totals), outs = refs[:n], refs[n : n + 4], refs[n + 4 :]
    rows, width = sums.shape[1:]
    base = info[0]

    def run(with_halo):
        units = []
        for t, turn in enumerate(turns):
            first, second = [ref[ref.shape[0] - 1] for ref in queries[2 * t : 2 * t + 2]]
            q_inner = jnp.where(base == 0, second, first)
            q_both = jnp.concatenate([jnp.where(base == 0, first, second), q_inner], axis=0)
            slots = [base ^ (place ^ turn) for place in range(3)]
            for at in range(0, width, HDIM):
                head = slice(at, at + HDIM)
                scores = []
                for q, js in ((q_both, slots[:2]), (q_inner, slots[2:])) if with_halo else ():
                    key = jnp.concatenate([halo[j, 0, :, head] for j in js], axis=0)
                    scores.append(
                        lax.dot_general(
                            q[:, head],
                            key,
                            (((1,), (1,)), ((), ())),
                            preferred_element_type=jnp.float32,
                        )
                    )
                units.append((t, slots, head, scores))
        for t, slots, head, scores in units:
            outer, inner = 2 * t + base, 2 * t + 1 - base
            summed, old_top, total = [
                jnp.concatenate([ref[outer, :, head], ref[inner, :, head]], axis=0)
                for ref in (sums, tops, totals)
            ]
            if with_halo:
                s_pair, s_third = scores
                val, val_third = [
                    jnp.concatenate([halo[j, 1, :, head] for j in js], axis=0)
                    for js in (slots[:2], slots[2:])
                ]
                top = jnp.max(s_pair, axis=-1, keepdims=True)
                top_third = jnp.max(s_third, axis=-1, keepdims=True)
                top = jnp.concatenate([top[:rows], jnp.maximum(top[rows:], top_third)], axis=0)
                top = jnp.maximum(top * exp2_scale, old_top[:, :1])
                keep = jnp.exp2(old_top - top)
                w = jnp.exp2(s_pair * exp2_scale - top)
                w_third = jnp.exp2(s_third * exp2_scale - top[rows:])
                added, added_third = [
                    jnp.dot(x.astype(jnp.bfloat16), v, preferred_element_type=jnp.float32)
                    for x, v in ((w, val), (w_third, val_third))
                ]
                more = jnp.sum(w, axis=-1, keepdims=True)
                more_third = jnp.sum(w_third, axis=-1, keepdims=True)
                summed = summed * keep + jnp.concatenate(
                    [added[:rows], added[rows:] + added_third], axis=0
                )
                total = total * keep + jnp.concatenate(
                    [more[:rows], more[rows:] + more_third], axis=0
                )
            result = (summed / total).astype(jnp.bfloat16)
            o_outer, o_inner = result[:rows], result[rows:]
            outs[2 * t][0, :, head] = jnp.where(base == 0, o_outer, o_inner)
            outs[2 * t + 1][0, :, head] = jnp.where(base == 0, o_inner, o_outer)

    pl.when(info[flag] == 1)(lambda: run(True))
    pl.when(info[flag] == 0)(lambda: run(False))


def finish(info, flag, turns, queries, halo, began):
    _, rows, width = began[0].shape
    length = halo.shape[2]
    pairs = len(queries) * width // HDIM * rows * 3 * length
    return pl.pallas_call(
        functools.partial(finish_kernel, flag, turns),
        in_specs=[pl.BlockSpec(memory_space=pltpu.SMEM)]
        + [pl.BlockSpec(memory_space=pltpu.VMEM)] * (len(queries) + 4),
        out_shape=[jax.ShapeDtypeStruct((1, rows, width), jnp.bfloat16)] * len(queries),
        cost_estimate=pl.CostEstimate(
            flops=4 * pairs * HDIM,
            bytes_accessed=width * (4 * 3 * length + 16 * rows * len(queries)),
            transcendentals=pairs,
        ),
        compiler_params=pltpu.CompilerParams(vmem_limit_bytes=vmem_limit),
    )(info, *queries, halo, *began)


def attend(info, flag, turns, queries, text, own, other, halo=None):
    rows = queries[-1].shape[1]
    length, width = own.shape[2:]
    total_keys = 9 * length + text.shape[1]
    pairs = len(queries) * width // HDIM * rows * total_keys
    if halo is None:
        out_shape = [jax.ShapeDtypeStruct((len(queries), rows, width), jnp.float32)] * 3
    else:
        out_shape = [jax.ShapeDtypeStruct((1, rows, width), jnp.bfloat16)] * len(queries)
    begin, halo = halo is None, own if halo is None else halo
    return pl.pallas_call(
        functools.partial(attend_kernel, flag, turns, begin),
        in_specs=[pl.BlockSpec(memory_space=pltpu.SMEM)]
        + [pl.BlockSpec(memory_space=pltpu.VMEM)] * (len(queries) + 4),
        scratch_shapes=[pltpu.VMEM((total_keys, width), jnp.bfloat16)] * 2,
        out_shape=out_shape,
        cost_estimate=pl.CostEstimate(
            flops=4 * pairs * HDIM,
            bytes_accessed=width * 4 * (total_keys + rows * len(queries)),
            transcendentals=pairs,
        ),
        compiler_params=pltpu.CompilerParams(vmem_limit_bytes=vmem_limit),
    )(info, *queries, text, own, other, halo)


def spread_kernel(slots, place, *refs):
    out, sems = refs[-2:]
    width = refs[0].shape[2]
    copies = []
    for i, (k, ref) in enumerate(zip(slots, refs)):
        at = pl.multiple_of((place[0] ^ k) * width, width)
        copies.append(pltpu.make_async_copy(ref, out.at[:, :, pl.ds(at, width)], sems.at[i]))
    for copy in copies:
        copy.start()
    for copy in copies:
        copy.wait()


def spread(place, pieces, out_width, into=None):
    slots = sorted(pieces)
    shape = (*pieces[slots[0]].shape[:2], out_width)
    extra = [] if into is None else [into]
    return pl.pallas_call(
        functools.partial(spread_kernel, slots),
        in_specs=[pl.BlockSpec(memory_space=pltpu.SMEM)]
        + [pl.BlockSpec(memory_space=pltpu.VMEM)] * len(slots)
        + [pl.BlockSpec(memory_space=pl.ANY)] * len(extra),
        out_specs=pl.BlockSpec(memory_space=pl.ANY),
        out_shape=jax.ShapeDtypeStruct(shape, jnp.bfloat16),
        input_output_aliases={1 + len(slots): 0} if extra else {},
        scratch_shapes=[pltpu.SemaphoreType.DMA((len(slots),))],
        cost_estimate=pl.CostEstimate(
            flops=0, bytes_accessed=4 * math.prod(shape), transcendentals=0
        ),
        compiler_params=pltpu.CompilerParams(vmem_limit_bytes=move_limit),
    )(place, *[pieces[k] for k in slots], *extra)


def after(x, *others):
    return lax.optimization_barrier((x, *others))[0]


def body(queries, keys, values, text_keys, text_values, text_count):
    n_seq, n_sp = lax.axis_size("seq"), lax.axis_size("sp")
    tile = lax.axis_index("sp") * n_seq + lax.axis_index("seq")
    n_tiles, span = n_sp * n_seq, 2 * COLS
    col, odd, place, pair = tile % COLS, tile // COLS % 2, tile % span, tile // span
    n_pairs = n_tiles // span
    if lax.axis_size("rep") > 1:
        keys = lax.all_gather(keys, "rep", axis=1, tiled=True)
        values = lax.all_gather(values, "rep", axis=1, tiled=True)
    part = queries.shape[2] // span
    near_slots, far_slots = range(COLS), range(COLS, span)

    def send(x, k):
        return lax.ppermute(x, "seq", [(i, i ^ k) for i in range(n_seq)])

    def to_halo(x, down):
        pairs = [(i, i + span if i // COLS % 2 == down else i - span) for i in range(n_tiles)]
        flat = lambda i: i % n_seq * n_sp + i // n_seq
        pairs = [(flat(i), flat(j)) for i, j in pairs if 0 <= j < n_tiles]
        return lax.ppermute(x, ("seq", "sp"), pairs)

    low_halo, high_halo = pair > 0, pair < n_pairs - 1
    near_halo = jnp.where(odd == 1, low_halo, high_halo)
    far_halo = jnp.where(odd == 1, high_halo, low_halo)
    base = (col == 1) | (col == 2)
    entries = (base, text_count[0], near_halo, far_halo)
    info = jnp.stack([jnp.asarray(x, jnp.int32) for x in entries])

    block = place.reshape(1)
    sources = [keys, values, queries]
    kinds = [(0, 1, 2)] if queries.shape == keys.shape else [(0, 1), (2,)]

    sent = dict(zip(far_slots, pack(block, sources[:2], part, [(k, (0, 1)) for k in far_slots])))
    kv = {k: send(sent[k], k) for k in (4, 5)}
    inputs = [after(x, *sent.values()) for x in sources]
    wanted = [(k, kind) for k in near_slots for kind in kinds]
    near_sent = pack(block, inputs, part, wanted)
    near_sent = [near_sent[k * len(kinds) : (k + 1) * len(kinds)] for k in near_slots]
    near = [near_sent[0]] + [[send(x, k) for x in near_sent[k]] for k in (1, 2, 3)]
    inputs = [after(x, near[1][0]) for x in (queries, text_keys[None], text_values[None])]
    wanted = [(k, (0,)) for k in far_slots] + [(0, (1, 2))]
    q4, q5, q6, q7, text = pack(block, inputs, part, wanted)
    kv[6] = send(after(sent[6], near[1][0]), 6)
    kv[7] = send(after(sent[7], near[1][0], text), 7)
    kv.update({k: near[k][0] for k in near_slots})
    q = {k: near[k][-1] for k in near_slots}
    own = join([kv[k] for k in near_slots])
    own_halo = to_halo(after(own, kv[4], kv[5], kv[6]), 1)
    other = join([kv[k] for k in far_slots])
    other_halo = to_halo(other, 0)
    q4, q5 = after(q4, other), after(q5, other)
    q[4], q[5] = send(q4, 4), send(q5, 5)
    q[6], q[7] = send(after(q6, own_halo), 6), send(after(q7, own_halo), 7)
    o = {}
    pieces = [q[0], q[1], q[3], q[2]]
    began = attend(info, 3, [0, 3], pieces, text, own, other)
    x4, x5 = attend(info, 2, [0], [after(q[4], began[0]), q[5]], text, own, other, own_halo)
    o[4], o[5] = send(x4, 4), send(x5, 5)
    x7, x6 = attend(info, 2, [3], [after(q[7], x4), q[6]], text, own, other, own_halo)
    o[7], o[6] = send(x7, 7), send(x6, 6)
    other_halo = after(other_halo, x7, o[4])
    o[0], x1, x3, x2 = finish(info, 3, [0, 3], pieces, other_halo, began)
    o[3], o[2], o[1] = send(x3, 3), send(x2, 2), send(x1, 1)
    out = spread(block, {k: o[k] for k in far_slots}, queries.shape[2])
    return spread(block, {k: o[k] for k in near_slots}, queries.shape[2], into=out)


def solution(mesh):
    in_specs = (
        P(("grp", "sp", "seq"), "rep", None),
        P(("grp", "sp", "seq"), "rep", None),
        P(("grp", "sp", "seq"), "rep", None),
        P("grp", None),
        P("grp", None),
        P("grp"),
    )
    out_specs = P(("grp", "sp", "seq"), "rep", None)
    return jax.shard_map(body, mesh=mesh, in_specs=in_specs, out_specs=out_specs, check_vma=False)
```

```python
import functools
import math

import jax
import jax.numpy as jnp
from jax import lax
from jax.experimental import pallas as pl
from jax.experimental.pallas import tpu as pltpu
from jax.sharding import PartitionSpec as P

HDIM = 128
COLS = 4

masked_score = -1e30
exp2_scale = math.log2(math.e) / math.sqrt(HDIM)
vmem_limit = 14 * 2**20
move_limit = 2 * 2**20


def pack_kernel(slots, at, *refs):
    n = len(refs) - len(slots) - 1
    sources, outs, sems = refs[:n], refs[n:-1], refs[-1]
    copies = []
    for (k, chosen), out in zip(slots, outs):
        width = out.shape[2]
        head = pl.multiple_of((at[0] ^ k) * width, width)
        for j, i in enumerate(chosen):
            source = sources[i].at[0, :, pl.ds(head, width)]
            copies.append(pltpu.make_async_copy(source, out.at[j], sems.at[len(copies)]))
    for copy in copies:
        copy.start()
    for copy in copies:
        copy.wait()


def pack(place, sources, width, slots):
    shapes = [(len(chosen), sources[chosen[0]].shape[1], width) for _, chosen in slots]
    return pl.pallas_call(
        functools.partial(pack_kernel, slots),
        in_specs=[pl.BlockSpec(memory_space=pltpu.SMEM)]
        + [pl.BlockSpec(memory_space=pltpu.HBM)] * len(sources),
        out_specs=[pl.BlockSpec(memory_space=pltpu.VMEM)] * len(slots),
        out_shape=[jax.ShapeDtypeStruct(shape, jnp.bfloat16) for shape in shapes],
        scratch_shapes=[pltpu.SemaphoreType.DMA((sum(shape[0] for shape in shapes),))],
        cost_estimate=pl.CostEstimate(
            flops=0, bytes_accessed=4 * sum(map(math.prod, shapes)), transcendentals=0
        ),
        compiler_params=pltpu.CompilerParams(vmem_limit_bytes=move_limit),
    )(place, *sources)


def join_kernel(tiles, *refs):
    at = 0
    for ref in refs[:-1]:
        if tiles:
            refs[-1][at] = ref[:2]
            at += 1
        else:
            refs[-1][at : at + ref.shape[0]] = ref[...]
            at += ref.shape[0]


def join(parts):
    tiles = parts[0].ndim == 3
    count = len(parts) if tiles else sum(part.shape[0] for part in parts)
    shape = (count, 2, *parts[0].shape[-2:])
    return pl.pallas_call(
        functools.partial(join_kernel, tiles),
        out_shape=jax.ShapeDtypeStruct(shape, jnp.bfloat16),
        cost_estimate=pl.CostEstimate(
            flops=0, bytes_accessed=4 * math.prod(shape), transcendentals=0
        ),
        compiler_params=pltpu.CompilerParams(vmem_limit_bytes=move_limit),
    )(*parts)


def attend_kernel(flag, turns, begin, info, *refs):
    n = 2 * len(turns)
    queries, (text, own, other, halo) = refs[:n], refs[n : n + 4]
    outs, (keys, vals) = refs[n + 4 : -2], refs[-2:]
    length, width = own.shape[2:]
    rows = queries[0].shape[1]
    text_len = text.shape[1]
    base = info[0]
    text_live = lax.broadcasted_iota(jnp.int32, (1, text_len), 1) < info[1]

    def run(turn, at_query, with_halo):
        q_refs, out_refs = queries[at_query : at_query + 2], outs[at_query : at_query + 2]
        pieces = [(own, 0), (own, 1), (other, 0), (other, 1), None]
        pieces += [(halo, 0), (halo, 1)] if with_halo else []
        cut = len(pieces)
        pieces += [(own, 2), (other, 2)] + ([(halo, 2)] if with_halo else [])
        ends = [0]
        for piece in pieces:
            at = slice(ends[-1], ends[-1] + (text_len if piece is None else length))
            for side, dst in enumerate((keys, vals)):
                if piece is None:
                    dst[at] = text[side]
                else:
                    dst[at] = piece[0][base ^ (piece[1] ^ turn), side]
            ends.append(at.stop)
        main, inner = ends[cut], slice(ends[cut], ends[-1])
        first, second = [ref[ref.shape[0] - 1] for ref in q_refs]
        q_outer = jnp.where(base == 0, first, second)
        q_inner = jnp.where(base == 0, second, first)
        q_both = jnp.concatenate([q_outer, q_inner], axis=0)

        def scores_of(q, span, head):
            return lax.dot_general(
                q[:, head],
                keys[span, head],
                (((1,), (1,)), ((), ())),
                preferred_element_type=jnp.float32,
            )

        heads = [slice(at, at + HDIM) for at in range(0, width, HDIM)]
        scores = [
            (scores_of(q_both, slice(0, main), head), scores_of(q_inner, inner, head))
            for head in heads
        ]
        for head, (s_main, s_inner) in zip(heads, scores):
            parts = [
                s_main[:, : ends[4]],
                jnp.where(text_live, s_main[:, ends[4] : ends[5]], masked_score),
            ]
            if with_halo:
                parts.append(s_main[:, ends[5] :])
            tops = [jnp.max(s, axis=-1, keepdims=True) for s in parts]
            top = functools.reduce(jnp.maximum, tops)
            top_inner = jnp.maximum(top[rows:], jnp.max(s_inner, axis=-1, keepdims=True))
            top = jnp.concatenate([top[:rows], top_inner], axis=0) * exp2_scale
            total, summed, at = 0.0, 0.0, 0
            for s in parts:
                w = jnp.exp2(s * exp2_scale - top)
                total = total + jnp.sum(w, axis=-1, keepdims=True)
                summed = summed + jnp.dot(
                    w.astype(jnp.bfloat16),
                    vals[at : at + s.shape[1], head],
                    preferred_element_type=jnp.float32,
                )
                at += s.shape[1]
            w = jnp.exp2(s_inner * exp2_scale - top[rows:])
            total_inner = total[rows:] + jnp.sum(w, axis=-1, keepdims=True)
            summed_inner = summed[rows:] + jnp.dot(
                w.astype(jnp.bfloat16), vals[inner, head], preferred_element_type=jnp.float32
            )
            if begin:
                for i, row in (
                    (at_query + base, (summed[:rows], top[:rows], total[:rows])),
                    (at_query + 1 - base, (summed_inner, top[rows:], total_inner)),
                ):
                    for out, x in zip(outs, row):
                        out[i, :, head] = jnp.broadcast_to(x, (rows, HDIM))
                continue
            o_outer = (summed[:rows] / total[:rows]).astype(jnp.bfloat16)
            o_inner = (summed_inner / total_inner).astype(jnp.bfloat16)
            out_refs[0][0, :, head] = jnp.where(base == 0, o_outer, o_inner)
            out_refs[1][0, :, head] = jnp.where(base == 0, o_inner, o_outer)

    def run_all(with_halo):
        for t, turn in enumerate(turns):
            run(turn, 2 * t, with_halo)

    if begin:
        run_all(False)
    else:
        pl.when(info[flag] == 1)(lambda: run_all(True))
        pl.when(info[flag] == 0)(lambda: run_all(False))


def finish_kernel(flag, turns, info, *refs):
    n = 2 * len(turns)
    queries, (halo, sums, tops, totals), outs = refs[:n], refs[n : n + 4], refs[n + 4 :]
    rows, width = sums.shape[1:]
    base = info[0]

    def run(with_halo):
        units = []
        for t, turn in enumerate(turns):
            first, second = [ref[ref.shape[0] - 1] for ref in queries[2 * t : 2 * t + 2]]
            q_inner = jnp.where(base == 0, second, first)
            q_both = jnp.concatenate([jnp.where(base == 0, first, second), q_inner], axis=0)
            slots = [base ^ (place ^ turn) for place in range(3)]
            for at in range(0, width, HDIM):
                head = slice(at, at + HDIM)
                scores = []
                for q, js in ((q_both, slots[:2]), (q_inner, slots[2:])) if with_halo else ():
                    key = jnp.concatenate([halo[j, 0, :, head] for j in js], axis=0)
                    scores.append(
                        lax.dot_general(
                            q[:, head],
                            key,
                            (((1,), (1,)), ((), ())),
                            preferred_element_type=jnp.float32,
                        )
                    )
                units.append((t, slots, head, scores))
        for t, slots, head, scores in units:
            outer, inner = 2 * t + base, 2 * t + 1 - base
            summed, old_top, total = [
                jnp.concatenate([ref[outer, :, head], ref[inner, :, head]], axis=0)
                for ref in (sums, tops, totals)
            ]
            if with_halo:
                s_pair, s_third = scores
                val, val_third = [
                    jnp.concatenate([halo[j, 1, :, head] for j in js], axis=0)
                    for js in (slots[:2], slots[2:])
                ]
                top = jnp.max(s_pair, axis=-1, keepdims=True)
                top_third = jnp.max(s_third, axis=-1, keepdims=True)
                top = jnp.concatenate([top[:rows], jnp.maximum(top[rows:], top_third)], axis=0)
                top = jnp.maximum(top * exp2_scale, old_top[:, :1])
                keep = jnp.exp2(old_top - top)
                w = jnp.exp2(s_pair * exp2_scale - top)
                w_third = jnp.exp2(s_third * exp2_scale - top[rows:])
                added, added_third = [
                    jnp.dot(x.astype(jnp.bfloat16), v, preferred_element_type=jnp.float32)
                    for x, v in ((w, val), (w_third, val_third))
                ]
                more = jnp.sum(w, axis=-1, keepdims=True)
                more_third = jnp.sum(w_third, axis=-1, keepdims=True)
                summed = summed * keep + jnp.concatenate(
                    [added[:rows], added[rows:] + added_third], axis=0
                )
                total = total * keep + jnp.concatenate(
                    [more[:rows], more[rows:] + more_third], axis=0
                )
            result = (summed / total).astype(jnp.bfloat16)
            o_outer, o_inner = result[:rows], result[rows:]
            outs[2 * t][0, :, head] = jnp.where(base == 0, o_outer, o_inner)
            outs[2 * t + 1][0, :, head] = jnp.where(base == 0, o_inner, o_outer)

    pl.when(info[flag] == 1)(lambda: run(True))
    pl.when(info[flag] == 0)(lambda: run(False))


def finish(info, flag, turns, queries, halo, began):
    _, rows, width = began[0].shape
    length = halo.shape[2]
    pairs = len(queries) * width // HDIM * rows * 3 * length
    return pl.pallas_call(
        functools.partial(finish_kernel, flag, turns),
        in_specs=[pl.BlockSpec(memory_space=pltpu.SMEM)]
        + [pl.BlockSpec(memory_space=pltpu.VMEM)] * (len(queries) + 4),
        out_shape=[jax.ShapeDtypeStruct((1, rows, width), jnp.bfloat16)] * len(queries),
        cost_estimate=pl.CostEstimate(
            flops=4 * pairs * HDIM,
            bytes_accessed=width * (4 * 3 * length + 16 * rows * len(queries)),
            transcendentals=pairs,
        ),
        compiler_params=pltpu.CompilerParams(vmem_limit_bytes=vmem_limit),
    )(info, *queries, halo, *began)


def attend(info, flag, turns, queries, text, own, other, halo=None):
    rows = queries[-1].shape[1]
    length, width = own.shape[2:]
    total_keys = 9 * length + text.shape[1]
    pairs = len(queries) * width // HDIM * rows * total_keys
    if halo is None:
        out_shape = [jax.ShapeDtypeStruct((len(queries), rows, width), jnp.float32)] * 3
    else:
        out_shape = [jax.ShapeDtypeStruct((1, rows, width), jnp.bfloat16)] * len(queries)
    begin, halo = halo is None, own if halo is None else halo
    return pl.pallas_call(
        functools.partial(attend_kernel, flag, turns, begin),
        in_specs=[pl.BlockSpec(memory_space=pltpu.SMEM)]
        + [pl.BlockSpec(memory_space=pltpu.VMEM)] * (len(queries) + 4),
        scratch_shapes=[pltpu.VMEM((total_keys, width), jnp.bfloat16)] * 2,
        out_shape=out_shape,
        cost_estimate=pl.CostEstimate(
            flops=4 * pairs * HDIM,
            bytes_accessed=width * 4 * (total_keys + rows * len(queries)),
            transcendentals=pairs,
        ),
        compiler_params=pltpu.CompilerParams(vmem_limit_bytes=vmem_limit),
    )(info, *queries, text, own, other, halo)


def spread_kernel(slots, place, *refs):
    out, sems = refs[-2:]
    width = refs[0].shape[2]
    copies = []
    for i, (k, ref) in enumerate(zip(slots, refs)):
        at = pl.multiple_of((place[0] ^ k) * width, width)
        copies.append(pltpu.make_async_copy(ref, out.at[:, :, pl.ds(at, width)], sems.at[i]))
    for copy in copies:
        copy.start()
    for copy in copies:
        copy.wait()


def spread(place, pieces, out_width, into=None):
    slots = sorted(pieces)
    shape = (*pieces[slots[0]].shape[:2], out_width)
    extra = [] if into is None else [into]
    return pl.pallas_call(
        functools.partial(spread_kernel, slots),
        in_specs=[pl.BlockSpec(memory_space=pltpu.SMEM)]
        + [pl.BlockSpec(memory_space=pltpu.VMEM)] * len(slots)
        + [pl.BlockSpec(memory_space=pl.ANY)] * len(extra),
        out_specs=pl.BlockSpec(memory_space=pl.ANY),
        out_shape=jax.ShapeDtypeStruct(shape, jnp.bfloat16),
        input_output_aliases={1 + len(slots): 0} if extra else {},
        scratch_shapes=[pltpu.SemaphoreType.DMA((len(slots),))],
        cost_estimate=pl.CostEstimate(
            flops=0, bytes_accessed=4 * math.prod(shape), transcendentals=0
        ),
        compiler_params=pltpu.CompilerParams(vmem_limit_bytes=move_limit),
    )(place, *[pieces[k] for k in slots], *extra)


def after(x, *others):
    return lax.optimization_barrier((x, *others))[0]


def body(queries, keys, values, text_keys, text_values, text_count):
    n_seq, n_sp = lax.axis_size("seq"), lax.axis_size("sp")
    tile = lax.axis_index("sp") * n_seq + lax.axis_index("seq")
    n_tiles, span = n_sp * n_seq, 2 * COLS
    col, odd, place, pair = tile % COLS, tile // COLS % 2, tile % span, tile // span
    n_pairs = n_tiles // span
    if lax.axis_size("rep") > 1:
        keys = lax.all_gather(keys, "rep", axis=1, tiled=True)
        values = lax.all_gather(values, "rep", axis=1, tiled=True)
    part = queries.shape[2] // span
    near_slots, far_slots = range(COLS), range(COLS, span)

    def send(x, k):
        return lax.ppermute(x, "seq", [(i, i ^ k) for i in range(n_seq)])

    def to_halo(x, down):
        pairs = [(i, i + span if i // COLS % 2 == down else i - span) for i in range(n_tiles)]
        flat = lambda i: i % n_seq * n_sp + i // n_seq
        pairs = [(flat(i), flat(j)) for i, j in pairs if 0 <= j < n_tiles]
        return lax.ppermute(x, ("seq", "sp"), pairs)

    low_halo, high_halo = pair > 0, pair < n_pairs - 1
    near_halo = jnp.where(odd == 1, low_halo, high_halo)
    far_halo = jnp.where(odd == 1, high_halo, low_halo)
    base = (col == 1) | (col == 2)
    entries = (base, text_count[0], near_halo, far_halo)
    info = jnp.stack([jnp.asarray(x, jnp.int32) for x in entries])

    block = place.reshape(1)
    sources = [keys, values, queries]
    kinds = [(0, 1, 2)] if queries.shape == keys.shape else [(0, 1), (2,)]

    sent = dict(zip(far_slots, pack(block, sources[:2], part, [(k, (0, 1)) for k in far_slots])))
    kv = {k: send(sent[k], k) for k in (4, 5)}
    inputs = [after(x, *sent.values()) for x in sources]
    wanted = [(k, kind) for k in near_slots for kind in kinds]
    near_sent = pack(block, inputs, part, wanted)
    near_sent = [near_sent[k * len(kinds) : (k + 1) * len(kinds)] for k in near_slots]
    near = [near_sent[0]] + [[send(x, k) for x in near_sent[k]] for k in (1, 2, 3)]
    inputs = [after(x, near[1][0]) for x in (queries, text_keys[None], text_values[None])]
    wanted = [(k, (0,)) for k in far_slots] + [(0, (1, 2))]
    q4, q5, q6, q7, text = pack(block, inputs, part, wanted)
    kv[6] = send(after(sent[6], near[1][0]), 6)
    kv[7] = send(after(sent[7], near[1][0], text), 7)
    kv.update({k: near[k][0] for k in near_slots})
    q = {k: near[k][-1] for k in near_slots}
    own = join([kv[k] for k in near_slots])
    own_halo = to_halo(after(own, kv[4], kv[5], kv[6]), 1)
    other = join([kv[k] for k in far_slots])
    other_halo = to_halo(other, 0)
    q4, q5 = after(q4, other), after(q5, other)
    q[4], q[5] = send(q4, 4), send(q5, 5)
    q[6], q[7] = send(after(q6, own_halo), 6), send(after(q7, other), 7)
    o = {}
    pieces = [q[0], q[1], q[3], q[2]]
    began = attend(info, 3, [0, 3], pieces, text, own, other)
    x4, x5 = attend(info, 2, [0], [after(q[4], began[0]), q[5]], text, own, other, own_halo)
    o[4], o[5] = send(x4, 4), send(x5, 5)
    x7, x6 = attend(info, 2, [3], [after(q[7], x4), q[6]], text, own, other, own_halo)
    o[7], o[6] = send(x7, 7), send(x6, 6)
    other_halo = after(other_halo, x7, o[4])
    o[0], x1, x3, x2 = finish(info, 3, [0, 3], pieces, other_halo, began)
    o[3], o[2], o[1] = send(x3, 3), send(x2, 2), send(x1, 1)
    out = spread(block, {k: o[k] for k in far_slots}, queries.shape[2])
    return spread(block, {k: o[k] for k in near_slots}, queries.shape[2], into=out)


def solution(mesh):
    in_specs = (
        P(("grp", "sp", "seq"), "rep", None),
        P(("grp", "sp", "seq"), "rep", None),
        P(("grp", "sp", "seq"), "rep", None),
        P("grp", None),
        P("grp", None),
        P("grp"),
    )
    out_specs = P(("grp", "sp", "seq"), "rep", None)
    return jax.shard_map(body, mesh=mesh, in_specs=in_specs, out_specs=out_specs, check_vma=False)
```

```python
import functools
import math

import jax
import jax.numpy as jnp
from jax import lax
from jax.experimental import pallas as pl
from jax.experimental.pallas import tpu as pltpu
from jax.sharding import PartitionSpec as P

HDIM = 128
COLS = 4

masked_score = -1e30
exp2_scale = math.log2(math.e) / math.sqrt(HDIM)
vmem_limit = 14 * 2**20
move_limit = 2 * 2**20


def pack_kernel(slots, at, *refs):
    n = len(refs) - len(slots) - 1
    sources, outs, sems = refs[:n], refs[n:-1], refs[-1]
    copies = []
    for (k, chosen), out in zip(slots, outs):
        width = out.shape[2]
        head = pl.multiple_of((at[0] ^ k) * width, width)
        for j, i in enumerate(chosen):
            source = sources[i].at[0, :, pl.ds(head, width)]
            copies.append(pltpu.make_async_copy(source, out.at[j], sems.at[len(copies)]))
    for copy in copies:
        copy.start()
    for copy in copies:
        copy.wait()


def pack(place, sources, width, slots):
    shapes = [(len(chosen), sources[chosen[0]].shape[1], width) for _, chosen in slots]
    return pl.pallas_call(
        functools.partial(pack_kernel, slots),
        in_specs=[pl.BlockSpec(memory_space=pltpu.SMEM)]
        + [pl.BlockSpec(memory_space=pltpu.HBM)] * len(sources),
        out_specs=[pl.BlockSpec(memory_space=pltpu.VMEM)] * len(slots),
        out_shape=[jax.ShapeDtypeStruct(shape, jnp.bfloat16) for shape in shapes],
        scratch_shapes=[pltpu.SemaphoreType.DMA((sum(shape[0] for shape in shapes),))],
        cost_estimate=pl.CostEstimate(
            flops=0, bytes_accessed=4 * sum(map(math.prod, shapes)), transcendentals=0
        ),
        compiler_params=pltpu.CompilerParams(vmem_limit_bytes=move_limit),
    )(place, *sources)


def join_kernel(tiles, *refs):
    at = 0
    for ref in refs[:-1]:
        if tiles:
            refs[-1][at] = ref[:2]
            at += 1
        else:
            refs[-1][at : at + ref.shape[0]] = ref[...]
            at += ref.shape[0]


def join(parts):
    tiles = parts[0].ndim == 3
    count = len(parts) if tiles else sum(part.shape[0] for part in parts)
    shape = (count, 2, *parts[0].shape[-2:])
    return pl.pallas_call(
        functools.partial(join_kernel, tiles),
        out_shape=jax.ShapeDtypeStruct(shape, jnp.bfloat16),
        cost_estimate=pl.CostEstimate(
            flops=0, bytes_accessed=4 * math.prod(shape), transcendentals=0
        ),
        compiler_params=pltpu.CompilerParams(vmem_limit_bytes=move_limit),
    )(*parts)


def attend_kernel(flag, turns, begin, info, *refs):
    n = 2 * len(turns)
    queries, (text, own, other, halo) = refs[:n], refs[n : n + 4]
    outs, (keys, vals) = refs[n + 4 : -2], refs[-2:]
    length, width = own.shape[2:]
    rows = queries[0].shape[1]
    text_len = text.shape[1]
    base = info[0]
    text_live = lax.broadcasted_iota(jnp.int32, (1, text_len), 1) < info[1]

    def run(turn, at_query, with_halo):
        q_refs, out_refs = queries[at_query : at_query + 2], outs[at_query : at_query + 2]
        pieces = [(own, 0), (own, 1), (other, 0), (other, 1), None]
        pieces += [(halo, 0), (halo, 1)] if with_halo else []
        cut = len(pieces)
        pieces += [(own, 2), (other, 2)] + ([(halo, 2)] if with_halo else [])
        ends = [0]
        for piece in pieces:
            at = slice(ends[-1], ends[-1] + (text_len if piece is None else length))
            for side, dst in enumerate((keys, vals)):
                if piece is None:
                    dst[at] = text[side]
                else:
                    dst[at] = piece[0][base ^ (piece[1] ^ turn), side]
            ends.append(at.stop)
        main, inner = ends[cut], slice(ends[cut], ends[-1])
        first, second = [ref[ref.shape[0] - 1] for ref in q_refs]
        q_outer = jnp.where(base == 0, first, second)
        q_inner = jnp.where(base == 0, second, first)
        q_both = jnp.concatenate([q_outer, q_inner], axis=0)

        def scores_of(q, span, head):
            return lax.dot_general(
                q[:, head],
                keys[span, head],
                (((1,), (1,)), ((), ())),
                preferred_element_type=jnp.float32,
            )

        heads = [slice(at, at + HDIM) for at in range(0, width, HDIM)]
        scores = [
            (scores_of(q_both, slice(0, main), head), scores_of(q_inner, inner, head))
            for head in heads
        ]
        for head, (s_main, s_inner) in zip(heads, scores):
            parts = [
                s_main[:, : ends[4]],
                jnp.where(text_live, s_main[:, ends[4] : ends[5]], masked_score),
            ]
            if with_halo:
                parts.append(s_main[:, ends[5] :])
            tops = [jnp.max(s, axis=-1, keepdims=True) for s in parts]
            top = functools.reduce(jnp.maximum, tops)
            top_inner = jnp.maximum(top[rows:], jnp.max(s_inner, axis=-1, keepdims=True))
            top = jnp.concatenate([top[:rows], top_inner], axis=0) * exp2_scale
            total, summed, at = 0.0, 0.0, 0
            for s in parts:
                w = jnp.exp2(s * exp2_scale - top)
                val = vals[at : at + s.shape[1], head]
                both = jnp.dot(
                    w.astype(jnp.bfloat16),
                    jnp.concatenate([val, jnp.ones_like(val)], axis=1),
                    preferred_element_type=jnp.float32,
                )
                summed, total = summed + both[:, :HDIM], total + both[:, HDIM:]
                at += s.shape[1]
            w = jnp.exp2(s_inner * exp2_scale - top[rows:])
            val = vals[inner, head]
            both = jnp.dot(
                w.astype(jnp.bfloat16),
                jnp.concatenate([val, jnp.ones_like(val)], axis=1),
                preferred_element_type=jnp.float32,
            )
            summed_inner, total_inner = summed[rows:] + both[:, :HDIM], total[rows:] + both[:, HDIM:]
            if begin:
                for i, row in (
                    (at_query + base, (summed[:rows], top[:rows], total[:rows])),
                    (at_query + 1 - base, (summed_inner, top[rows:], total_inner)),
                ):
                    for out, x in zip(outs, row):
                        out[i, :, head] = jnp.broadcast_to(x, (rows, HDIM))
                continue
            o_outer = (summed[:rows] / total[:rows]).astype(jnp.bfloat16)
            o_inner = (summed_inner / total_inner).astype(jnp.bfloat16)
            out_refs[0][0, :, head] = jnp.where(base == 0, o_outer, o_inner)
            out_refs[1][0, :, head] = jnp.where(base == 0, o_inner, o_outer)

    def run_all(with_halo):
        for t, turn in enumerate(turns):
            run(turn, 2 * t, with_halo)

    if begin:
        run_all(False)
    else:
        pl.when(info[flag] == 1)(lambda: run_all(True))
        pl.when(info[flag] == 0)(lambda: run_all(False))


def finish_kernel(flag, turns, info, *refs):
    n = 2 * len(turns)
    queries, (halo, sums, tops, totals), outs = refs[:n], refs[n : n + 4], refs[n + 4 :]
    rows, width = sums.shape[1:]
    base = info[0]

    def run(with_halo):
        units = []
        for t, turn in enumerate(turns):
            first, second = [ref[ref.shape[0] - 1] for ref in queries[2 * t : 2 * t + 2]]
            q_inner = jnp.where(base == 0, second, first)
            q_both = jnp.concatenate([jnp.where(base == 0, first, second), q_inner], axis=0)
            slots = [base ^ (place ^ turn) for place in range(3)]
            for at in range(0, width, HDIM):
                head = slice(at, at + HDIM)
                scores = []
                for q, js in ((q_both, slots[:2]), (q_inner, slots[2:])) if with_halo else ():
                    key = jnp.concatenate([halo[j, 0, :, head] for j in js], axis=0)
                    scores.append(
                        lax.dot_general(
                            q[:, head],
                            key,
                            (((1,), (1,)), ((), ())),
                            preferred_element_type=jnp.float32,
                        )
                    )
                units.append((t, slots, head, scores))
        for t, slots, head, scores in units:
            outer, inner = 2 * t + base, 2 * t + 1 - base
            summed, old_top, total = [
                jnp.concatenate([ref[outer, :, head], ref[inner, :, head]], axis=0)
                for ref in (sums, tops, totals)
            ]
            if with_halo:
                s_pair, s_third = scores
                val, val_third = [
                    jnp.concatenate([halo[j, 1, :, head] for j in js], axis=0)
                    for js in (slots[:2], slots[2:])
                ]
                top = jnp.max(s_pair, axis=-1, keepdims=True)
                top_third = jnp.max(s_third, axis=-1, keepdims=True)
                top = jnp.concatenate([top[:rows], jnp.maximum(top[rows:], top_third)], axis=0)
                top = jnp.maximum(top * exp2_scale, old_top[:, :1])
                keep = jnp.exp2(old_top - top)
                w = jnp.exp2(s_pair * exp2_scale - top)
                w_third = jnp.exp2(s_third * exp2_scale - top[rows:])
                added, added_third = [
                    jnp.dot(x.astype(jnp.bfloat16), v, preferred_element_type=jnp.float32)
                    for x, v in ((w, val), (w_third, val_third))
                ]
                more = jnp.sum(w, axis=-1, keepdims=True)
                more_third = jnp.sum(w_third, axis=-1, keepdims=True)
                summed = summed * keep + jnp.concatenate(
                    [added[:rows], added[rows:] + added_third], axis=0
                )
                total = total * keep + jnp.concatenate(
                    [more[:rows], more[rows:] + more_third], axis=0
                )
            result = (summed / total).astype(jnp.bfloat16)
            o_outer, o_inner = result[:rows], result[rows:]
            outs[2 * t][0, :, head] = jnp.where(base == 0, o_outer, o_inner)
            outs[2 * t + 1][0, :, head] = jnp.where(base == 0, o_inner, o_outer)

    pl.when(info[flag] == 1)(lambda: run(True))
    pl.when(info[flag] == 0)(lambda: run(False))


def finish(info, flag, turns, queries, halo, began):
    _, rows, width = began[0].shape
    length = halo.shape[2]
    pairs = len(queries) * width // HDIM * rows * 3 * length
    return pl.pallas_call(
        functools.partial(finish_kernel, flag, turns),
        in_specs=[pl.BlockSpec(memory_space=pltpu.SMEM)]
        + [pl.BlockSpec(memory_space=pltpu.VMEM)] * (len(queries) + 4),
        out_shape=[jax.ShapeDtypeStruct((1, rows, width), jnp.bfloat16)] * len(queries),
        cost_estimate=pl.CostEstimate(
            flops=4 * pairs * HDIM,
            bytes_accessed=width * (4 * 3 * length + 16 * rows * len(queries)),
            transcendentals=pairs,
        ),
        compiler_params=pltpu.CompilerParams(vmem_limit_bytes=vmem_limit),
    )(info, *queries, halo, *began)


def attend(info, flag, turns, queries, text, own, other, halo=None):
    rows = queries[-1].shape[1]
    length, width = own.shape[2:]
    total_keys = 9 * length + text.shape[1]
    pairs = len(queries) * width // HDIM * rows * total_keys
    if halo is None:
        out_shape = [jax.ShapeDtypeStruct((len(queries), rows, width), jnp.float32)] * 3
    else:
        out_shape = [jax.ShapeDtypeStruct((1, rows, width), jnp.bfloat16)] * len(queries)
    begin, halo = halo is None, own if halo is None else halo
    return pl.pallas_call(
        functools.partial(attend_kernel, flag, turns, begin),
        in_specs=[pl.BlockSpec(memory_space=pltpu.SMEM)]
        + [pl.BlockSpec(memory_space=pltpu.VMEM)] * (len(queries) + 4),
        scratch_shapes=[pltpu.VMEM((total_keys, width), jnp.bfloat16)] * 2,
        out_shape=out_shape,
        cost_estimate=pl.CostEstimate(
            flops=4 * pairs * HDIM,
            bytes_accessed=width * 4 * (total_keys + rows * len(queries)),
            transcendentals=pairs,
        ),
        compiler_params=pltpu.CompilerParams(vmem_limit_bytes=vmem_limit),
    )(info, *queries, text, own, other, halo)


def spread_kernel(slots, place, *refs):
    out, sems = refs[-2:]
    width = refs[0].shape[2]
    copies = []
    for i, (k, ref) in enumerate(zip(slots, refs)):
        at = pl.multiple_of((place[0] ^ k) * width, width)
        copies.append(pltpu.make_async_copy(ref, out.at[:, :, pl.ds(at, width)], sems.at[i]))
    for copy in copies:
        copy.start()
    for copy in copies:
        copy.wait()


def spread(place, pieces, out_width, into=None):
    slots = sorted(pieces)
    shape = (*pieces[slots[0]].shape[:2], out_width)
    extra = [] if into is None else [into]
    return pl.pallas_call(
        functools.partial(spread_kernel, slots),
        in_specs=[pl.BlockSpec(memory_space=pltpu.SMEM)]
        + [pl.BlockSpec(memory_space=pltpu.VMEM)] * len(slots)
        + [pl.BlockSpec(memory_space=pl.ANY)] * len(extra),
        out_specs=pl.BlockSpec(memory_space=pl.ANY),
        out_shape=jax.ShapeDtypeStruct(shape, jnp.bfloat16),
        input_output_aliases={1 + len(slots): 0} if extra else {},
        scratch_shapes=[pltpu.SemaphoreType.DMA((len(slots),))],
        cost_estimate=pl.CostEstimate(
            flops=0, bytes_accessed=4 * math.prod(shape), transcendentals=0
        ),
        compiler_params=pltpu.CompilerParams(vmem_limit_bytes=move_limit),
    )(place, *[pieces[k] for k in slots], *extra)


def after(x, *others):
    return lax.optimization_barrier((x, *others))[0]


def body(queries, keys, values, text_keys, text_values, text_count):
    n_seq, n_sp = lax.axis_size("seq"), lax.axis_size("sp")
    tile = lax.axis_index("sp") * n_seq + lax.axis_index("seq")
    n_tiles, span = n_sp * n_seq, 2 * COLS
    col, odd, place, pair = tile % COLS, tile // COLS % 2, tile % span, tile // span
    n_pairs = n_tiles // span
    if lax.axis_size("rep") > 1:
        keys = lax.all_gather(keys, "rep", axis=1, tiled=True)
        values = lax.all_gather(values, "rep", axis=1, tiled=True)
    part = queries.shape[2] // span
    near_slots, far_slots = range(COLS), range(COLS, span)

    def send(x, k):
        return lax.ppermute(x, "seq", [(i, i ^ k) for i in range(n_seq)])

    def to_halo(x, down):
        pairs = [(i, i + span if i // COLS % 2 == down else i - span) for i in range(n_tiles)]
        flat = lambda i: i % n_seq * n_sp + i // n_seq
        pairs = [(flat(i), flat(j)) for i, j in pairs if 0 <= j < n_tiles]
        return lax.ppermute(x, ("seq", "sp"), pairs)

    low_halo, high_halo = pair > 0, pair < n_pairs - 1
    near_halo = jnp.where(odd == 1, low_halo, high_halo)
    far_halo = jnp.where(odd == 1, high_halo, low_halo)
    base = (col == 1) | (col == 2)
    entries = (base, text_count[0], near_halo, far_halo)
    info = jnp.stack([jnp.asarray(x, jnp.int32) for x in entries])

    block = place.reshape(1)
    sources = [keys, values, queries]
    kinds = [(0, 1, 2)] if queries.shape == keys.shape else [(0, 1), (2,)]

    sent = dict(zip(far_slots, pack(block, sources[:2], part, [(k, (0, 1)) for k in far_slots])))
    kv = {k: send(sent[k], k) for k in (4, 5)}
    inputs = [after(x, *sent.values()) for x in sources]
    wanted = [(k, kind) for k in near_slots for kind in kinds]
    near_sent = pack(block, inputs, part, wanted)
    near_sent = [near_sent[k * len(kinds) : (k + 1) * len(kinds)] for k in near_slots]
    near = [near_sent[0]] + [[send(x, k) for x in near_sent[k]] for k in (1, 2, 3)]
    inputs = [after(x, near[1][0]) for x in (queries, text_keys[None], text_values[None])]
    wanted = [(k, (0,)) for k in far_slots] + [(0, (1, 2))]
    q4, q5, q6, q7, text = pack(block, inputs, part, wanted)
    kv[6] = send(after(sent[6], near[1][0]), 6)
    kv[7] = send(after(sent[7], near[1][0], text), 7)
    kv.update({k: near[k][0] for k in near_slots})
    q = {k: near[k][-1] for k in near_slots}
    own = join([kv[k] for k in near_slots])
    own_halo = to_halo(after(own, kv[4], kv[5], kv[6]), 1)
    other = join([kv[k] for k in far_slots])
    other_halo = to_halo(other, 0)
    q4, q5 = after(q4, other), after(q5, other)
    q[4], q[5] = send(q4, 4), send(q5, 5)
    q[6], q[7] = send(after(q6, own_halo), 6), send(after(q7, other), 7)
    o = {}
    pieces = [q[0], q[1], q[3], q[2]]
    began = attend(info, 3, [0, 3], pieces, text, own, other)
    x4, x5 = attend(info, 2, [0], [after(q[4], began[0]), q[5]], text, own, other, own_halo)
    o[4], o[5] = send(x4, 4), send(x5, 5)
    x7, x6 = attend(info, 2, [3], [after(q[7], x4), q[6]], text, own, other, own_halo)
    o[7], o[6] = send(x7, 7), send(x6, 6)
    other_halo = after(other_halo, x7, o[4])
    o[0], x1, x3, x2 = finish(info, 3, [0, 3], pieces, other_halo, began)
    o[3], o[2], o[1] = send(x3, 3), send(x2, 2), send(x1, 1)
    out = spread(block, {k: o[k] for k in far_slots}, queries.shape[2])
    return spread(block, {k: o[k] for k in near_slots}, queries.shape[2], into=out)


def solution(mesh):
    in_specs = (
        P(("grp", "sp", "seq"), "rep", None),
        P(("grp", "sp", "seq"), "rep", None),
        P(("grp", "sp", "seq"), "rep", None),
        P("grp", None),
        P("grp", None),
        P("grp"),
    )
    out_specs = P(("grp", "sp", "seq"), "rep", None)
    return jax.shard_map(body, mesh=mesh, in_specs=in_specs, out_specs=out_specs, check_vma=False)
```
